32 devices in a mesh: fsdp: 16 (over z, y, x), rep: 2 (over core).
Axes of the slice: x: 2, y: 2, z: 4, core: 2. Of those that a mesh axis runs over, the one named last changes fastest.
Arguments:
- tokens: bfloat16 [32768, 768], P(('fsdp', 'rep')), may hold values from -6 to 6
- doc_ids: int32 [32768], P(('fsdp', 'rep')), may hold values from 0 to 3, as said below
- cotangent: bfloat16 [32768, 768], P(('fsdp', 'rep')), may hold values from -6 to 6
- attn_weights: float32 [768, 3072], P('fsdp'), may hold values from -0.8660254 to 0.8660254, as said below
- mlp_weights: float32 [768, 6144], P('fsdp'), may hold values from -0.21875 to 0.21875
- gains: float32 [2, 768], P(None, 'fsdp'), may hold values from 0.5 to 1.5
- moment_attn: float32 [768, 3072], P('fsdp'), may hold values from -320 to 320
- moment_mlp: float32 [768, 6144], P('fsdp'), may hold values from -320 to 320
- moment_gains: float32 [2, 768], P(None, 'fsdp'), may hold values from -1024 to 1024
- ema_attn: float32 [768, 3072], P('fsdp'), may hold values from -0.21875 to 0.21875
- ema_mlp: float32 [768, 6144], P('fsdp'), may hold values from -0.21875 to 0.21875
- ema_gains: float32 [2, 768], P(None, 'fsdp'), may hold values from 0.5 to 1.5
Outputs:
- block_out: bfloat16 [32768, 768], P(('fsdp', 'rep'))
- input_grad: bfloat16 [32768, 768], P(('fsdp', 'rep'))
- grad_attn: float32 [768, 3072], P('fsdp')
- grad_mlp: float32 [768, 6144], P('fsdp')
- grad_gains: float32 [2, 768], P(None, 'fsdp')
- next_attn: float32 [768, 3072], P('fsdp')
- next_mlp: float32 [768, 6144], P('fsdp')
- next_gains: float32 [2, 768], P(None, 'fsdp')
- velocity_attn: float32 [768, 3072], P('fsdp')
- velocity_mlp: float32 [768, 6144], P('fsdp')
- velocity_gains: float32 [2, 768], P(None, 'fsdp')
- average_attn: float32 [768, 3072], P('fsdp')
- average_mlp: float32 [768, 6144], P('fsdp')
- average_gains: float32 [2, 768], P(None, 'fsdp')
- copy_attn: bfloat16 [768, 3072], P('fsdp')
- copy_mlp: bfloat16 [768, 6144], P('fsdp')
- copy_gains: bfloat16 [2, 768], P(None, 'fsdp')
The draws below stay inside these ranges and needn't reach their ends.
Inputs may be any that keep to these rules, and one draw needn't show every extreme that they name: `doc_ids`: within each device's 1024 tokens the numbers start at 0 and never fall; a document holds 256, 512 or 1024 tokens; some device holds a single document and another holds four. `attn_weights`: independent entries; the last 768 columns are four times larger than the others.
All inputs are finite; a program needn't handle non-finite values.
Results may differ from the reference program's by a relative error of at most 0.015.
The reference program's roundings to bfloat16 on the way count: a program that leaves them out, or rounds other values in their place, can miss the bound.
Values may be sent and summed in bfloat16 or wider, within the bound.
A program may use at most 256 MiB of HBM per device.

```python
import math
from functools import partial
import jax
import jax.numpy as jnp
from jax import lax

D = 768
HEAD = 64
FF = 2048
TOK_DEV = 1024
STEP = 5
WARMUP = 10
TOKENS = 32768


def draw_doc_ids(key, part):
    key = jax.random.fold_in(key, 11)
    block_count = TOKENS // TOK_DEV
    table = jnp.array([[0, 0, 0, 0], [0, 0, 1, 1], [0, 1, 2, 3], [0, 0, 1, 2], [0, 1, 1, 2], [0, 1, 2, 2]], jnp.int32)
    pattern = jax.random.randint(jax.random.fold_in(key, 1), (block_count,), 0, 6)
    chosen = jax.random.randint(jax.random.fold_in(key, 2), (), 0, block_count)
    pattern = pattern.at[chosen].set(0)
    pattern = pattern.at[(chosen + 1) % block_count].set(2)
    quarters = table[pattern]
    return jnp.repeat(quarters, TOK_DEV // 4, axis=1).reshape(TOKENS).astype(jnp.int32)


def draw_attn_weights(key, part):
    key = jax.random.fold_in(key, 5)
    normal_rows = jnp.clip(jax.random.normal(key, (D, 4 * D), jnp.float32), -6.0, 6.0)
    columns = jnp.arange(4 * D)
    factor = jnp.where(columns >= 3 * D, 4.0, 1.0) / jnp.sqrt(jnp.float32(D))
    return (normal_rows * factor[None, :]).astype(jnp.float32)


def level_of(rng, dims, cuts, smallest, largest):
    def one(position, blocks):
        heights = jax.random.uniform(jax.random.fold_in(jax.random.fold_in(rng, 6), position), (blocks,), jnp.float32, smallest / len(cuts), largest / len(cuts))
        return jnp.repeat(jnp.exp(heights), dims[position] // blocks).reshape((-1,) + (1,) * (len(dims) - position - 1))

    factor_of = one(*cuts[0])
    for cut in cuts[1:]:
        factor_of = factor_of * one(*cut)
    return factor_of


def gaussian(stream_key, shape, scale, most, cuts=(), held_as=jnp.bfloat16):
    factor_of = level_of(stream_key, shape, cuts, -0.22, 0.18) if cuts else 1.0
    values = jax.random.normal(stream_key, shape, jnp.float32) * scale * factor_of
    return jnp.minimum(jnp.maximum(values, -most), most).astype(held_as)


def setup_inputs(seed: int = 0) -> dict:
    keys = jax.random.split(jax.random.key(seed), 13)
    tokens = gaussian(keys[0], (TOKENS, D), 1.0, 6.0, ((0, 32),))
    doc_ids = draw_doc_ids(jax.random.fold_in(keys[12], 71), 0)
    cotangent = gaussian(keys[2], (TOKENS, D), 1.0, 6.0, ((0, 32),))
    attn_weights = draw_attn_weights(jax.random.fold_in(keys[12], 71), 0)
    mlp_weights = gaussian(keys[4], (D, 3 * FF), D ** -0.5, 0.21875, ((0, 16),), jnp.float32)
    gains = jnp.clip(1.0 + 0.1 * jax.random.normal(keys[5], (2, D), jnp.float32), 0.5, 1.5)
    moment_attn = gaussian(keys[6], (D, 4 * D), (0.3 * TOKENS ** 0.5), 320.0, ((0, 16),), jnp.float32)
    moment_mlp = gaussian(keys[7], (D, 3 * FF), (0.3 * TOKENS ** 0.5), 320.0, ((0, 16),), jnp.float32)
    moment_gains = gaussian(keys[8], (2, D), (TOKENS ** 0.5), 1024.0, ((1, 16),), jnp.float32)
    ema_attn = gaussian(keys[9], (D, 4 * D), D ** -0.5, 0.21875, ((0, 16),), jnp.float32)
    ema_mlp = gaussian(keys[10], (D, 3 * FF), D ** -0.5, 0.21875, ((0, 16),), jnp.float32)
    ema_gains = jnp.clip(1.0 + 0.1 * jax.random.normal(keys[11], (2, D), jnp.float32), 0.5, 1.5)
    return dict(tokens=tokens, doc_ids=doc_ids, cotangent=cotangent, attn_weights=attn_weights, mlp_weights=mlp_weights, gains=gains, moment_attn=moment_attn, moment_mlp=moment_mlp, moment_gains=moment_gains, ema_attn=ema_attn, ema_mlp=ema_mlp, ema_gains=ema_gains)


@jax.custom_vjp
def low(v):
    return lax.optimization_barrier(v.astype(jnp.bfloat16)).astype(jnp.float32)

@jax.custom_vjp
def low_back(v):
    return v

def low_keep(v):
    return (low(v), None)

def low_pass(kept, grad):
    return (grad,)

def back_keep(v):
    return (v, None)

def back_low(kept, grad):
    return (low(grad),)
low.defvjp(low_keep, low_pass)
low_back.defvjp(back_keep, back_low)
EPSILON = 1e-05
MASKED = -1e+30
MOMENTUM = 0.5
DECAY = 0.5
PEAK_RATE = 0.1
HIGHEST = lax.Precision.HIGHEST

def doc_positions(doc_block):
    row_count = doc_block.shape[0]
    places = jnp.arange(row_count, dtype=jnp.int32)
    boundary = jnp.concatenate([jnp.ones((1,), jnp.int32), (doc_block[1:] != doc_block[:-1]).astype(jnp.int32)])
    starts = lax.cummax(places * boundary, axis=0)
    return places - starts

def rotary_tables(positions):
    half_size = HEAD // 2
    frequency = 10000.0 ** (-jnp.arange(half_size, dtype=jnp.float32) / half_size)
    angles = positions.astype(jnp.float32)[:, None] * frequency[None, :]
    return (jnp.cos(angles)[:, None, :], jnp.sin(angles)[:, None, :])

def rotate(tensor, cosine, sine):
    half_size = tensor.shape[-1] // 2
    first_half = tensor[..., :half_size]
    second_half = tensor[..., half_size:]
    return jnp.concatenate([first_half * cosine - second_half * sine, second_half * cosine + first_half * sine], axis=-1)

def rms_scale(tensor):
    return lax.rsqrt(lax.optimization_barrier(jnp.mean(tensor * tensor, axis=-1, keepdims=True)) + EPSILON)

def matmul(left, right):
    return jnp.dot(left, right, precision=HIGHEST, preferred_element_type=jnp.float32)

def forward(params, stream, doc_block):
    attn_full, mlp_full, gain_rows = params
    attn_low = low(attn_full)
    mlp_low = low(mlp_full)
    gain_low = low(gain_rows)
    row_count, model_width = stream.shape
    head_count = model_width // HEAD
    hidden_width = mlp_full.shape[1] // 3
    shape_heads = (row_count, head_count, HEAD)
    cosine, sine = rotary_tables(doc_positions(doc_block))
    normed_one = low(stream * rms_scale(stream) * gain_low[0])
    query_pre = low_back(matmul(normed_one, attn_low[:, :model_width]))
    key_pre = low_back(matmul(normed_one, attn_low[:, model_width:2 * model_width]))
    value_pre = low_back(matmul(normed_one, attn_low[:, 2 * model_width:3 * model_width]))
    queries = low(rotate(query_pre.reshape(shape_heads), cosine, sine))
    key_rows = low(rotate(key_pre.reshape(shape_heads), cosine, sine))
    values = low(value_pre).reshape(shape_heads)
    scores = low_back(jnp.einsum('qhe,khe->hqk', queries, key_rows, precision=HIGHEST) * 0.125)
    places = jnp.arange(row_count)
    allowed = (places[:, None] >= places[None, :]) & (doc_block[:, None] == doc_block[None, :])
    scores = jnp.where(allowed[None], scores, MASKED)
    attn_probs = jax.nn.softmax(scores, axis=-1)
    mixed = jnp.einsum('hqk,khe->qhe', low(attn_probs), values, precision=HIGHEST).reshape(row_count, model_width)
    mixed = low(low_back(mixed))
    after_attn = stream + low_back(matmul(mixed, attn_low[:, 3 * model_width:]))
    normed_two = low(after_attn * rms_scale(after_attn) * gain_low[1])
    gate_pre = low_back(matmul(normed_two, mlp_low[:, :hidden_width]))
    up_pre = low_back(matmul(normed_two, mlp_low[:, hidden_width:2 * hidden_width]))
    hidden = low(jax.nn.silu(gate_pre) * up_pre)
    branch = low_back(matmul(hidden, mlp_low[:, 2 * hidden_width:].T))
    return after_attn + branch

def reference(tokens, doc_ids, cotangent, attn_weights, mlp_weights, gains, moment_attn, moment_mlp, moment_gains, ema_attn, ema_mlp, ema_gains):
    block_count = TOKENS // TOK_DEV
    model_width = tokens.shape[1]
    stream_all = tokens.astype(jnp.float32).reshape(block_count, TOK_DEV, model_width)
    back_all = cotangent.astype(jnp.float32).reshape(block_count, TOK_DEV, model_width)
    docs_all = doc_ids.reshape(block_count, TOK_DEV)
    params = (attn_weights, mlp_weights, gains)

    def one_block(totals, inputs):
        stream, back_rows, docs = inputs
        result, pullback = jax.vjp(partial(forward, doc_block=docs), params, stream)
        grads, stream_grad = pullback(back_rows)
        totals = jax.tree.map(jnp.add, totals, grads)
        return (totals, (result.astype(jnp.bfloat16), stream_grad.astype(jnp.bfloat16)))
    zero_grads = jax.tree.map(jnp.zeros_like, params)
    totals, (outputs, input_grads) = lax.scan(one_block, zero_grads, (stream_all, back_all, docs_all))
    grad_attn, grad_mlp, grad_gains = totals
    rate = PEAK_RATE * STEP / (WARMUP * math.sqrt(TOKENS))

    def update(weight, grad, moment, average):
        velocity = MOMENTUM * moment + grad
        weight_new = weight - rate * (grad + MOMENTUM * velocity)
        average_new = DECAY * average + (1.0 - DECAY) * weight_new
        return (weight_new, velocity, average_new, weight_new.astype(jnp.bfloat16))
    next_attn, velocity_attn, average_attn, copy_attn = update(attn_weights, grad_attn, moment_attn, ema_attn)
    next_mlp, velocity_mlp, average_mlp, copy_mlp = update(mlp_weights, grad_mlp, moment_mlp, ema_mlp)
    next_gains, velocity_gains, average_gains, copy_gains = update(gains, grad_gains, moment_gains, ema_gains)
    return (outputs.reshape(TOKENS, model_width), input_grads.reshape(TOKENS, model_width), grad_attn, grad_mlp, grad_gains, next_attn, next_mlp, next_gains, velocity_attn, velocity_mlp, velocity_gains, average_attn, average_mlp, average_gains, copy_attn, copy_mlp, copy_gains)
```

```python
import functools
import math

import jax
import jax.numpy as jnp
import numpy as np
from jax import lax
from jax.experimental import pallas as pl
from jax.experimental.pallas import tpu as pltpu
from jax.sharding import PartitionSpec as P

HEAD = 64
STEP = 5
WARMUP = 10
EPSILON = 1e-05
MASKED = -1e30
MOMENTUM = 0.5
DECAY = 0.5
PEAK_RATE = 0.1
LANES = 128
BLOCK = 256

f32 = jnp.float32
bf16 = jnp.bfloat16


def nn(left, right):
    return jnp.dot(left, right, preferred_element_type=f32)


def nt(left, right):
    return lax.dot_general(
        left, right, (((1,), (1,)), ((), ())), preferred_element_type=f32
    )


def rotary_tables(row_count):
    half = HEAD // 2
    frequency = np.float32(10000.0) ** (-np.arange(half, dtype=np.float32) / np.float32(half))
    angles = np.arange(row_count, dtype=np.float32)[None, :] * frequency.astype(np.float32)[:, None]
    angles = angles.astype(np.float64)
    split = lambda t: np.ascontiguousarray(
        t.astype(np.float32).reshape(half, row_count // BLOCK, BLOCK).transpose(1, 0, 2)
    )
    return split(np.cos(angles)), split(np.sin(angles))


def rotate_rows(rows, cosine, sine):
    half = HEAD // 2
    first, second = rows[:half], rows[half:]
    return jnp.concatenate(
        [first * cosine - second * sine, second * cosine + first * sine], axis=0
    )


def rms_scale(rows):
    return lax.rsqrt(jnp.mean(rows * rows, axis=-1, keepdims=True) + EPSILON)


def block_kernel(
    doc_ref,
    x_ref,
    cot_ref,
    cos_ref,
    sin_ref,
    gain_ref,
    w_ref,
    out_ref,
    input_grad_ref,
    gain_grad_ref,
    g_out,
    g_ref,
    g_sem,
    y_ref,
    total_ref,
    dn_ref,
    n1t_ref,
    qt_ref,
    kt_ref,
    vt_ref,
    k_ref,
    v_ref,
    mixt_ref,
    n2_ref,
    n2t_ref,
    cott_ref,
    hid_ref,
    dgu_ref,
    lse_ref,
    cost_ref,
    sint_ref,
    acc_ref,
):
    row_count, width = x_ref.shape
    blocks = row_count // BLOCK
    pairs = width // LANES
    thirds = pairs // 2
    half_width = width // 2
    mlp_chunks = w_ref.shape[0] - thirds - 1
    slots = g_ref.shape[0]

    def load_w(chunk, half):
        return w_ref[chunk, half].reshape(width, half_width)

    def store_g(chunk, half, lanes, value):
        g_ref[chunk % slots, half, :, lanes] = value.astype(bf16)

    def grad_copy(chunk):
        slot = chunk % slots
        return pltpu.make_async_copy(g_ref.at[slot], g_out.at[chunk], g_sem.at[slot])

    def before_chunk(chunk):
        @pl.when(chunk >= slots)
        def _():
            grad_copy(chunk - slots).wait()

    def after_chunk(chunk):
        grad_copy(chunk).start()

    docs = [doc_ref[BLOCK * j] for j in range(blocks)]
    bias = [
        [jnp.where(docs[i] == docs[j], 0.0, MASKED).astype(f32) for j in range(i)] + [0.0]
        for i in range(blocks)
    ]
    causal = lax.broadcasted_iota(jnp.int32, (BLOCK, BLOCK), 0) <= lax.broadcasted_iota(
        jnp.int32, (BLOCK, BLOCK), 1
    )
    gain_one = gain_ref[0:1, :]
    gain_two = gain_ref[1:2, :]

    def rows_of(i):
        return pl.ds(i * BLOCK, BLOCK)

    for i in range(blocks):
        place = sum([(docs[j] == docs[i]).astype(jnp.int32) for j in range(i)], jnp.int32(0))
        cost_ref[:, rows_of(i)] = cos_ref[place]
        sint_ref[:, rows_of(i)] = sin_ref[place]
        stream = x_ref[rows_of(i), :].astype(f32)
        normed = (stream * rms_scale(stream) * gain_one).astype(bf16)
        n1t_ref[:, rows_of(i)] = normed.T
        cott_ref[:, rows_of(i)] = cot_ref[rows_of(i), :].T
        dn_ref[rows_of(i), :] = jnp.zeros((BLOCK, width), f32)

    def masked_pair(rows, h):
        zero = jnp.zeros((HEAD, BLOCK), bf16)
        parts = [rows[:HEAD], zero] if h == 0 else [zero, rows[HEAD:]]
        return jnp.concatenate(parts, axis=0)

    def scores_of(p, i, h):
        span = (i + 1) * BLOCK
        query = masked_pair(qt_ref[p, :, rows_of(i)], h)
        scores = nn(k_ref[p, pl.ds(0, span), :], query)
        parts = [scores[j * BLOCK : (j + 1) * BLOCK] for j in range(i + 1)]
        parts[i] = jnp.where(causal, parts[i], MASKED)
        return parts

    def attention_forward(p, carry):
        weights_t = load_w(p // 2, p % 2).T
        for i in range(blocks):
            cosine, sine = cost_ref[:, rows_of(i)], sint_ref[:, rows_of(i)]
            projected = nn(weights_t, n1t_ref[:, rows_of(i)])
            for h in range(2):
                lo, hi = h * HEAD, (h + 1) * HEAD
                query = rotate_rows(projected[lo:hi], cosine, sine).astype(bf16)
                qt_ref[p, lo:hi, rows_of(i)] = query * bf16(0.125)
                key = rotate_rows(projected[LANES + lo : LANES + hi], cosine, sine)
                kt_ref[p, lo:hi, rows_of(i)] = key.astype(bf16)
            vt_ref[p, :, rows_of(i)] = projected[2 * LANES :].astype(bf16)
            k_ref[p, rows_of(i), :] = kt_ref[p, :, rows_of(i)].T
            v_ref[p, rows_of(i), :] = vt_ref[p, :, rows_of(i)].T
        for i in range(blocks):
            span = (i + 1) * BLOCK
            for h in range(2):
                parts = scores_of(p, i, h)
                tops = [
                    jnp.max(part, axis=0, keepdims=True) + bias[i][j]
                    for j, part in enumerate(parts)
                ]
                top = functools.reduce(jnp.maximum, tops)
                exps = [jnp.exp(part - (top - bias[i][j])) for j, part in enumerate(parts)]
                total = sum([jnp.sum(e, axis=0, keepdims=True) for e in exps])
                exps_low = jnp.concatenate([e.astype(bf16) for e in exps], axis=0)
                heads = pl.ds(h * HEAD, HEAD)
                mixed = nn(vt_ref[p, heads, pl.ds(0, span)], exps_low)
                mixt_ref[p, heads, rows_of(i)] = (mixed * (1.0 / total)).astype(bf16)
                lse_ref[p, h : h + 1, rows_of(i)] = top + jnp.log(total)
        return carry

    lax.fori_loop(0, pairs, attention_forward, 0)

    out_chunk = thirds
    for i in range(blocks):
        mixed = mixt_ref[:, :, rows_of(i)].reshape(width, BLOCK).T
        branch = jnp.concatenate(
            [nn(mixed, load_w(out_chunk, half)) for half in range(2)], axis=1
        )
        after = x_ref[rows_of(i), :].astype(f32) + branch
        y_ref[rows_of(i), :] = after
        total_ref[rows_of(i), :] = after
        normed = (after * rms_scale(after) * gain_two).astype(bf16)
        n2_ref[rows_of(i), :] = normed
        n2t_ref[:, :, rows_of(i)] = normed.T.reshape(pairs, LANES, BLOCK)

    def feed_forward(chunk, carry):
        before_chunk(chunk)
        low = [load_w(thirds + 1 + chunk, half) for half in range(2)]
        w_gu = [w[:, : 2 * LANES] for w in low]
        w_gu_all = jnp.concatenate(w_gu, axis=1)
        w_down = jnp.concatenate([w[:, 2 * LANES :] for w in low], axis=1)
        for i in range(blocks):
            normed = n2_ref[rows_of(i), :]
            d_hidden = nn(cot_ref[rows_of(i), :], w_down)
            for half in range(2):
                gate_up = nn(normed, w_gu[half])
                gate, up = gate_up[:, :LANES], gate_up[:, LANES:]
                back = d_hidden[:, half * LANES : (half + 1) * LANES]
                sig = jax.nn.sigmoid(gate)
                silu = gate * sig
                lanes = pl.ds(half * LANES, LANES)
                hid_ref[rows_of(i), lanes] = (silu * up).astype(bf16)
                dgu_ref[rows_of(i), pl.ds(2 * half * LANES, LANES)] = (
                    back * up * (sig + silu * (1.0 - sig))
                ).astype(bf16)
                dgu_ref[rows_of(i), pl.ds((2 * half + 1) * LANES, LANES)] = (
                    back * silu
                ).astype(bf16)
            total_ref[rows_of(i), :] += nt(hid_ref[rows_of(i), :], w_down)
            dn_ref[rows_of(i), :] += nt(dgu_ref[rows_of(i), :], w_gu_all)
        n2t = n2t_ref[...].reshape(width, row_count)
        for half in range(2):
            store_g(
                chunk,
                half,
                pl.ds(0, 2 * LANES),
                nn(n2t, dgu_ref[:, pl.ds(2 * half * LANES, 2 * LANES)]),
            )
        grad_down = nn(cott_ref[...], hid_ref[...])
        for half in range(2):
            store_g(
                chunk,
                half,
                pl.ds(2 * LANES, LANES),
                grad_down[:, half * LANES : (half + 1) * LANES],
            )
        after_chunk(chunk)
        return carry

    lax.fori_loop(0, mlp_chunks, feed_forward, 0)

    gain_grad_two = jnp.zeros((1, width), f32)
    for i in range(blocks):
        after = y_ref[rows_of(i), :]
        scale = rms_scale(after)
        unit = after * scale
        d_normed = dn_ref[rows_of(i), :]
        d_unit = d_normed * gain_two
        gain_grad_two += jnp.sum(d_normed * unit, axis=0, keepdims=True)
        grad_after = cot_ref[rows_of(i), :].astype(f32) + scale * (
            d_unit - unit * jnp.mean(d_unit * unit, axis=-1, keepdims=True)
        )
        y_ref[rows_of(i), :] = grad_after
        n2_ref[rows_of(i), :] = grad_after.astype(bf16)
        out_ref[rows_of(i), :] = total_ref[rows_of(i), :].astype(bf16)
        dn_ref[rows_of(i), :] = jnp.zeros((BLOCK, width), f32)

    before_chunk(mlp_chunks)
    mixt = mixt_ref[...].reshape(width, row_count)
    for half in range(2):
        store_g(
            mlp_chunks,
            half,
            pl.ds(0, half_width),
            nn(mixt, n2_ref[:, pl.ds(half * half_width, half_width)]),
        )
    after_chunk(mlp_chunks)
    dmt_ref = n2t_ref
    w_out = jnp.concatenate([load_w(out_chunk, half) for half in range(2)], axis=1)
    for i in range(blocks):
        d_mixed = nt(w_out, n2_ref[rows_of(i), :])
        dmt_ref[:, :, rows_of(i)] = d_mixed.astype(bf16).reshape(pairs, LANES, BLOCK)

    def attention_backward(p, carry):
        acc_ref[1] = jnp.zeros((LANES, row_count), f32)
        acc_ref[2] = jnp.zeros((LANES, row_count), f32)
        for i in range(blocks):
            span = (i + 1) * BLOCK
            for h in range(2):
                heads = pl.ds(h * HEAD, HEAD)
                parts = scores_of(p, i, h)
                lse = lse_ref[p, h : h + 1, rows_of(i)]
                probs = [jnp.exp(part - (lse - bias[i][j])) for j, part in enumerate(parts)]
                probs = jnp.concatenate(probs, axis=0)
                back = masked_pair(dmt_ref[p, :, rows_of(i)], h)
                d_probs = nn(v_ref[p, pl.ds(0, span), :], back)
                weighted = probs * d_probs
                inner = jnp.sum(weighted, axis=0, keepdims=True)
                d_scores = (weighted - probs * inner).astype(bf16)
                acc_ref[0, heads, rows_of(i)] = nn(
                    kt_ref[p, heads, pl.ds(0, span)], d_scores
                )
                acc_ref[1, heads, pl.ds(0, span)] += nt(
                    qt_ref[p, heads, rows_of(i)], d_scores
                )
                acc_ref[2, heads, pl.ds(0, span)] += nt(
                    dmt_ref[p, heads, rows_of(i)], probs.astype(bf16)
                )
        dqkv_ref = dgu_ref
        for i in range(blocks):
            cosine, sine = cost_ref[:, rows_of(i)], -sint_ref[:, rows_of(i)]
            pieces = []
            for kind in range(2):
                for h in range(2):
                    piece = acc_ref[kind, pl.ds(h * HEAD, HEAD), rows_of(i)]
                    piece = rotate_rows(piece, cosine, sine)
                    pieces.append((piece * 0.125 if kind == 0 else piece).astype(bf16))
            pieces.append(acc_ref[2, :, rows_of(i)].astype(bf16))
            dqkv_ref[rows_of(i), pl.ds(0, 3 * LANES)] = jnp.concatenate(pieces, axis=0).T
        weights = load_w(p // 2, p % 2)
        chunk = mlp_chunks + 1 + p // 2

        @pl.when(p % 2 == 0)
        def _():
            before_chunk(chunk)

        d_qkv = dqkv_ref[:, pl.ds(0, 3 * LANES)]
        store_g(chunk, p % 2, pl.ds(0, half_width), nn(n1t_ref[...], d_qkv))

        @pl.when(p % 2 == 1)
        def _():
            after_chunk(chunk)

        for i in range(blocks):
            dn_ref[rows_of(i), :] += nt(dqkv_ref[rows_of(i), pl.ds(0, 3 * LANES)], weights)
        return carry

    lax.fori_loop(0, pairs, attention_backward, 0)

    gain_grad_one = jnp.zeros((1, width), f32)
    for i in range(blocks):
        stream = x_ref[rows_of(i), :].astype(f32)
        scale = rms_scale(stream)
        unit = stream * scale
        d_normed = dn_ref[rows_of(i), :]
        d_unit = d_normed * gain_one
        gain_grad_one += jnp.sum(d_normed * unit, axis=0, keepdims=True)
        input_grad_ref[rows_of(i), :] = (
            y_ref[rows_of(i), :]
            + scale * (d_unit - unit * jnp.mean(d_unit * unit, axis=-1, keepdims=True))
        ).astype(bf16)
    gain_grad_ref[...] = jnp.concatenate([gain_grad_one, gain_grad_two], axis=0)
    chunks = w_ref.shape[0]
    for chunk in range(chunks - slots, chunks):
        grad_copy(chunk).wait()


def local(
    tokens,
    doc_ids,
    cotangent,
    attn_weights,
    mlp_weights,
    gains,
    moment_attn,
    moment_mlp,
    moment_gains,
    ema_attn,
    ema_mlp,
    ema_gains,
):
    row_count, width = tokens.shape
    shard_rows = attn_weights.shape[0]
    group = width // shard_rows
    pairs = width // LANES
    hidden = mlp_weights.shape[1] // 3
    half_width = width // 2
    thirds = pairs // 2
    mlp_chunks = hidden // (2 * LANES)
    chunks = thirds + 1 + mlp_chunks

    def pack(attn, mlp):
        qkv = attn[:, : 3 * width].reshape(shard_rows, 3, pairs, LANES).transpose(2, 0, 1, 3)
        out = attn[:, 3 * width :].reshape(shard_rows, 2, half_width).transpose(1, 0, 2)
        ffn = mlp.reshape(shard_rows, 3, 2 * mlp_chunks, LANES).transpose(2, 0, 1, 3)
        return jnp.concatenate(
            [
                qkv.reshape(pairs, shard_rows, half_width),
                out,
                ffn.reshape(2 * mlp_chunks, shard_rows, half_width),
            ],
            axis=0,
        ).reshape(chunks, 2, shard_rows, half_width)

    packed = pack(attn_weights.astype(bf16), mlp_weights.astype(bf16))
    full = lax.all_gather(packed, "fsdp", axis=2, tiled=True)
    gain_rows = lax.all_gather(gains.astype(bf16), "fsdp", axis=1, tiled=True).astype(f32)
    cos_table, sin_table = rotary_tables(row_count)
    vmem = pl.BlockSpec(memory_space=pltpu.VMEM)
    hbm = pl.BlockSpec(memory_space=pl.ANY)
    slots = 3
    block_out, input_grad, gain_grads, grads = pl.pallas_call(
        block_kernel,
        out_shape=(
            jax.ShapeDtypeStruct((row_count, width), bf16),
            jax.ShapeDtypeStruct((row_count, width), bf16),
            jax.ShapeDtypeStruct((2, width), f32),
            jax.ShapeDtypeStruct((chunks, 2, width, half_width), bf16),
        ),
        in_specs=[pl.BlockSpec(memory_space=pltpu.SMEM)] + [vmem] * 6,
        out_specs=(vmem, vmem, vmem, hbm),
        scratch_shapes=[
            pltpu.VMEM((slots, 2, width, half_width), bf16),
            pltpu.SemaphoreType.DMA((slots,)),
            pltpu.VMEM((row_count, width), f32),
            pltpu.VMEM((row_count, width), f32),
            pltpu.VMEM((row_count, width), f32),
            pltpu.VMEM((width, row_count), bf16),
            pltpu.VMEM((pairs, LANES, row_count), bf16),
            pltpu.VMEM((pairs, LANES, row_count), bf16),
            pltpu.VMEM((pairs, LANES, row_count), bf16),
            pltpu.VMEM((pairs, row_count, LANES), bf16),
            pltpu.VMEM((pairs, row_count, LANES), bf16),
            pltpu.VMEM((pairs, LANES, row_count), bf16),
            pltpu.VMEM((row_count, width), bf16),
            pltpu.VMEM((pairs, LANES, row_count), bf16),
            pltpu.VMEM((width, row_count), bf16),
            pltpu.VMEM((row_count, 2 * LANES), bf16),
            pltpu.VMEM((row_count, 4 * LANES), bf16),
            pltpu.VMEM((pairs, 8, row_count), f32),
            pltpu.VMEM((HEAD // 2, row_count), f32),
            pltpu.VMEM((HEAD // 2, row_count), f32),
            pltpu.VMEM((3, LANES, row_count), f32),
        ],
        compiler_params=pltpu.CompilerParams(vmem_limit_bytes=63 * 2**20),
        name="block",
    )(doc_ids, tokens, cotangent, cos_table, sin_table, gain_rows, full)

    part = lax.psum_scatter(grads, "fsdp", scatter_dimension=2, tiled=True)
    part = lax.psum(part.astype(bf16), "rep").astype(f32)
    part = jnp.concatenate([part[mlp_chunks + 1 :], part[mlp_chunks:][:1], part[:mlp_chunks]])
    part = part.reshape(2 * chunks, shard_rows, half_width)
    qkv = part[:pairs].reshape(pairs, shard_rows, 3, LANES).transpose(1, 2, 0, 3)
    out = part[pairs : pairs + 2].transpose(1, 0, 2)
    ffn = part[pairs + 2 :].reshape(2 * mlp_chunks, shard_rows, 3, LANES).transpose(1, 2, 0, 3)
    grad_attn = jnp.concatenate(
        [qkv.reshape(shard_rows, 3 * width), out.reshape(shard_rows, width)], axis=1
    )
    grad_mlp = ffn.reshape(shard_rows, 3 * hidden)
    grad_gains = lax.psum_scatter(gain_grads, "fsdp", scatter_dimension=1, tiled=True)
    grad_gains = lax.psum(grad_gains, "rep")

    total_tokens = row_count * lax.axis_size("fsdp") * lax.axis_size("rep")
    rate = PEAK_RATE * STEP / (WARMUP * math.sqrt(total_tokens))

    def update(weight, grad, moment, average):
        velocity = MOMENTUM * moment + grad
        weight_new = weight - rate * (grad + MOMENTUM * velocity)
        average_new = DECAY * average + (1.0 - DECAY) * weight_new
        return (weight_new, velocity, average_new, weight_new.astype(bf16))

    kinds = [
        update(attn_weights, grad_attn, moment_attn, ema_attn),
        update(mlp_weights, grad_mlp, moment_mlp, ema_mlp),
        update(gains, grad_gains, moment_gains, ema_gains),
    ]
    return (block_out, input_grad, grad_attn, grad_mlp, grad_gains) + tuple(
        kind[what] for what in range(4) for kind in kinds
    )


def solution(mesh):
    rows = P(("fsdp", "rep"), None)
    shard = P("fsdp", None)
    columns = P(None, "fsdp")
    kinds = (shard, shard, columns)
    return jax.shard_map(
        local,
        mesh=mesh,
        in_specs=(rows, P(("fsdp", "rep")), rows) + kinds * 3,
        out_specs=(rows, rows) + kinds * 5,
        check_vma=False,
    )
```

```python
import functools
import math

import jax
import jax.numpy as jnp
import numpy as np
from jax import lax
from jax.experimental import pallas as pl
from jax.experimental.pallas import tpu as pltpu
from jax.sharding import PartitionSpec as P

HEAD = 64
STEP = 5
WARMUP = 10
EPSILON = 1e-05
MASKED = -1e30
MOMENTUM = 0.5
DECAY = 0.5
PEAK_RATE = 0.1
LANES = 128
BLOCK = 256

f32 = jnp.float32
bf16 = jnp.bfloat16


def nn(left, right):
    return jnp.dot(left, right, preferred_element_type=f32)


def nt(left, right):
    return lax.dot_general(
        left, right, (((1,), (1,)), ((), ())), preferred_element_type=f32
    )


def rotary_tables(row_count):
    half = HEAD // 2
    frequency = np.float32(10000.0) ** (-np.arange(half, dtype=np.float32) / np.float32(half))
    angles = np.arange(row_count, dtype=np.float32)[None, :] * frequency.astype(np.float32)[:, None]
    angles = angles.astype(np.float64)
    split = lambda t: np.ascontiguousarray(
        t.astype(np.float32).reshape(half, row_count // BLOCK, BLOCK).transpose(1, 0, 2)
    )
    return split(np.cos(angles)), split(np.sin(angles))


def rotate_rows(rows, cosine, sine):
    half = HEAD // 2
    first, second = rows[:half], rows[half:]
    return jnp.concatenate(
        [first * cosine - second * sine, second * cosine + first * sine], axis=0
    )


def rms_scale(rows):
    return lax.rsqrt(jnp.mean(rows * rows, axis=-1, keepdims=True) + EPSILON)


class Scratch:
    def __init__(self, names, refs):
        for name, ref in zip(names, refs, strict=True):
            setattr(self, name, ref)


def block_kernel(linked, names, *refs):
    s = Scratch(names, refs)
    row_count, width = s.x.shape
    blocks = row_count // BLOCK
    pairs = width // LANES
    thirds = pairs // 2
    half_width = width // 2
    chunks = s.w.shape[0]
    mlp_chunks = chunks - thirds - 1
    slots = s.g.shape[0]
    last_step = mlp_chunks + 2 * thirds

    def rows_of(i):
        return pl.ds(i * BLOCK, BLOCK)

    def load_w(chunk, half):
        return s.w[chunk, half].reshape(width, half_width)

    def store_g(chunk, half, lanes, value):
        low = value.astype(bf16)
        if linked:
            low = low.reshape(s.g.shape[2:5] + (low.shape[1],))
            s.g[chunk % slots, half, :, :, :, lanes] = low
        else:
            s.g[chunk % slots, half, :, lanes] = low

    def chunk_of(step):
        return jnp.where(step <= mlp_chunks, step, mlp_chunks + (step - mlp_chunks) // 2)

    def is_step(step):
        late = (step > mlp_chunks) & ((step - mlp_chunks) % 2 == 0) & (step <= last_step)
        return (step >= 0) & ((step <= mlp_chunks) | late)

    if linked:
        gather_start, gather_step, reduce_step, gain_sum = links(
            s, chunks, thirds, mlp_chunks, chunk_of, is_step
        )
    else:

        def gather_start():
            pass

        def gather_step(step):
            pass

        def grad_copy(chunk):
            slot = chunk % slots
            return pltpu.make_async_copy(s.g.at[slot], s.g_out.at[chunk], s.g_sem.at[slot])

        def reduce_step(step):
            @pl.when(is_step(step - 1))
            def _():
                grad_copy(chunk_of(step - 1)).wait()

            @pl.when(is_step(step))
            def _():
                grad_copy(chunk_of(step)).start()

    copies = [
        pltpu.make_async_copy(s.x_in, s.x, s.local_sem.at[0]),
        pltpu.make_async_copy(s.cot_in, s.cot, s.local_sem.at[1]),
    ]
    for copy in copies:
        copy.start()

    docs = [s.doc[BLOCK * j] for j in range(blocks)]
    bias = [
        [jnp.where(docs[i] == docs[j], 0.0, MASKED).astype(f32) for j in range(i)] + [0.0]
        for i in range(blocks)
    ]
    causal = lax.broadcasted_iota(jnp.int32, (BLOCK, BLOCK), 0) <= lax.broadcasted_iota(
        jnp.int32, (BLOCK, BLOCK), 1
    )

    gather_start()
    for i in range(blocks):
        place = sum([(docs[j] == docs[i]).astype(jnp.int32) for j in range(i)], jnp.int32(0))
        s.cost[:, rows_of(i)] = s.cos[place]
        s.sint[:, rows_of(i)] = s.sin[place]
    for copy in copies:
        copy.wait()
    gather_step(0)
    for i in range(blocks):
        s.cott[:, rows_of(i)] = s.cot[rows_of(i), :].T
        if i < 2:
            gather_step(i + 1)
    gain_one = s.gain[0:1, :]
    gain_two = s.gain[1:2, :]
    for i in range(blocks):
        stream = s.x[rows_of(i), :].astype(f32)
        normed = (stream * rms_scale(stream) * gain_one).astype(bf16)
        s.n1t[:, rows_of(i)] = normed.T
        s.dn[rows_of(i), :] = jnp.zeros((BLOCK, width), f32)
    gather_step(3)

    def masked_pair(rows, h):
        zero = jnp.zeros((HEAD, BLOCK), bf16)
        parts = [rows[:HEAD], zero] if h == 0 else [zero, rows[HEAD:]]
        return jnp.concatenate(parts, axis=0)

    def scores_of(p, i, h):
        span = (i + 1) * BLOCK
        query = masked_pair(s.qt[p, :, rows_of(i)], h)
        scores = nn(s.k[p, pl.ds(0, span), :], query)
        parts = [scores[j * BLOCK : (j + 1) * BLOCK] for j in range(i + 1)]
        parts[i] = jnp.where(causal, parts[i], MASKED)
        return parts

    def attention_forward(p, carry):
        @pl.when((p == 1) | (p == 2))
        def _():
            gather_step(p + 3)

        @pl.when(p >= 4)
        def _():
            gather_step(p + 2)

        weights_t = load_w(p // 2, p % 2).T
        for i in range(blocks):
            cosine, sine = s.cost[:, rows_of(i)], s.sint[:, rows_of(i)]
            projected = nn(weights_t, s.n1t[:, rows_of(i)])
            for h in range(2):
                lo, hi = h * HEAD, (h + 1) * HEAD
                query = rotate_rows(projected[lo:hi], cosine, sine).astype(bf16)
                s.qt[p, lo:hi, rows_of(i)] = query * bf16(0.125)
                key = rotate_rows(projected[LANES + lo : LANES + hi], cosine, sine)
                s.kt[p, lo:hi, rows_of(i)] = key.astype(bf16)
            s.vt[p, :, rows_of(i)] = projected[2 * LANES :].astype(bf16)
            s.k[p, rows_of(i), :] = s.kt[p, :, rows_of(i)].T
            s.v[p, rows_of(i), :] = s.vt[p, :, rows_of(i)].T
        for i in range(blocks):
            span = (i + 1) * BLOCK
            for h in range(2):
                parts = scores_of(p, i, h)
                tops = [
                    jnp.max(part, axis=0, keepdims=True) + bias[i][j]
                    for j, part in enumerate(parts)
                ]
                top = functools.reduce(jnp.maximum, tops)
                exps = [jnp.exp(part - (top - bias[i][j])) for j, part in enumerate(parts)]
                total = sum([jnp.sum(e, axis=0, keepdims=True) for e in exps])
                exps_low = jnp.concatenate([e.astype(bf16) for e in exps], axis=0)
                heads = pl.ds(h * HEAD, HEAD)
                mixed = nn(s.vt[p, heads, pl.ds(0, span)], exps_low)
                s.mixt[p, heads, rows_of(i)] = (mixed * (1.0 / total)).astype(bf16)
                s.lse[p, h : h + 1, rows_of(i)] = top + jnp.log(total)
        return carry

    lax.fori_loop(0, pairs, attention_forward, 0)

    out_chunk = thirds
    for i in range(blocks):
        mixed = s.mixt[:, :, rows_of(i)].reshape(width, BLOCK).T
        branch = jnp.concatenate(
            [nn(mixed, load_w(out_chunk, half)) for half in range(2)], axis=1
        )
        after = s.x[rows_of(i), :].astype(f32) + branch
        s.y[rows_of(i), :] = after
        s.total[rows_of(i), :] = after
        normed = (after * rms_scale(after) * gain_two).astype(bf16)
        s.n2[rows_of(i), :] = normed
        s.n2t[:, :, rows_of(i)] = normed.T.reshape(pairs, LANES, BLOCK)

    def feed_forward(chunk, carry):
        gather_step(chunk + pairs + 2)
        low = [load_w(thirds + 1 + chunk, half) for half in range(2)]
        w_gu = [w[:, : 2 * LANES] for w in low]
        w_gu_all = jnp.concatenate(w_gu, axis=1)
        w_down = jnp.concatenate([w[:, 2 * LANES :] for w in low], axis=1)
        for i in range(blocks):
            normed = s.n2[rows_of(i), :]
            d_hidden = nn(s.cot[rows_of(i), :], w_down)
            for half in range(2):
                gate_up = nn(normed, w_gu[half])
                gate, up = gate_up[:, :LANES], gate_up[:, LANES:]
                back = d_hidden[:, half * LANES : (half + 1) * LANES]
                sig = jax.nn.sigmoid(gate)
                silu = gate * sig
                s.hid[rows_of(i), pl.ds(half * LANES, LANES)] = (silu * up).astype(bf16)
                s.dgu[rows_of(i), pl.ds(2 * half * LANES, LANES)] = (
                    back * up * (sig + silu * (1.0 - sig))
                ).astype(bf16)
                s.dgu[rows_of(i), pl.ds((2 * half + 1) * LANES, LANES)] = (
                    back * silu
                ).astype(bf16)
            s.total[rows_of(i), :] += nt(s.hid[rows_of(i), :], w_down)
            s.dn[rows_of(i), :] += nt(s.dgu[rows_of(i), :], w_gu_all)
        n2t = s.n2t[...].reshape(width, row_count)
        for half in range(2):
            store_g(
                chunk,
                half,
                pl.ds(0, 2 * LANES),
                nn(n2t, s.dgu[:, pl.ds(2 * half * LANES, 2 * LANES)]),
            )
        grad_down = nn(s.cott[...], s.hid[...])
        for half in range(2):
            store_g(
                chunk,
                half,
                pl.ds(2 * LANES, LANES),
                grad_down[:, half * LANES : (half + 1) * LANES],
            )
        reduce_step(chunk)
        return carry

    lax.fori_loop(0, mlp_chunks, feed_forward, 0)

    gain_grad_two = jnp.zeros((1, width), f32)
    for i in range(blocks):
        after = s.y[rows_of(i), :]
        scale = rms_scale(after)
        unit = after * scale
        d_normed = s.dn[rows_of(i), :]
        d_unit = d_normed * gain_two
        gain_grad_two += jnp.sum(d_normed * unit, axis=0, keepdims=True)
        grad_after = s.cot[rows_of(i), :].astype(f32) + scale * (
            d_unit - unit * jnp.mean(d_unit * unit, axis=-1, keepdims=True)
        )
        s.y[rows_of(i), :] = grad_after
        s.n2[rows_of(i), :] = grad_after.astype(bf16)
        s.cot[rows_of(i), :] = s.total[rows_of(i), :].astype(bf16)
        s.dn[rows_of(i), :] = jnp.zeros((BLOCK, width), f32)
    out_copy = pltpu.make_async_copy(s.cot, s.block_out, s.local_sem.at[0])
    out_copy.start()

    mixt = s.mixt[...].reshape(width, row_count)
    for half in range(2):
        store_g(
            mlp_chunks,
            half,
            pl.ds(0, half_width),
            nn(mixt, s.n2[:, pl.ds(half * half_width, half_width)]),
        )
    reduce_step(mlp_chunks)
    dmt = s.n2t
    w_out = jnp.concatenate([load_w(out_chunk, half) for half in range(2)], axis=1)
    for i in range(blocks):
        d_mixed = nt(w_out, s.n2[rows_of(i), :])
        dmt[:, :, rows_of(i)] = d_mixed.astype(bf16).reshape(pairs, LANES, BLOCK)

    def attention_backward(p, carry):
        s.acc[1] = jnp.zeros((LANES, row_count), f32)
        s.acc[2] = jnp.zeros((LANES, row_count), f32)
        for i in range(blocks):
            span = (i + 1) * BLOCK
            for h in range(2):
                heads = pl.ds(h * HEAD, HEAD)
                parts = scores_of(p, i, h)
                lse = s.lse[p, h : h + 1, rows_of(i)]
                probs = [jnp.exp(part - (lse - bias[i][j])) for j, part in enumerate(parts)]
                probs = jnp.concatenate(probs, axis=0)
                back = masked_pair(dmt[p, :, rows_of(i)], h)
                d_probs = nn(s.v[p, pl.ds(0, span), :], back)
                weighted = probs * d_probs
                inner = jnp.sum(weighted, axis=0, keepdims=True)
                d_scores = (weighted - probs * inner).astype(bf16)
                s.acc[0, heads, rows_of(i)] = nn(s.kt[p, heads, pl.ds(0, span)], d_scores)
                s.acc[1, heads, pl.ds(0, span)] += nt(s.qt[p, heads, rows_of(i)], d_scores)
                s.acc[2, heads, pl.ds(0, span)] += nt(
                    dmt[p, heads, rows_of(i)], probs.astype(bf16)
                )
        for i in range(blocks):
            cosine, sine = s.cost[:, rows_of(i)], -s.sint[:, rows_of(i)]
            pieces = []
            for kind in range(2):
                for h in range(2):
                    piece = s.acc[kind, pl.ds(h * HEAD, HEAD), rows_of(i)]
                    piece = rotate_rows(piece, cosine, sine)
                    pieces.append((piece * 0.125 if kind == 0 else piece).astype(bf16))
            pieces.append(s.acc[2, :, rows_of(i)].astype(bf16))
            s.dgu[rows_of(i), pl.ds(0, 3 * LANES)] = jnp.concatenate(pieces, axis=0).T
        weights = load_w(p // 2, p % 2)
        store_g(
            mlp_chunks + 1 + p // 2,
            p % 2,
            pl.ds(0, half_width),
            nn(s.n1t[...], s.dgu[:, pl.ds(0, 3 * LANES)]),
        )
        reduce_step(mlp_chunks + 1 + p)
        for i in range(blocks):
            s.dn[rows_of(i), :] += nt(s.dgu[rows_of(i), pl.ds(0, 3 * LANES)], weights)
        return carry

    lax.fori_loop(0, pairs, attention_backward, 0)

    reduce_step(last_step + 1)
    gain_grad_one = jnp.zeros((1, width), f32)
    for i in range(blocks):
        stream = s.x[rows_of(i), :].astype(f32)
        scale = rms_scale(stream)
        unit = stream * scale
        d_normed = s.dn[rows_of(i), :]
        d_unit = d_normed * gain_one
        gain_grad_one += jnp.sum(d_normed * unit, axis=0, keepdims=True)
        s.x[rows_of(i), :] = (
            s.y[rows_of(i), :]
            + scale * (d_unit - unit * jnp.mean(d_unit * unit, axis=-1, keepdims=True))
        ).astype(bf16)
    grad_copy_out = pltpu.make_async_copy(s.x, s.input_grad, s.local_sem.at[1])
    grad_copy_out.start()
    gain_grads = jnp.concatenate(
        [gain_grad_one, gain_grad_two, jnp.zeros((6, width), f32)], axis=0
    )
    if linked:
        gain_sum[0](gain_grads)
        reduce_step(last_step + 2)
        gain_sum[1]()
        reduce_step(last_step + 3)
        gain_sum[2]()
        reduce_step(last_step + 4)
        gain_sum[3]()
        reduce_step(last_step + 5)
        s.g_out[...] = s.gout[...]
    else:
        s.gain_out[...] = gain_grads
    out_copy.wait()
    grad_copy_out.wait()


def links(s, chunks, thirds, mlp_chunks, chunk_of, is_step):
    planes = s.w.shape[2]
    me = lax.axis_index("fsdp")
    core = lax.axis_index("rep")
    z, m = me // 4, me % 4
    over_x, over_y, over_both = m + 1 - 2 * (m % 2), (m + 2) % 4, 3 - m
    m1 = (1 - core) * over_x + core * over_y
    m2 = (1 - core) * over_y + core * over_x
    m3 = over_both
    other = 1 - core

    def chip(plane, place):
        return (plane * 4 + place, core)

    sibling = (me, other)

    def far(k):
        return (z + k) % planes

    peers = [chip(far(k), m) for k in range(1, planes)]

    def remote(src, dst, sems, index, device):
        return pltpu.make_async_remote_copy(
            src_ref=src,
            dst_ref=dst,
            send_sem=sems.at[(0,) + index],
            recv_sem=sems.at[(1,) + index],
            device_id=device,
            device_id_type=pl.DeviceIdType.MESH,
        )

    def along_z(chunk, k):
        block = s.w.at[chunk, core, z, m]
        return remote(block, block, s.z_sem, (chunk, k), peers[k])

    def line(chunk, place, index, device):
        block = s.w.at[chunk, core, :, place]
        return remote(block, block, s.line_sem, (chunk, index), device)

    hops = [
        (m, chip(z, m1)),
        (m, chip(z, m2)),
        (m1, chip(z, m2)),
        (m, sibling),
        (m1, sibling),
        (m2, sibling),
        (m3, sibling),
    ]

    def hop(chunk, index):
        return line(chunk, hops[index][0], index, hops[index][1])

    def gain_along_z(k):
        block = s.gt.at[z, m]
        return remote(block, block, s.gain_sem, (k,), peers[k])

    def gain_line(place, index, device):
        block = s.gt.at[:, place]
        return remote(block, block, s.gain_sem, (planes - 1 + index,), device)

    def gain_hop(index):
        return gain_line(hops[index][0], index, hops[index][1])

    width = s.x.shape[1]
    pairs = width // LANES
    shard_rows = s.w.shape[4]
    half_width = s.w.shape[5]
    hidden = s.mlp_in.shape[1] // 3

    def gather_start():
        loads = [
            pltpu.make_async_copy(
                s.attn_in.at[:, pl.ds(k * width, width)],
                s.dn.at[pl.ds(k * shard_rows, shard_rows)],
                s.load_sem.at[k],
            )
            for k in range(4)
        ] + [
            pltpu.make_async_copy(
                s.mlp_in.at[:, pl.ds(k * width, width)],
                s.dn.at[pl.ds((4 + k) * shard_rows, shard_rows)],
                s.load_sem.at[4 + k],
            )
            for k in range(3 * hidden // width)
        ]
        for load in loads:
            load.start()
        barrier = pltpu.get_barrier_semaphore()
        partners = [chip(z, over_x), chip(z, over_y), chip(z, over_both), sibling] + peers
        for partner in partners:
            pl.semaphore_signal(
                barrier, inc=1, device_id=partner, device_id_type=pl.DeviceIdType.MESH
            )
        own = s.gains_in[...].astype(bf16)
        own = jnp.concatenate([own, jnp.zeros((2, LANES - shard_rows), bf16)], axis=1)
        s.gt[z, m] = jnp.concatenate([own, jnp.zeros((14, LANES), bf16)], axis=0)
        for load in loads:
            load.wait()

        def piece(row, lane):
            rows = s.dn[pl.ds(row * shard_rows, shard_rows), pl.ds(lane, LANES)]
            return rows.astype(bf16)

        for third in range(thirds):
            lane = pl.multiple_of((2 * third + core) * LANES, LANES)
            for kind in range(3):
                s.w[third, core, z, m, :, kind * LANES : (kind + 1) * LANES] = piece(kind, lane)
        lane = pl.multiple_of(core * half_width, LANES)
        s.w[thirds, core, z, m] = s.dn[
            pl.ds(3 * shard_rows, shard_rows), pl.ds(lane, half_width)
        ].astype(bf16)
        pl.semaphore_wait(barrier, len(partners))
        for k in range(planes - 1):
            gain_along_z(k).start()
        for chunk in range(thirds + 1):
            for k in range(planes - 1):
                along_z(chunk, k).start()
        for j in range(mlp_chunks):
            for kind in range(3):
                place = kind * hidden + 2 * j * LANES
                row, first = 4 + place // width, place % width
                lane = pl.multiple_of(first + core * LANES, LANES)
                s.w[thirds + 1 + j, core, z, m, :, kind * LANES : (kind + 1) * LANES] = piece(
                    row, lane
                )
            for k in range(planes - 1):
                along_z(thirds + 1 + j, k).start()

    def gather_step(step):
        early = isinstance(step, int) and step < 3
        if early and step == 0:
            for k in range(planes - 1):
                gain_along_z(k).wait()
            gain_hop(0).start()
            gain_hop(1).start()
        if early and step == 1:
            gain_hop(0).wait()
            gain_hop(2).start()
        if early and step == 2:
            gain_hop(1).wait()
            gain_hop(2).wait()
            rows = jnp.zeros((8, width), f32)
            for d in range(planes * 4):
                tile = s.gt[d // 4, d % 4].astype(f32)[:8]
                wide = jnp.concatenate([tile, jnp.zeros((8, width - LANES), f32)], axis=1)
                rows += pltpu.roll(wide, d * shard_rows, 1) if d else wide
            s.gain[...] = rows

        def stage(chunk, todo):
            if isinstance(chunk, int):
                if 0 <= chunk < chunks:
                    todo(chunk)
            else:
                pl.when((chunk >= 0) & (chunk < chunks))(lambda: todo(chunk))

        def ready(chunk):
            for index in range(3, 7):
                hop(chunk, index).wait_recv()
            for k in range(planes - 1):
                along_z(chunk, k).wait_send()
            for index in range(7):
                hop(chunk, index).wait_send()

        def third_hop(chunk):
            hop(chunk, 1).wait_recv()
            hop(chunk, 5).start()
            hop(chunk, 2).wait_recv()
            hop(chunk, 6).start()

        def second_hop(chunk):
            hop(chunk, 0).wait_recv()
            hop(chunk, 2).start()
            hop(chunk, 4).start()

        def first_hop(chunk):
            for k in range(planes - 1):
                along_z(chunk, k).wait_recv()
            for index in (0, 1, 3):
                hop(chunk, index).start()

        stage(step, first_hop)
        stage(step - 1, second_hop)
        stage(step - 2, third_hop)
        stage(step - 3, ready)

    def to_sibling(step):
        chunk = chunk_of(step)
        return remote(
            s.g.at[chunk % 2, other], s.a.at[chunk % 4], s.rs_sem, (step, 0), sibling
        )

    def to_second(step):
        return remote(s.bs, s.b.at[chunk_of(step) % 2], s.rs_sem, (step, 1), chip(z, m2))

    def to_first(step):
        return remote(s.cs, s.c.at[chunk_of(step) % 2], s.rs_sem, (step, 2), chip(z, m1))

    def to_plane(step, k):
        return remote(
            s.ds.at[far(k + 1)],
            s.d.at[chunk_of(step) % 2, k],
            s.rs_sem,
            (step, 3 + k),
            peers[k],
        )

    def half_block(step):
        place = jnp.where(
            step < mlp_chunks,
            thirds + 1 + step,
            jnp.where(step == mlp_chunks, thirds, (step - mlp_chunks) // 2 - 1),
        )
        return s.gout.at[place, core]

    def to_copy(step):
        block = half_block(step)
        return remote(block, block, s.rs_sem, (step, 2 + planes), sibling)

    def reduce_step(step):
        def when(number, todo):
            pl.when(is_step(number))(lambda: todo(number))

        def begin(number):
            to_sibling(number).start()

        def halves(number):
            chunk = chunk_of(number)
            to_sibling(number).wait()

            def both(place):
                return s.g[chunk % 2, core, :, place].astype(f32) + s.a[
                    chunk % 4, :, place
                ].astype(f32)

            s.bs[:, 0] = both(m2).astype(bf16)
            s.bs[:, 1] = both(m3).astype(bf16)
            to_second(number).start()
            s.h[:, 0] = both(m).astype(bf16)
            s.h[:, 1] = both(m1).astype(bf16)

        def quarters(number):
            chunk = chunk_of(number)
            to_second(number).wait()
            s.cs[...] = (s.h[:, 1].astype(f32) + s.b[chunk % 2, :, 1].astype(f32)).astype(bf16)
            to_first(number).start()
            s.kept[...] = s.h[:, 0].astype(f32) + s.b[chunk % 2, :, 0].astype(f32)

        def lines(number):
            chunk = chunk_of(number)
            to_first(number).wait()
            s.kept[...] = s.kept[...] + s.c[chunk % 2].astype(f32)
            s.ds[...] = s.kept[...].astype(bf16)
            for k in range(planes - 1):
                to_plane(number, k).start()
            s.own[...] = s.kept[z]

        def last(number):
            chunk = chunk_of(number)
            total = s.own[...]
            for k in range(planes - 1):
                to_plane(number, k).wait()
                total += s.d[chunk % 2, k].astype(f32)
            half_block(number)[...] = total
            to_copy(number).start()

        def end(number):
            to_copy(number).wait()

        when(step, begin)
        when(step - 5, end)
        when(step - 4, last)
        when(step - 3, lines)
        when(step - 2, quarters)
        when(step - 1, halves)

    def plane_sum():
        block = s.gp.at[m]
        return [
            remote(block, block, s.gsum_sem, (k,), chip(z, place))
            for k, place in enumerate([over_x, over_y, over_both])
        ]

    def line_sum():
        block = s.gz.at[z]
        return [
            remote(block, block, s.gsum_sem, (3 + k,), peers[k]) for k in range(planes - 1)
        ]

    def core_sum():
        return remote(s.gc.at[0], s.gc.at[1], s.gsum_sem, (2 + planes,), sibling)

    def gain_begin(value):
        s.gp[m] = value
        for copy in plane_sum():
            copy.start()

    def gain_lines_sum():
        for copy in plane_sum():
            copy.wait()
        s.gz[z] = (s.gp[0] + s.gp[1]) + (s.gp[2] + s.gp[3])
        for copy in line_sum():
            copy.start()

    def gain_cores():
        for copy in line_sum():
            copy.wait()
        total = s.gz[0]
        for k in range(1, planes):
            total += s.gz[k]
        s.gc[0] = total
        core_sum().start()

    def gain_end():
        core_sum().wait()
        total = s.gc[0] + s.gc[1]
        s.gain_out[...] = pltpu.roll(total, (width - me * shard_rows) % width, 1)[:, :LANES]

    return gather_start, gather_step, reduce_step, (gain_begin, gain_lines_sum, gain_cores, gain_end)


def local(
    tokens,
    doc_ids,
    cotangent,
    attn_weights,
    mlp_weights,
    gains,
    moment_attn,
    moment_mlp,
    moment_gains,
    ema_attn,
    ema_mlp,
    ema_gains,
):
    row_count, width = tokens.shape
    shard_rows = attn_weights.shape[0]
    group = width // shard_rows
    pairs = width // LANES
    hidden = mlp_weights.shape[1] // 3
    half_width = width // 2
    thirds = pairs // 2
    mlp_chunks = hidden // (2 * LANES)
    chunks = thirds + 1 + mlp_chunks

    def pack(attn, mlp):
        qkv = attn[:, : 3 * width].reshape(shard_rows, 3, pairs, LANES).transpose(2, 0, 1, 3)
        out = attn[:, 3 * width :].reshape(shard_rows, 2, half_width).transpose(1, 0, 2)
        ffn = mlp.reshape(shard_rows, 3, 2 * mlp_chunks, LANES).transpose(2, 0, 1, 3)
        return jnp.concatenate(
            [
                qkv.reshape(pairs, shard_rows, half_width),
                out,
                ffn.reshape(2 * mlp_chunks, shard_rows, half_width),
            ],
            axis=0,
        ).reshape(chunks, 2, shard_rows, half_width)

    cos_table, sin_table = rotary_tables(row_count)
    vmem = pl.BlockSpec(memory_space=pltpu.VMEM)
    hbm = pl.BlockSpec(memory_space=pl.ANY)
    smem = pl.BlockSpec(memory_space=pltpu.SMEM)
    linked = shard_rows % 16 == 0 and group % 4 == 0
    planes = group // 4
    inputs = [("doc", smem, doc_ids), ("x_in", hbm, tokens), ("cot_in", hbm, cotangent)]
    inputs += [("cos", vmem, cos_table), ("sin", vmem, sin_table)]
    token_rows = (row_count, width)
    outputs = [
        ("block_out", hbm, jax.ShapeDtypeStruct(token_rows, bf16)),
        ("input_grad", hbm, jax.ShapeDtypeStruct(token_rows, bf16)),
    ]
    by_pair = (pairs, LANES, row_count)
    scratch = [
        ("x", pltpu.VMEM(token_rows, bf16)),
        ("cot", pltpu.VMEM(token_rows, bf16)),
        ("y", pltpu.VMEM(token_rows, f32)),
        ("total", pltpu.VMEM(token_rows, f32)),
        ("dn", pltpu.VMEM(token_rows, f32)),
        ("n1t", pltpu.VMEM((width, row_count), bf16)),
        ("qt", pltpu.VMEM(by_pair, bf16)),
        ("kt", pltpu.VMEM(by_pair, bf16)),
        ("vt", pltpu.VMEM(by_pair, bf16)),
        ("k", pltpu.VMEM((pairs, row_count, LANES), bf16)),
        ("v", pltpu.VMEM((pairs, row_count, LANES), bf16)),
        ("mixt", pltpu.VMEM(by_pair, bf16)),
        ("n2", pltpu.VMEM(token_rows, bf16)),
        ("n2t", pltpu.VMEM(by_pair, bf16)),
        ("cott", pltpu.VMEM((width, row_count), bf16)),
        ("hid", pltpu.VMEM((row_count, 2 * LANES), bf16)),
        ("dgu", pltpu.VMEM((row_count, 4 * LANES), bf16)),
        ("lse", pltpu.VMEM((pairs, 8, row_count), f32)),
        ("cost", pltpu.VMEM((HEAD // 2, row_count), f32)),
        ("sint", pltpu.VMEM((HEAD // 2, row_count), f32)),
        ("acc", pltpu.VMEM((3, LANES, row_count), f32)),
        ("local_sem", pltpu.SemaphoreType.DMA((2,))),
    ]
    if linked:
        lines = (planes, shard_rows, half_width)
        pair_lines = (planes, 2, shard_rows, half_width)
        whole = (planes, 4, shard_rows, half_width)
        gain_rows = (8, width)
        steps = mlp_chunks + 2 * thirds + 1
        inputs += [
            ("attn_in", hbm, attn_weights),
            ("mlp_in", hbm, mlp_weights),
            ("gains_in", vmem, gains),
        ]
        outputs += [
            ("g_out", vmem, jax.ShapeDtypeStruct((chunks, 2, shard_rows, half_width), f32)),
            ("gain_out", vmem, jax.ShapeDtypeStruct((8, LANES), f32)),
        ]
        scratch += [
            ("w", pltpu.VMEM((chunks, 2) + whole, bf16)),
            ("g", pltpu.VMEM((2, 2) + whole, bf16)),
            ("a", pltpu.VMEM((4,) + whole, bf16)),
            ("bs", pltpu.VMEM(pair_lines, bf16)),
            ("b", pltpu.VMEM((2,) + pair_lines, bf16)),
            ("h", pltpu.VMEM(pair_lines, bf16)),
            ("cs", pltpu.VMEM(lines, bf16)),
            ("c", pltpu.VMEM((2,) + lines, bf16)),
            ("kept", pltpu.VMEM(lines, f32)),
            ("ds", pltpu.VMEM(lines, bf16)),
            ("d", pltpu.VMEM((2, planes - 1) + lines[1:], bf16)),
            ("own", pltpu.VMEM(lines[1:], f32)),
            ("gout", pltpu.VMEM((chunks, 2) + lines[1:], f32)),
            ("gt", pltpu.VMEM((planes, 4, 16, LANES), bf16)),
            ("gain", pltpu.VMEM(gain_rows, f32)),
            ("gp", pltpu.VMEM((4,) + gain_rows, f32)),
            ("gz", pltpu.VMEM((planes,) + gain_rows, f32)),
            ("gc", pltpu.VMEM((2,) + gain_rows, f32)),
            ("load_sem", pltpu.SemaphoreType.DMA((4 + 3 * hidden // width,))),
            ("z_sem", pltpu.SemaphoreType.DMA((2, chunks, planes - 1))),
            ("line_sem", pltpu.SemaphoreType.DMA((2, chunks, 7))),
            ("gain_sem", pltpu.SemaphoreType.DMA((2, planes + 2))),
            ("rs_sem", pltpu.SemaphoreType.DMA((2, steps, planes + 3))),
            ("gsum_sem", pltpu.SemaphoreType.DMA((2, planes + 3))),
        ]
        params = pltpu.CompilerParams(
            collective_id=0, has_side_effects=True, vmem_limit_bytes=63 * 2**20
        )
    else:
        packed = pack(attn_weights.astype(bf16), mlp_weights.astype(bf16))
        full = lax.all_gather(packed, "fsdp", axis=2, tiled=True)
        gain_full = lax.all_gather(gains.astype(bf16), "fsdp", axis=1, tiled=True).astype(f32)
        inputs += [("w", vmem, full), ("gain", vmem, gain_full)]
        outputs += [
            ("g_out", hbm, jax.ShapeDtypeStruct((chunks, 2, width, half_width), bf16)),
            ("gain_out", vmem, jax.ShapeDtypeStruct((8, width), f32)),
        ]
        scratch += [
            ("g", pltpu.VMEM((2, 2, width, half_width), bf16)),
            ("g_sem", pltpu.SemaphoreType.DMA((2,))),
        ]
        params = pltpu.CompilerParams(vmem_limit_bytes=63 * 2**20)
    names = [entry[0] for entry in inputs + outputs + scratch]
    block_out, input_grad, part, gain_part = pl.pallas_call(
        functools.partial(block_kernel, linked, names),
        out_shape=[entry[2] for entry in outputs],
        in_specs=[entry[1] for entry in inputs],
        out_specs=[entry[1] for entry in outputs],
        scratch_shapes=[entry[1] for entry in scratch],
        compiler_params=params,
        name="block",
    )(*[entry[2] for entry in inputs])

    if linked:
        grad_gains = gain_part[:2, :shard_rows]
    else:
        part = lax.psum_scatter(part, "fsdp", scatter_dimension=2, tiled=True)
        part = lax.psum(part.astype(bf16), "rep").astype(f32)
        part = jnp.concatenate([part[mlp_chunks + 1 :], part[mlp_chunks:][:1], part[:mlp_chunks]])
        grad_gains = lax.psum_scatter(gain_part[:2], "fsdp", scatter_dimension=1, tiled=True)
        grad_gains = lax.psum(grad_gains, "rep")
    part = part.reshape(2 * chunks, shard_rows, half_width)
    qkv = part[:pairs].reshape(pairs, shard_rows, 3, LANES).transpose(1, 2, 0, 3)
    out = part[pairs : pairs + 2].transpose(1, 0, 2)
    ffn = part[pairs + 2 :].reshape(2 * mlp_chunks, shard_rows, 3, LANES).transpose(1, 2, 0, 3)
    grad_attn = jnp.concatenate(
        [qkv.reshape(shard_rows, 3 * width), out.reshape(shard_rows, width)], axis=1
    )
    grad_mlp = ffn.reshape(shard_rows, 3 * hidden)
    total_tokens = row_count * lax.axis_size("fsdp") * lax.axis_size("rep")
    rate = PEAK_RATE * STEP / (WARMUP * math.sqrt(total_tokens))

    def update(weight, grad, moment, average):
        velocity = MOMENTUM * moment + grad
        weight_new = weight - rate * (grad + MOMENTUM * velocity)
        average_new = DECAY * average + (1.0 - DECAY) * weight_new
        return (weight_new, velocity, average_new, weight_new.astype(bf16))

    kinds = [
        update(attn_weights, grad_attn, moment_attn, ema_attn),
        update(mlp_weights, grad_mlp, moment_mlp, ema_mlp),
        update(gains, grad_gains, moment_gains, ema_gains),
    ]
    return (block_out, input_grad, grad_attn, grad_mlp, grad_gains) + tuple(
        kind[what] for what in range(4) for kind in kinds
    )


def solution(mesh):
    rows = P(("fsdp", "rep"), None)
    shard = P("fsdp", None)
    columns = P(None, "fsdp")
    kinds = (shard, shard, columns)
    return jax.shard_map(
        local,
        mesh=mesh,
        in_specs=(rows, P(("fsdp", "rep")), rows) + kinds * 3,
        out_specs=(rows, rows) + kinds * 5,
        check_vma=False,
    )
```

```python
import functools
import math

import jax
import jax.numpy as jnp
import numpy as np
from jax import lax
from jax.experimental import pallas as pl
from jax.experimental.pallas import tpu as pltpu
from jax.sharding import PartitionSpec as P

HEAD = 64
VMEM_BYTES = 67_000_000
STEP = 5
WARMUP = 10
EPSILON = 1e-05
MASKED = -1e30
MOMENTUM = 0.5
DECAY = 0.5
PEAK_RATE = 0.1
LANES = 128
BLOCK = 256
PLAN = {
    ("fwd", 0): [
        ("R", (0, -1, -1, -1, -1, -1)),
        ("S", (-1, -1, 2, -1, 4, -1)),
        ("F", (1, -1, 4, -1, 6, -1)),
        ("T", (-1, -1, 1, -1, -1, 3)),
        ("S", (-1, -1, 3, -1, -1, -1)),
        ("F", (2, -1, 5, -1, -1, -1)),
        ("R", (-1, -1, 1, -1, 2, -1)),
    ],
    ("fwd", 1): [
        ("S", (-1, 1, -1, -1, -1, 5)),
        ("F", (-1, 3, -1, -1, -1, 7)),
        ("T", (-1, -1, -1, 2, -1, -1)),
    ],
    ("wo", 0): [
        ("R", (3,)),
    ],
    ("wo", 1): [
        ("T", (4,)),
    ],
    ("mlp", 0): [
        ("Q", (-1, -1, -1, -1, -1, -1, 0, 1)),
        ("H", (-1, -1, 0, 1, 2, 3, 4, 5)),
        ("S", (6, 7, 8, 9, 10, -1, -1, -1)),
        ("F", (8, 9, -1, -1, -1, -1, -1, -1)),
        ("B", (-1, -1, -1, -1, -1, 0, 2, 3)),
        ("B", (-1, -1, -1, -1, -1, 1, -1, -1)),
        ("T", (-1, -1, -1, -1, -1, -1, -1, 11)),
        ("L", (-1, -1, -1, -1, -1, -1, -1, 0)),
        ("R", (4, 5, 6, 7, 8, 9, 10, 11)),
        ("A", (-1, 0, 1, 2, 3, 4, 5, 6)),
        ("F", (-1, -1, 10, 11, -1, -1, -1, -1)),
        ("S", (-1, -1, -1, -1, -1, 11, -1, -1)),
    ],
    ("mlp", 1): [
        ("T", (5, 6, 7, 8, 9, 10, -1, -1)),
        ("Q", (-1, -1, -1, -1, -1, -1, -1, 2)),
        ("B", (-1, -1, -1, -1, -1, -1, -1, 4)),
    ],
    ("d", 0): [
        ("E", (0,)),
        ("L", (1,)),
        ("H", (6,)),
        ("A", (7,)),
    ],
    ("o", 0): [
        ("X", (0,)),
        ("Q", (3,)),
        ("B", (5,)),
    ],
    ("o", 1): [
        ("L", (2,)),
        ("H", (7,)),
        ("A", (8,)),
    ],
    ("bwd", 0): [
        ("E", (1, -1, -1, -1, -1, -1)),
        ("X", (-1, -1, -1, 4, -1, 6)),
    ],
    ("bwd", 1): [
        ("X", (1, 2, 3, -1, 5, 7)),
        ("E", (-1, 3, 4, 5, 6, -1)),
        ("L", (3, 4, 5, -1, -1, 9)),
        ("Q", (4, -1, -1, 8, 9, -1)),
        ("H", (8, -1, 9, -1, 10, -1)),
        ("B", (6, -1, -1, -1, 10, -1)),
    ],
    ("bwd", 2): [
        ("E", (2, -1, -1, -1, 7, -1)),
        ("L", (-1, -1, 6, 7, 8, -1)),
        ("Q", (5, 6, 7, -1, -1, 10)),
        ("A", (-1, 9, -1, 10, -1, 11)),
        ("B", (7, 8, 9, -1, -1, -1)),
    ],
    ("tail", 0): [
        ("E", (8,)),
    ],
    ("tail", 1): [
    ],
    ("tail", 2): [
        ("X", (8,)),
        ("L", (10,)),
        ("H", (11,)),
        ("B", (11,)),
    ],
    ("tail", 3): [
        ("E", (9,)),
    ],
    ("end", 0): [
        ("X", (9,)),
        ("E", (10,)),
        ("Q", (11,)),
        ("X", (10,)),
        ("L", (11,)),
        ("E", (11,)),
        ("X", (11,)),
    ],
}
HELD = 4

f32 = jnp.float32
bf16 = jnp.bfloat16


def nn(left, right):
    return jnp.dot(left, right, preferred_element_type=f32)


def nt(left, right):
    return lax.dot_general(
        left, right, (((1,), (1,)), ((), ())), preferred_element_type=f32
    )


def in_turn(items, stages):
    values = {}
    for turn in range(len(items) + len(stages) - 1):
        for number, stage in enumerate(stages):
            index = turn - number
            if 0 <= index < len(items):
                values[index] = stage(items[index], *values.get(index, ()))


def rotary_tables(row_count):
    half = HEAD // 2
    frequency = np.float32(10000.0) ** (-np.arange(half, dtype=np.float32) / np.float32(half))
    angles = np.arange(row_count, dtype=np.float32)[None, :] * frequency.astype(np.float32)[:, None]
    angles = angles.astype(np.float64)
    tables = np.stack([np.cos(angles), np.sin(angles)]).astype(np.float32)
    tables = tables.reshape(2, half, row_count // BLOCK, BLOCK).transpose(0, 2, 1, 3)
    return np.ascontiguousarray(tables.reshape(-1, BLOCK))


def rotate_rows(rows, cosine, sine):
    half = HEAD // 2
    first, second = rows[:half], rows[half:]
    return jnp.concatenate(
        [first * cosine - second * sine, second * cosine + first * sine], axis=0
    )


def rms_scale(rows):
    return lax.rsqrt(jnp.mean(rows * rows, axis=-1, keepdims=True) + EPSILON)


class Scratch:
    def __init__(self, names, refs):
        for name, ref in zip(names, refs, strict=True):
            setattr(self, name, ref)


def block_kernel(linked, names, *refs):
    s = Scratch(names, refs)
    row_count, width = s.x.shape
    blocks = row_count // BLOCK
    pairs = width // LANES
    thirds = pairs // 2
    half_width = width // 2
    chunks = s.w.shape[0]
    mlp_chunks = chunks - thirds - 1
    slots = s.g.shape[0]

    def rows_of(i):
        return pl.ds(i * BLOCK, BLOCK)

    def store_pairs(i, value):
        for p in range(pairs):
            s.n2[p, rows_of(i), :] = value[:, p * LANES : (p + 1) * LANES]

    def load_pairs(i):
        return jnp.concatenate([s.n2[p, rows_of(i), :] for p in range(pairs)], axis=1)

    def sums_at(kind, first, count, j):
        return (pl.ds(j * LANES + first, count), pl.ds(kind * BLOCK, BLOCK))

    def load_w(chunk, half):
        return s.w[chunk, half].reshape(width, half_width)

    def store_g(chunk, half, lanes, value):
        low = value.astype(bf16)
        if linked:
            low = low.reshape(s.g.shape[2:5] + (low.shape[1],))
            s.g[chunk % slots, half, :, :, :, lanes] = low
        else:
            s.g[chunk % slots, half, :, lanes] = low

    if linked:
        gather_start, actions, gain_steps = links(s, chunks, thirds, mlp_chunks)
    else:


        def grad_copy(chunk):
            slot = chunk % slots
            return pltpu.make_async_copy(s.g.at[slot], s.g_out.at[chunk], s.g_sem.at[slot])

        actions = {"A": lambda chunk: grad_copy(chunk).start()}
        actions["H"] = lambda chunk: grad_copy(chunk).wait()

    def events(loop, place, index=0):
        for kind, table in PLAN[loop, place]:
            if kind not in actions:
                continue
            if isinstance(index, int):
                if table[index] >= 0:
                    actions[kind](table[index])
                continue
            used = [i for i, entry in enumerate(table) if entry >= 0]
            shift = table[used[0]] - used[0]
            in_line = all(table[i] == i + shift for i in used)
            in_line = in_line and used == list(range(used[0], used[-1] + 1))
            if in_line:
                chunk = index + shift
            else:
                chunk = jnp.int32(table[used[0]])
                for i in used[1:]:
                    chunk = jnp.where(index == i, table[i], chunk)
            if len(used) == len(table):
                actions[kind](chunk)
                continue
            if in_line:
                now = (index >= used[0]) & (index <= used[-1])
            else:
                now = functools.reduce(lambda u, v: u | v, [index == i for i in used])
            pl.when(now)(functools.partial(actions[kind], chunk))

    copies = [
        pltpu.make_async_copy(s.x_in, s.x, s.local_sem.at[0]),
        pltpu.make_async_copy(s.cot_in, s.cot, s.local_sem.at[1]),
    ]
    tables = s.total.at[pl.ds(0, HEAD * blocks), pl.ds(0, BLOCK)]
    copies.append(pltpu.make_async_copy(s.tables, tables, s.local_sem.at[2]))
    for copy in copies:
        copy.start()

    docs = [s.doc[BLOCK * j] for j in range(blocks)]
    bias = [
        [jnp.where(docs[i] == docs[j], 0.0, MASKED).astype(f32) for j in range(i)] + [0.0]
        for i in range(blocks)
    ]
    causal = lax.broadcasted_iota(jnp.int32, (BLOCK, BLOCK), 0) <= lax.broadcasted_iota(
        jnp.int32, (BLOCK, BLOCK), 1
    )

    if linked:
        gather_start[0]()
    copies.pop().wait()
    for i in range(blocks):
        place = sum([(docs[j] == docs[i]).astype(jnp.int32) for j in range(i)], jnp.int32(0))
        for index, table in enumerate([s.cost, s.sint]):
            chosen = None
            for t in range(i + 1):
                first = (index * blocks + t) * (HEAD // 2)
                part = s.total[pl.ds(first, HEAD // 2), pl.ds(0, BLOCK)]
                chosen = part if t == 0 else jnp.where(place == t, part, chosen)
            table[:, rows_of(i)] = chosen
    if linked:
        gather_start[1]()
    for copy in copies:
        copy.wait()
    if linked:
        gather_start[2]()
    if linked:
        gather_start[3]()
    gain_one = s.gain[0:1, :]
    gain_two = s.gain[1:2, :]
    for i in range(blocks):
        stream = s.x[rows_of(i), :].astype(f32)
        normed = (stream * rms_scale(stream) * gain_one).astype(bf16)
        s.n1t[:, rows_of(i)] = normed.T
        s.dn[rows_of(i), :] = jnp.zeros((BLOCK, width), f32)

    def masked_pair(rows, h):
        zero = jnp.zeros((HEAD, BLOCK), bf16)
        parts = [rows[:HEAD], zero] if h == 0 else [zero, rows[HEAD:]]
        return jnp.concatenate(parts, axis=0)

    def scores_of(p, i, h):
        span = (i + 1) * BLOCK
        query = masked_pair(s.qt[p, :, rows_of(i)], h)
        scores = nn(s.k[p, pl.ds(0, span), :], query)
        parts = [scores[j * BLOCK : (j + 1) * BLOCK] for j in range(i + 1)]
        parts[i] = jnp.where(causal, parts[i], MASKED)
        return parts

    bodies = [(i, h) for i in range(blocks) for h in range(2)]

    def attention_forward(p, carry):
        events("fwd", 0, p)
        weights_t = load_w(p // 2, p % 2).T
        for i in range(blocks):
            cosine, sine = s.cost[:, rows_of(i)], s.sint[:, rows_of(i)]
            projected = nn(weights_t, s.n1t[:, rows_of(i)])
            for h in range(2):
                lo, hi = h * HEAD, (h + 1) * HEAD
                query = rotate_rows(projected[lo:hi], cosine, sine).astype(bf16)
                s.qt[p, lo:hi, rows_of(i)] = query * bf16(0.125)
                key = rotate_rows(projected[LANES + lo : LANES + hi], cosine, sine)
                s.kt[p, lo:hi, rows_of(i)] = key.astype(bf16)
            s.vt[p, :, rows_of(i)] = projected[2 * LANES :].astype(bf16)
            s.k[p, rows_of(i), :] = s.kt[p, :, rows_of(i)].T
            s.v[p, rows_of(i), :] = s.vt[p, :, rows_of(i)].T
        events("fwd", 1, p)

        def shares(n, parts):
            i, h = n
            tops = [
                jnp.max(part, axis=0, keepdims=True) + bias[i][j]
                for j, part in enumerate(parts)
            ]
            top = functools.reduce(jnp.maximum, tops)
            exps = [jnp.exp(part - (top - bias[i][j])) for j, part in enumerate(parts)]
            total = sum([jnp.sum(e, axis=0, keepdims=True) for e in exps])
            s.lse[p // 2, pl.ds(2 * (p % 2) + h, 1), rows_of(i)] = top + jnp.log(total)
            return jnp.concatenate([e.astype(bf16) for e in exps], axis=0), 1.0 / total

        def mix(n, exps_low, inverse):
            i, h = n
            heads = pl.ds(h * HEAD, HEAD)
            mixed = nn(s.vt[p, heads, pl.ds(0, (i + 1) * BLOCK)], exps_low)
            s.mixt[p, heads, rows_of(i)] = (mixed * inverse).astype(bf16)

        in_turn(bodies, [lambda n: (scores_of(p, *n),), shares, mix])
        return carry

    lax.fori_loop(0, pairs, attention_forward, 0)

    out_chunk = thirds
    for i in range(blocks):
        if i % 2 == 0:
            events("wo", i // 2)
        mixed = s.mixt[:, :, rows_of(i)].reshape(width, BLOCK).T
        branch = jnp.concatenate(
            [nn(mixed, load_w(out_chunk, half)) for half in range(2)], axis=1
        )
        after = s.x[rows_of(i), :].astype(f32) + branch
        s.y[rows_of(i), :] = after
        s.total[rows_of(i), :] = after
        normed = (after * rms_scale(after) * gain_two).astype(bf16)
        store_pairs(i, normed)
        s.n2t[:, :, rows_of(i)] = normed.T.reshape(pairs, LANES, BLOCK)

    tiles = [pl.ds(t * BLOCK, BLOCK) for t in range(width // BLOCK)]
    for i in range(blocks):
        for tile in tiles:
            s.x[rows_of(i), tile] = s.cot[rows_of(i), tile].T

    def feed_forward(chunk, carry):
        events("mlp", 0, chunk)
        low = [load_w(thirds + 1 + chunk, half) for half in range(2)]
        w_gu = [w[:, : 2 * LANES] for w in low]
        w_gu_all = jnp.concatenate(w_gu, axis=1)
        w_down = jnp.concatenate([w[:, 2 * LANES :] for w in low], axis=1)

        def products(i):
            normed = load_pairs(i)
            d_hidden = nn(s.cot[rows_of(i), :], w_down)
            return d_hidden, [nn(normed, w) for w in w_gu]

        def slopes(i, d_hidden, gate_ups):
            for half, gate_up in enumerate(gate_ups):
                gate, up = gate_up[:, :LANES], gate_up[:, LANES:]
                back = d_hidden[:, half * LANES : (half + 1) * LANES]
                sig = jax.nn.sigmoid(gate)
                silu = gate * sig
                s.hid[rows_of(i), pl.ds(half * LANES, LANES)] = (silu * up).astype(bf16)
                s.dgu[rows_of(i), pl.ds(2 * half * LANES, LANES)] = (
                    back * up * (sig + silu * (1.0 - sig))
                ).astype(bf16)
                s.dgu[rows_of(i), pl.ds((2 * half + 1) * LANES, LANES)] = (
                    back * silu
                ).astype(bf16)
            return ()

        def sums(i):
            s.total[rows_of(i), :] += nt(s.hid[rows_of(i), :], w_down)
            s.dn[rows_of(i), :] += nt(s.dgu[rows_of(i), :], w_gu_all)

        in_turn(list(range(blocks)), [products, slopes, sums])
        events("mlp", 1, chunk)
        n2t = s.n2t[...].reshape(width, row_count)
        for half in range(2):
            store_g(
                chunk,
                half,
                pl.ds(0, 2 * LANES),
                nn(n2t, s.dgu[:, pl.ds(2 * half * LANES, 2 * LANES)]),
            )
        grad_down = jnp.concatenate(
            [
                nn(
                    jnp.concatenate([s.x[rows_of(i), tile] for i in range(blocks)], axis=1),
                    s.hid[...],
                )
                for tile in tiles
            ],
            axis=0,
        )
        for half in range(2):
            store_g(
                chunk,
                half,
                pl.ds(2 * LANES, LANES),
                grad_down[:, half * LANES : (half + 1) * LANES],
            )
        return carry

    lax.fori_loop(0, mlp_chunks, feed_forward, 0)

    events("d", 0)
    x_copy = pltpu.make_async_copy(s.x_in, s.x, s.local_sem.at[1])
    x_copy.start()

    gain_grad_two = jnp.zeros((1, width), f32)
    for i in range(blocks):
        after = s.y[rows_of(i), :]
        scale = rms_scale(after)
        unit = after * scale
        d_normed = s.dn[rows_of(i), :]
        d_unit = d_normed * gain_two
        gain_grad_two += jnp.sum(d_normed * unit, axis=0, keepdims=True)
        grad_after = s.cot[rows_of(i), :].astype(f32) + scale * (
            d_unit - unit * jnp.mean(d_unit * unit, axis=-1, keepdims=True)
        )
        s.y[rows_of(i), :] = grad_after
        store_pairs(i, grad_after.astype(bf16))
        s.cot[rows_of(i), :] = s.total[rows_of(i), :].astype(bf16)
    out_copy = pltpu.make_async_copy(s.cot, s.block_out, s.local_sem.at[0])
    out_copy.start()

    events("o", 0)
    mixt = s.mixt[...].reshape(width, row_count)
    for half in range(2):
        store_g(
            mlp_chunks,
            half,
            pl.ds(0, half_width),
            nn(mixt, jnp.concatenate([s.n2[p] for p in range(half * thirds, (half + 1) * thirds)], axis=1)),
        )
    events("o", 1)
    dmt = s.n2t
    w_out = jnp.concatenate([load_w(out_chunk, half) for half in range(2)], axis=1)
    for i in range(blocks):
        d_mixed = nt(w_out, load_pairs(i))
        dmt[:, :, rows_of(i)] = d_mixed.astype(bf16).reshape(pairs, LANES, BLOCK)

    def attention_backward(p, carry):
        events("bwd", 0, p)
        for j in range(blocks):
            for kind in (1, 2):
                s.total[sums_at(kind, 0, LANES, j)] = jnp.zeros((LANES, BLOCK), f32)
        def begin(n):
            i, h = n
            back = masked_pair(dmt[p, :, rows_of(i)], h)
            return scores_of(p, i, h), nn(s.v[p, pl.ds(0, (i + 1) * BLOCK), :], back)

        def middle(n, parts, d_probs):
            i, h = n
            lse = s.lse[p // 2, pl.ds(2 * (p % 2) + h, 1), rows_of(i)]
            probs = [jnp.exp(part - (lse - bias[i][j])) for j, part in enumerate(parts)]
            probs = jnp.concatenate(probs, axis=0)
            weighted = probs * d_probs
            inner = jnp.sum(weighted, axis=0, keepdims=True)
            return (weighted - probs * inner).astype(bf16), probs.astype(bf16)

        def finish(n, d_scores, probs_low):
            i, h = n
            heads, keys = pl.ds(h * HEAD, HEAD), pl.ds(0, (i + 1) * BLOCK)
            s.total[sums_at(0, h * HEAD, HEAD, i)] = nn(s.kt[p, heads, keys], d_scores)
            d_keys = nt(s.qt[p, heads, rows_of(i)], d_scores)
            d_values = nt(dmt[p, heads, rows_of(i)], probs_low)
            for j in range(i + 1):
                span = slice(j * BLOCK, (j + 1) * BLOCK)
                s.total[sums_at(1, h * HEAD, HEAD, j)] += d_keys[:, span]
                s.total[sums_at(2, h * HEAD, HEAD, j)] += d_values[:, span]

        in_turn(bodies, [begin, middle, finish])
        events("bwd", 1, p)
        for i in range(blocks):
            cosine, sine = s.cost[:, rows_of(i)], -s.sint[:, rows_of(i)]
            pieces = []
            for kind in range(2):
                for h in range(2):
                    piece = s.total[sums_at(kind, h * HEAD, HEAD, i)]
                    piece = rotate_rows(piece, cosine, sine)
                    pieces.append((piece * 0.125 if kind == 0 else piece).astype(bf16))
            s.k[p, rows_of(i), :] = jnp.concatenate(pieces[:2], axis=0).T
            s.v[p, rows_of(i), :] = jnp.concatenate(pieces[2:], axis=0).T
            s.n2[p, rows_of(i), :] = s.total[sums_at(2, 0, LANES, i)].astype(bf16).T
        d_qkv = jnp.concatenate([s.k[p], s.v[p], s.n2[p]], axis=1)
        store_g(
            mlp_chunks + 1 + p // 2, p % 2, pl.ds(0, half_width), nn(s.n1t[...], d_qkv)
        )
        events("bwd", 2, p)
        return carry

    lax.fori_loop(0, pairs, attention_backward, 0)

    x_copy.wait()
    w_qkv_t = jnp.concatenate([load_w(p // 2, p % 2).T for p in range(pairs)], axis=0)
    gain_grad_one = jnp.zeros((1, width), f32)
    for i in range(blocks):
        events("tail", i)
        d_qkv = [
            ref[p, rows_of(i), :] for p in range(pairs) for ref in (s.k, s.v, s.n2)
        ]
        d_normed = nn(jnp.concatenate(d_qkv, axis=1), w_qkv_t)
        stream = s.x[rows_of(i), :].astype(f32)
        scale = rms_scale(stream)
        unit = stream * scale
        d_unit = d_normed * gain_one
        gain_grad_one += jnp.sum(d_normed * unit, axis=0, keepdims=True)
        s.x[rows_of(i), :] = (
            s.y[rows_of(i), :]
            + scale * (d_unit - unit * jnp.mean(d_unit * unit, axis=-1, keepdims=True))
        ).astype(bf16)
    grad_copy_out = pltpu.make_async_copy(s.x, s.input_grad, s.local_sem.at[1])
    grad_copy_out.start()
    gain_grads = jnp.concatenate(
        [gain_grad_one, gain_grad_two, jnp.zeros((6, width), f32)], axis=0
    )
    if linked:
        gain_steps[0](gain_grads)
        for kind, table in PLAN["end", 0]:
            actions[kind](table[0])
            if table[0] == chunks - 1 and kind in "LEX":
                gain_steps["LEX".index(kind) + 1]()
        gain_steps[4]()
    else:
        events("end", 0)
        s.gain_out[...] = gain_grads
    out_copy.wait()
    grad_copy_out.wait()


def links(s, chunks, thirds, mlp_chunks):
    planes = s.w.shape[2]
    me = lax.axis_index("fsdp")
    core = lax.axis_index("rep")
    z, m = me // 4, me % 4
    over_x, over_y, over_both = m + 1 - 2 * (m % 2), (m + 2) % 4, 3 - m
    m1 = (1 - core) * over_x + core * over_y
    m2 = (1 - core) * over_y + core * over_x
    m3 = over_both
    other = 1 - core

    def chip(plane, place):
        return (plane * 4 + place, core)

    sibling = (me, other)

    def far(k):
        return (z + k) % planes

    peers = [chip(far(k), m) for k in range(1, planes)]

    def remote(src, dst, sems, index, device):
        return pltpu.make_async_remote_copy(
            src_ref=src,
            dst_ref=dst,
            send_sem=sems.at[(0,) + index],
            recv_sem=sems.at[(1,) + index],
            device_id=device,
            device_id_type=pl.DeviceIdType.MESH,
        )

    def along_z(chunk, k):
        block = s.w.at[chunk, core, z, m]
        return remote(block, block, s.z_sem, (chunk, k), peers[k])

    def line(chunk, place, index, device):
        block = s.w.at[chunk, core, :, place]
        return remote(block, block, s.line_sem, (chunk, index), device)

    hops = [
        (m, chip(z, m1)),
        (m, chip(z, m2)),
        (m1, chip(z, m2)),
        (m, sibling),
        (m1, sibling),
        (m2, sibling),
        (m3, sibling),
    ]

    def hop(chunk, index):
        return line(chunk, hops[index][0], index, hops[index][1])

    def gain_along_z(k):
        block = s.gt.at[z, m]
        return remote(block, block, s.gain_sem, (k,), peers[k])

    def gain_line(place, index, device):
        block = s.gt.at[:, place]
        return remote(block, block, s.gain_sem, (planes - 1 + index,), device)

    def gain_hop(index):
        return gain_line(hops[index][0], index, hops[index][1])

    width = s.x.shape[1]
    pairs = width // LANES
    shard_rows = s.w.shape[4]
    half_width = s.w.shape[5]
    hidden = s.mlp_in.shape[1] // 3

    def gather_start():
        loads = [
            pltpu.make_async_copy(
                s.attn_in.at[:, pl.ds(k * width, width)],
                s.dn.at[pl.ds(k * shard_rows, shard_rows)],
                s.load_sem.at[k],
            )
            for k in range(4)
        ] + [
            pltpu.make_async_copy(
                s.mlp_in.at[:, pl.ds(k * width, width)],
                s.dn.at[pl.ds((4 + k) * shard_rows, shard_rows)],
                s.load_sem.at[4 + k],
            )
            for k in range(3 * hidden // width)
        ]
        for load in loads:
            load.start()
        barrier = pltpu.get_barrier_semaphore()
        partners = [chip(z, over_x), chip(z, over_y), chip(z, over_both), sibling] + peers
        for partner in partners:
            pl.semaphore_signal(
                barrier, inc=1, device_id=partner, device_id_type=pl.DeviceIdType.MESH
            )
        own = s.gains_in[...].astype(bf16)
        own = jnp.concatenate([own, jnp.zeros((2, LANES - shard_rows), bf16)], axis=1)
        s.gt[z, m] = jnp.concatenate([own, jnp.zeros((14, LANES), bf16)], axis=0)
        for load in loads:
            load.wait()
        for third in range(thirds):
            lane = pl.multiple_of((2 * third + core) * LANES, LANES)
            for kind in range(3):
                s.w[third, core, z, m, :, kind * LANES : (kind + 1) * LANES] = piece(kind, lane)
        lane = pl.multiple_of(core * half_width, LANES)
        s.w[thirds, core, z, m] = s.dn[
            pl.ds(3 * shard_rows, shard_rows), pl.ds(lane, half_width)
        ].astype(bf16)
        pl.semaphore_wait(barrier, len(partners))
        for k in range(planes - 1):
            along_z(0, k).start()
        for k in range(planes - 1):
            gain_along_z(k).start()
        for chunk in range(1, thirds + 1):
            for k in range(planes - 1):
                along_z(chunk, k).start()

    def piece(row, lane):
        rows = s.dn[pl.ds(row * shard_rows, shard_rows), pl.ds(lane, LANES)]
        return rows.astype(bf16)

    def gather_feed_forward():
        for j in range(mlp_chunks):
            for kind in range(3):
                place = kind * hidden + 2 * j * LANES
                row, first = 4 + place // width, place % width
                lane = pl.multiple_of(first + core * LANES, LANES)
                s.w[thirds + 1 + j, core, z, m, :, kind * LANES : (kind + 1) * LANES] = piece(
                    row, lane
                )
            for k in range(planes - 1):
                along_z(thirds + 1 + j, k).start()

    def gather_one():
        first_hop(0)
        for k in range(planes - 1):
            gain_along_z(k).wait()
        gain_hop(0).start()
        gain_hop(1).start()
        gather_feed_forward()

    def gather_two():
        second_hop(0)
        gain_hop(0).wait()
        gain_hop(2).start()

    def gather_three():
        third_hop(0)
        gain_hop(1).wait()
        gain_hop(2).wait()
        rows = jnp.zeros((8, width), f32)
        for d in range(planes * 4):
            tile = s.gt[d // 4, d % 4].astype(f32)[:8]
            wide = jnp.concatenate([tile, jnp.zeros((8, width - LANES), f32)], axis=1)
            rows += pltpu.roll(wide, d * shard_rows, 1) if d else wide
        s.gain[...] = rows

    def ready(chunk):
        for index in range(3, 7):
            hop(chunk, index).wait_recv()
        for k in range(planes - 1):
            along_z(chunk, k).wait_send()
        for index in range(7):
            hop(chunk, index).wait_send()

    def third_hop(chunk):
        hop(chunk, 1).wait_recv()
        hop(chunk, 5).start()
        hop(chunk, 2).wait_recv()
        hop(chunk, 6).start()

    def second_hop(chunk):
        hop(chunk, 0).wait_recv()
        hop(chunk, 2).start()
        hop(chunk, 4).start()

    def first_hop(chunk):
        for k in range(planes - 1):
            along_z(chunk, k).wait_recv()
        for index in (0, 1, 3):
            hop(chunk, index).start()

    def to_sibling(chunk):
        return remote(
            s.g.at[chunk % 2, other], s.a.at[chunk % 2], s.rs_sem, (chunk, 0), sibling
        )

    def to_second(chunk):
        return remote(
            s.h.at[chunk % held, :, pl.ds(2, 2)],
            s.b.at[chunk % 4],
            s.rs_sem,
            (chunk, 1),
            chip(z, m2),
        )

    def to_first(chunk):
        return remote(s.cs.at[chunk % 2], s.c.at[chunk % 4], s.rs_sem, (chunk, 2), chip(z, m1))

    def to_plane(chunk, k):
        return remote(
            s.ds.at[chunk % 2, far(k + 1)],
            s.d.at[chunk % 4, k],
            s.rs_sem,
            (chunk, 3 + k),
            peers[k],
        )

    def place_of(chunk):
        return jnp.where(
            chunk < mlp_chunks,
            thirds + 1 + chunk,
            jnp.where(chunk == mlp_chunks, thirds, chunk - mlp_chunks - 1),
        )

    def half_block(chunk):
        return s.gout.at[chunk % 6, core]

    def to_copy(chunk):
        block = half_block(chunk)
        return remote(block, block, s.rs_sem, (chunk, 2 + planes), sibling)

    def leave(chunk):
        place = place_of(chunk)
        return pltpu.make_async_copy(s.gout.at[chunk % 6], s.g_out.at[place], s.leave_sem.at[chunk])

    held = s.h.shape[0]

    def send_half(chunk):
        to_sibling(chunk).start()

    def add_half(chunk):
        to_sibling(chunk).wait()
        for index, place in enumerate([m, m1, m2, m3]):
            s.h[chunk % held, :, index] = (
                s.g[chunk % 2, core, :, place].astype(f32)
                + s.a[chunk % 2, :, place].astype(f32)
            ).astype(bf16)

    def halves(chunk):
        to_second(chunk).start()

    def quarters(chunk):
        to_second(chunk).wait()
        even = chunk % 2
        s.cs[even] = (
            s.h[chunk % held, :, 1].astype(f32) + s.b[chunk % 4, :, 1].astype(f32)
        ).astype(bf16)
        to_first(chunk).start()
        s.kept[even] = s.h[chunk % held, :, 0].astype(f32) + s.b[chunk % 4, :, 0].astype(f32)

    def lines(chunk):
        to_first(chunk).wait()
        even = chunk % 2
        s.kept[even] = s.kept[even] + s.c[chunk % 4].astype(f32)
        s.ds[even] = s.kept[even].astype(bf16)
        s.own[even] = s.kept[even, z]
        for k in range(planes - 1):
            to_plane(chunk, k).start()

    def last(chunk):
        total = s.own[chunk % 2]
        for k in range(planes - 1):
            to_plane(chunk, k).wait()
            total += s.d[chunk % 4, k].astype(f32)
        half_block(chunk)[...] = total
        to_copy(chunk).start()

    def end(chunk):
        to_copy(chunk).wait()
        leave(chunk).start()
        if isinstance(chunk, int):
            if chunk >= 2:
                leave(chunk - 2).wait()
        else:
            pl.when(chunk >= 2)(lambda: leave(chunk - 2).wait())

    actions = {"F": first_hop, "S": second_hop, "T": third_hop, "R": ready}
    actions.update({"A": send_half, "H": add_half, "B": halves, "Q": quarters})
    actions.update({"L": lines, "E": last, "X": end})

    def plane_sum():
        block = s.gp.at[m]
        return [
            remote(block, block, s.gsum_sem, (k,), chip(z, place))
            for k, place in enumerate([over_x, over_y, over_both])
        ]

    def line_sum():
        block = s.gz.at[z]
        return [
            remote(block, block, s.gsum_sem, (3 + k,), peers[k]) for k in range(planes - 1)
        ]

    def core_sum():
        return remote(s.gc.at[0], s.gc.at[1], s.gsum_sem, (2 + planes,), sibling)

    def gain_begin(value):
        s.gp[m] = value
        for copy in plane_sum():
            copy.start()

    def gain_lines_sum():
        for copy in plane_sum():
            copy.wait()
        s.gz[z] = (s.gp[0] + s.gp[1]) + (s.gp[2] + s.gp[3])
        for copy in line_sum():
            copy.start()

    def gain_cores():
        for copy in line_sum():
            copy.wait()
        total = s.gz[0]
        for k in range(1, planes):
            total += s.gz[k]
        s.gc[0] = total
        core_sum().start()

    def gain_end():
        core_sum().wait()
        total = s.gc[0] + s.gc[1]
        s.gain_out[...] = pltpu.roll(total, (width - me * shard_rows) % width, 1)[:, :LANES]

    def gain_out():
        for chunk in range(chunks - 2, chunks):
            leave(chunk).wait()

    start = (gather_start, gather_one, gather_two, gather_three)
    return start, actions, (gain_begin, gain_lines_sum, gain_cores, gain_end, gain_out)


def update_kernel(rate, names, *refs):
    s = Scratch(names, refs)
    width = s.attn_w.shape[1] // 4
    hidden = s.mlp_w.shape[1] // 3
    pairs = width // LANES
    thirds = pairs // 2
    half_width = width // 2
    whats = ["grad", "next", "velocity", "average", "copy"]

    def rule(weight, grad, moment, average):
        velocity = MOMENTUM * moment + grad
        weight_new = weight - rate * (grad + MOMENTUM * velocity)
        average_new = DECAY * average + (1.0 - DECAY) * weight_new
        return grad, weight_new, velocity, average_new, weight_new.astype(bf16)

    attn_blocks = [
        (kind * width + pair * LANES, LANES, (pair // 2, pair % 2), kind * LANES)
        for kind in range(3)
        for pair in range(pairs)
    ] + [(3 * width + half * half_width, half_width, (thirds, half), 0) for half in range(2)]
    pieces = [("attn", 0, 4 * width, attn_blocks)] + [
        (
            "mlp",
            kind * hidden,
            hidden,
            [
                (kind * hidden + b * LANES, LANES, (thirds + 1 + b // 2, b % 2), kind * LANES)
                for b in range(hidden // LANES)
            ],
        )
        for kind in range(3)
    ]

    def loads(index):
        kind, first, count, _ = pieces[index]
        span = pl.ds(first, count)
        return [
            pltpu.make_async_copy(
                getattr(s, f"{kind}_{what}").at[:, span],
                getattr(s, f"{kind}_{what}_here").at[:, span],
                s.in_sem.at[index, k],
            )
            for k, what in enumerate(["w", "m", "e"])
        ]

    def stores(index):
        kind, first, count, _ = pieces[index]
        span = pl.ds(first, count)
        return [
            pltpu.make_async_copy(
                getattr(s, f"{kind}_{what}_here").at[:, span],
                getattr(s, f"{kind}_{what}").at[:, span],
                s.out_sem.at[index, k],
            )
            for k, what in enumerate(whats)
        ]

    enter = [
        pltpu.make_async_copy(s.out_in, s.pass_here.at[0], s.pass_sem.at[0]),
        pltpu.make_async_copy(s.grad_in, s.pass_here.at[1], s.pass_sem.at[1]),
    ]
    leave = [
        pltpu.make_async_copy(s.pass_here.at[0], s.block_out, s.pass_sem.at[4]),
        pltpu.make_async_copy(s.pass_here.at[1], s.input_grad, s.pass_sem.at[5]),
    ]
    grads = [
        pltpu.make_async_copy(
            s.g.at[pl.ds(0, thirds + 1)], s.g_here.at[pl.ds(0, thirds + 1)], s.pass_sem.at[2]
        ),
        pltpu.make_async_copy(
            s.g.at[pl.ds(thirds + 1, s.g.shape[0] - thirds - 1)],
            s.g_here.at[pl.ds(thirds + 1, s.g.shape[0] - thirds - 1)],
            s.pass_sem.at[3],
        ),
    ]
    grads[0].start()
    for load in loads(0):
        load.start()
    grads[1].start()
    for index in range(1, len(pieces)):
        for load in loads(index):
            load.start()
    for copy in enter:
        copy.start()
    shard_rows = s.attn_w.shape[0]
    results = rule(s.gains_w[...], s.gain_part[:2, :shard_rows], s.gains_m[...], s.gains_e[...])
    for what, result in zip(whats, results, strict=True):
        getattr(s, f"gains_{what}")[...] = result
    for index, (kind, _, _, blocks) in enumerate(pieces):
        if index < 2:
            grads[index].wait()
        for load in loads(index):
            load.wait()
        for first, count, chunk, lane in blocks:
            span = slice(first, first + count)
            results = rule(
                getattr(s, f"{kind}_w_here")[:, span],
                s.g_here[chunk[0], chunk[1], :, lane : lane + count],
                getattr(s, f"{kind}_m_here")[:, span],
                getattr(s, f"{kind}_e_here")[:, span],
            )
            for what, result in zip(whats, results, strict=True):
                getattr(s, f"{kind}_{what}_here")[:, span] = result
        for store in stores(index):
            store.start()
    for copy_in, copy_out in zip(enter, leave, strict=True):
        copy_in.wait()
        copy_out.start()
    for index in range(len(pieces)):
        for store in stores(index):
            store.wait()
    for copy in leave:
        copy.wait()


def local(
    tokens,
    doc_ids,
    cotangent,
    attn_weights,
    mlp_weights,
    gains,
    moment_attn,
    moment_mlp,
    moment_gains,
    ema_attn,
    ema_mlp,
    ema_gains,
):
    row_count, width = tokens.shape
    shard_rows = attn_weights.shape[0]
    group = width // shard_rows
    pairs = width // LANES
    hidden = mlp_weights.shape[1] // 3
    half_width = width // 2
    thirds = pairs // 2
    mlp_chunks = hidden // (2 * LANES)
    chunks = thirds + 1 + mlp_chunks

    def pack(attn, mlp):
        qkv = attn[:, : 3 * width].reshape(shard_rows, 3, pairs, LANES).transpose(2, 0, 1, 3)
        out = attn[:, 3 * width :].reshape(shard_rows, 2, half_width).transpose(1, 0, 2)
        ffn = mlp.reshape(shard_rows, 3, 2 * mlp_chunks, LANES).transpose(2, 0, 1, 3)
        return jnp.concatenate(
            [
                qkv.reshape(pairs, shard_rows, half_width),
                out,
                ffn.reshape(2 * mlp_chunks, shard_rows, half_width),
            ],
            axis=0,
        ).reshape(chunks, 2, shard_rows, half_width)

    vmem = pl.BlockSpec(memory_space=pltpu.VMEM)
    hbm = pl.BlockSpec(memory_space=pl.ANY)
    smem = pl.BlockSpec(memory_space=pltpu.SMEM)
    linked = shard_rows % 16 == 0 and group % 4 == 0
    planes = group // 4
    inputs = [("doc", smem, doc_ids), ("x_in", hbm, tokens), ("cot_in", hbm, cotangent)]
    inputs += [("tables", hbm, rotary_tables(row_count))]
    token_rows = (row_count, width)
    outputs = [
        ("block_out", hbm, jax.ShapeDtypeStruct(token_rows, bf16)),
        ("input_grad", hbm, jax.ShapeDtypeStruct(token_rows, bf16)),
    ]
    by_pair = (pairs, LANES, row_count)
    scratch = [
        ("x", pltpu.VMEM(token_rows, bf16)),
        ("cot", pltpu.VMEM(token_rows, bf16)),
        ("y", pltpu.VMEM(token_rows, f32)),
        ("total", pltpu.VMEM(token_rows, f32)),
        ("dn", pltpu.VMEM(token_rows, f32)),
        ("n1t", pltpu.VMEM((width, row_count), bf16)),
        ("qt", pltpu.VMEM(by_pair, bf16)),
        ("kt", pltpu.VMEM(by_pair, bf16)),
        ("vt", pltpu.VMEM(by_pair, bf16)),
        ("k", pltpu.VMEM((pairs, row_count, LANES), bf16)),
        ("v", pltpu.VMEM((pairs, row_count, LANES), bf16)),
        ("mixt", pltpu.VMEM(by_pair, bf16)),
        ("n2", pltpu.VMEM((pairs, row_count, LANES), bf16)),
        ("n2t", pltpu.VMEM(by_pair, bf16)),
        ("hid", pltpu.VMEM((row_count, 2 * LANES), bf16)),
        ("dgu", pltpu.VMEM((row_count, 4 * LANES), bf16)),
        ("lse", pltpu.VMEM((pairs // 2, 8, row_count), f32)),
        ("cost", pltpu.VMEM((HEAD // 2, row_count), f32)),
        ("sint", pltpu.VMEM((HEAD // 2, row_count), f32)),
        ("local_sem", pltpu.SemaphoreType.DMA((3,))),
    ]
    if linked:
        lines = (planes, shard_rows, half_width)
        pair_lines = (planes, 2, shard_rows, half_width)
        whole = (planes, 4, shard_rows, half_width)
        gain_rows = (8, width)
        inputs += [
            ("attn_in", hbm, attn_weights),
            ("mlp_in", hbm, mlp_weights),
            ("gains_in", vmem, gains),
        ]
        outputs += [
            ("g_out", hbm, jax.ShapeDtypeStruct((chunks, 2, shard_rows, half_width), f32)),
            ("gain_out", vmem, jax.ShapeDtypeStruct((8, LANES), f32)),
        ]
        scratch += [
            ("w", pltpu.VMEM((chunks, 2) + whole, bf16)),
            ("g", pltpu.VMEM((2, 2) + whole, bf16)),
            ("a", pltpu.VMEM((2,) + whole, bf16)),
            ("h", pltpu.VMEM((HELD,) + whole, bf16)),
            ("b", pltpu.VMEM((4,) + pair_lines, bf16)),
            ("cs", pltpu.VMEM((2,) + lines, bf16)),
            ("c", pltpu.VMEM((4,) + lines, bf16)),
            ("kept", pltpu.VMEM((2,) + lines, f32)),
            ("ds", pltpu.VMEM((2,) + lines, bf16)),
            ("d", pltpu.VMEM((4, planes - 1) + lines[1:], bf16)),
            ("own", pltpu.VMEM((2,) + lines[1:], f32)),
            ("gout", pltpu.VMEM((6, 2) + lines[1:], f32)),
            ("gt", pltpu.VMEM((planes, 4, 16, LANES), bf16)),
            ("gain", pltpu.VMEM(gain_rows, f32)),
            ("gp", pltpu.VMEM((4,) + gain_rows, f32)),
            ("gz", pltpu.VMEM((planes,) + gain_rows, f32)),
            ("gc", pltpu.VMEM((2,) + gain_rows, f32)),
            ("load_sem", pltpu.SemaphoreType.DMA((4 + 3 * hidden // width,))),
            ("z_sem", pltpu.SemaphoreType.DMA((2, chunks, planes - 1))),
            ("line_sem", pltpu.SemaphoreType.DMA((2, chunks, 7))),
            ("gain_sem", pltpu.SemaphoreType.DMA((2, planes + 2))),
            ("rs_sem", pltpu.SemaphoreType.DMA((2, chunks, planes + 3))),
            ("leave_sem", pltpu.SemaphoreType.DMA((chunks,))),
            ("gsum_sem", pltpu.SemaphoreType.DMA((2, planes + 3))),
        ]
        params = pltpu.CompilerParams(
            collective_id=0, has_side_effects=True, vmem_limit_bytes=VMEM_BYTES
        )
    else:
        packed = pack(attn_weights.astype(bf16), mlp_weights.astype(bf16))
        full = lax.all_gather(packed, "fsdp", axis=2, tiled=True)
        gain_full = lax.all_gather(gains.astype(bf16), "fsdp", axis=1, tiled=True).astype(f32)
        inputs += [("w", vmem, full), ("gain", vmem, gain_full)]
        outputs += [
            ("g_out", hbm, jax.ShapeDtypeStruct((chunks, 2, width, half_width), bf16)),
            ("gain_out", vmem, jax.ShapeDtypeStruct((8, width), f32)),
        ]
        scratch += [
            ("g", pltpu.VMEM((2, 2, width, half_width), bf16)),
            ("g_sem", pltpu.SemaphoreType.DMA((2,))),
        ]
        params = pltpu.CompilerParams(vmem_limit_bytes=63 * 2**20)
    names = [entry[0] for entry in inputs + outputs + scratch]
    block_out, input_grad, part, gain_part = pl.pallas_call(
        functools.partial(block_kernel, linked, names),
        out_shape=[entry[2] for entry in outputs],
        in_specs=[entry[1] for entry in inputs],
        out_specs=[entry[1] for entry in outputs],
        scratch_shapes=[entry[1] for entry in scratch],
        compiler_params=params,
        name="block",
    )(*[entry[2] for entry in inputs])

    if not linked:
        part = lax.psum_scatter(part, "fsdp", scatter_dimension=2, tiled=True)
        part = lax.psum(part, "rep").astype(f32)
        part = jnp.concatenate([part[mlp_chunks + 1 :], part[mlp_chunks:][:1], part[:mlp_chunks]])
        gain_part = lax.psum_scatter(gain_part[:2], "fsdp", scatter_dimension=1, tiled=True)
        gain_part = lax.psum(gain_part, "rep")

    total_tokens = row_count * lax.axis_size("fsdp") * lax.axis_size("rep")
    rate = PEAK_RATE * STEP / (WARMUP * math.sqrt(total_tokens))

    sources = {
        "w": (attn_weights, mlp_weights, gains),
        "m": (moment_attn, moment_mlp, moment_gains),
        "e": (ema_attn, ema_mlp, ema_gains),
    }
    kinds = ["attn", "mlp", "gains"]
    whats = ["grad", "next", "velocity", "average", "copy"]
    inputs = [("out_in", hbm, block_out), ("grad_in", hbm, input_grad), ("g", hbm, part)]
    inputs += [("gain_part", vmem, gain_part)]
    outputs = [("block_out", hbm, block_out), ("input_grad", hbm, input_grad)]
    scratch = []
    for what, arrays in sources.items():
        for kind, array in zip(kinds, arrays, strict=True):
            inputs.append((f"{kind}_{what}", vmem if kind == "gains" else hbm, array))
            if kind != "gains":
                scratch.append((f"{kind}_{what}_here", pltpu.VMEM(array.shape, f32)))
    for what in whats:
        for kind, array in zip(kinds, sources["w"], strict=True):
            dtype = bf16 if what == "copy" else f32
            place = vmem if kind == "gains" else hbm
            outputs.append(
                (f"{kind}_{what}", place, jax.ShapeDtypeStruct(array.shape, dtype))
            )
            if kind != "gains":
                scratch.append((f"{kind}_{what}_here", pltpu.VMEM(array.shape, dtype)))
    scratch += [
        ("g_here", pltpu.VMEM(part.shape, f32)),
        ("in_sem", pltpu.SemaphoreType.DMA((4, 3))),
        ("out_sem", pltpu.SemaphoreType.DMA((4, 5))),
        ("pass_here", pltpu.VMEM((2,) + block_out.shape, bf16)),
        ("pass_sem", pltpu.SemaphoreType.DMA((6,))),
    ]
    names = [entry[0] for entry in inputs + outputs + scratch]
    return pl.pallas_call(
        functools.partial(update_kernel, rate, names),
        out_shape=[jax.ShapeDtypeStruct(entry[2].shape, entry[2].dtype) for entry in outputs],
        in_specs=[entry[1] for entry in inputs],
        out_specs=[entry[1] for entry in outputs],
        scratch_shapes=[entry[1] for entry in scratch],
        compiler_params=pltpu.CompilerParams(vmem_limit_bytes=63 * 2**20),
        name="update",
    )(*[entry[2] for entry in inputs])


def solution(mesh):
    rows = P(("fsdp", "rep"), None)
    shard = P("fsdp", None)
    columns = P(None, "fsdp")
    kinds = (shard, shard, columns)
    return jax.shard_map(
        local,
        mesh=mesh,
        in_specs=(rows, P(("fsdp", "rep")), rows) + kinds * 3,
        out_specs=(rows, rows) + kinds * 5,
        check_vma=False,
    )
```

```python
import functools
import math

import jax
import jax.numpy as jnp
import numpy as np
from jax import lax
from jax.experimental import pallas as pl
from jax.experimental.pallas import tpu as pltpu
from jax.sharding import PartitionSpec as P

HEAD = 64
VMEM_BYTES = 67_000_000
STEP = 5
WARMUP = 10
EPSILON = 1e-05
MASKED = -1e30
MOMENTUM = 0.5
DECAY = 0.5
PEAK_RATE = 0.1
LANES = 128
BLOCK = 256
PLAN = {
    ("pre", 0): [
        ("F", (1,)),
        ("F", (2,)),
    ],
    ("fwd", 0): [
        ("S", (1, -1, 4)),
        ("F", (3, 5, 7)),
        ("T", (-1, 1, -1)),
        ("S", (-1, 3, -1)),
        ("R", (0, 1, 2)),
        ("F", (-1, 6, -1)),
    ],
    ("fwd", 1): [
        ("S", (2, -1, 5)),
        ("F", (4, -1, -1)),
        ("f", (-1, -1, 8)),
    ],
    ("fwd", 2): [
        ("T", (-1, 2, 3)),
    ],
    ("wo", 0): [
        ("S", (6,)),
        ("f", (9,)),
        ("R", (3,)),
    ],
    ("wo", 1): [
    ],
    ("mlp", 0): [
        ("T", (4, -1, -1, 8, -1, -1, 11, -1)),
        ("S", (7, -1, -1, -1, -1, -1, -1, -1)),
        ("s", (-1, 8, -1, 11, -1, -1, -1, -1)),
        ("f", (10, 11, -1, -1, -1, -1, -1, -1)),
        ("R", (4, 5, 6, -1, -1, -1, 10, -1)),
        ("T", (-1, -1, 7, -1, -1, -1, -1, -1)),
        ("H", (-1, -1, -1, 1, 2, -1, -1, -1)),
        ("R", (-1, -1, -1, -1, 9, -1, -1, -1)),
        ("Q", (-1, -1, -1, -1, -1, 0, -1, -1)),
        ("L", (-1, -1, -1, -1, -1, -1, -1, 0)),
        ("A", (-1, 0, 1, 2, 3, 4, 5, 6)),
        ("B", (-1, -1, -1, 1, -1, 2, -1, -1)),
    ],
    ("mlp", 1): [
        ("T", (5, 6, -1, 9, -1, 10, -1, -1)),
        ("s", (-1, 9, 10, -1, -1, -1, -1, -1)),
        ("R", (-1, -1, 7, 8, -1, -1, 11, -1)),
        ("Q", (-1, -1, -1, -1, -1, -1, 1, -1)),
        ("H", (-1, 0, -1, -1, 3, 4, 5, -1)),
        ("B", (-1, 0, -1, -1, -1, -1, 3, -1)),
    ],
    ("d", 0): [
        ("Q", (2,)),
        ("H", (6,)),
        ("L", (1,)),
        ("A", (7,)),
        ("B", (4,)),
    ],
    ("o", 0): [
    ],
    ("o", 1): [
        ("Q", (3,)),
        ("H", (7,)),
        ("A", (8,)),
        ("B", (5,)),
    ],
    ("bwd", 0): [
        ("E", (0, -1, -1)),
        ("L", (2, -1, -1)),
    ],
    ("bwd", 1): [
        ("E", (-1, -1, 4)),
        ("L", (-1, 4, 6)),
        ("H", (-1, 9, 10)),
    ],
    ("bwd", 2): [
        ("E", (1, -1, -1)),
        ("Q", (4, -1, 8)),
        ("H", (8, -1, -1)),
        ("B", (6, -1, 10)),
    ],
    ("bwd", 3): [
        ("E", (-1, 3, 5)),
        ("L", (3, 5, 7)),
        ("Q", (-1, 6, -1)),
        ("B", (-1, 8, -1)),
    ],
    ("bwd", 4): [
    ],
    ("bwd", 5): [
        ("E", (2, -1, -1)),
        ("Q", (5, 7, 9)),
        ("A", (9, 10, 11)),
        ("B", (7, 9, -1)),
    ],
    ("tail", 0): [
    ],
    ("tail", 1): [
        ("E", (6,)),
        ("L", (8,)),
        ("H", (11,)),
        ("B", (11,)),
    ],
    ("tail", 2): [
        ("Q", (10,)),
    ],
    ("tail", 3): [
        ("E", (7,)),
        ("L", (9,)),
    ],
    ("end", 0): [
        ("Q", (11,)),
        ("E", (8,)),
        ("L", (10,)),
        ("E", (9,)),
        ("L", (11,)),
        ("E", (10,)),
        ("E", (11,)),
    ],
}
HELD = 4
LATE = 8

f32 = jnp.float32
bf16 = jnp.bfloat16


def nn(left, right):
    return jnp.dot(left, right, preferred_element_type=f32)


def nt(left, right):
    return lax.dot_general(
        left, right, (((1,), (1,)), ((), ())), preferred_element_type=f32
    )


def in_turn(items, stages, breaks=None):
    values = {}
    for turn in range(len(items) + len(stages) - 1):
        if breaks and turn in breaks:
            breaks[turn]()
        for number, stage in enumerate(stages):
            index = turn - number
            if 0 <= index < len(items):
                values[index] = stage(items[index], *values.get(index, ()))


def rotary_tables(row_count):
    half = HEAD // 2
    frequency = np.float32(10000.0) ** (-np.arange(half, dtype=np.float32) / np.float32(half))
    angles = np.arange(row_count, dtype=np.float32)[None, :] * frequency.astype(np.float32)[:, None]
    angles = angles.astype(np.float64)
    tables = np.stack([np.cos(angles), np.sin(angles)]).astype(np.float32)
    tables = tables.reshape(2, half, row_count // BLOCK, BLOCK).transpose(0, 2, 1, 3)
    return np.ascontiguousarray(tables.reshape(-1, BLOCK))


def rotate_rows(rows, cosine, sine):
    half = HEAD // 2
    first, second = rows[:half], rows[half:]
    return jnp.concatenate(
        [first * cosine - second * sine, second * cosine + first * sine], axis=0
    )


def rms_scale(rows):
    return lax.rsqrt(jnp.mean(rows * rows, axis=-1, keepdims=True) + EPSILON)


class Scratch:
    def __init__(self, names, refs):
        for name, ref in zip(names, refs, strict=True):
            setattr(self, name, ref)


def block_kernel(linked, names, *refs):
    s = Scratch(names, refs)
    row_count, width = s.x.shape
    blocks = row_count // BLOCK
    pairs = width // LANES
    thirds = pairs // 2
    half_width = width // 2
    chunks = s.w.shape[0]
    mlp_chunks = chunks - thirds - 1
    slots = s.g.shape[0]

    def rows_of(i):
        return pl.ds(i * BLOCK, BLOCK)

    def store_pairs(i, value):
        for p in range(pairs):
            s.n2[p, rows_of(i), :] = value[:, p * LANES : (p + 1) * LANES]

    def load_pairs(i):
        return jnp.concatenate([s.n2[p, rows_of(i), :] for p in range(pairs)], axis=1)

    def sums_at(kind, first, count, j):
        return (pl.ds(j * LANES + first, count), pl.ds(kind * BLOCK, BLOCK))

    places = [[0, 1, 2, 3], [0, 2, 1, 3]]

    def load_w(chunk, half):
        if not linked:
            return s.w[chunk, half]
        if half == 0:
            return s.w[chunk, 0].reshape(width, half_width)
        parts = [s.w[chunk, 1, z, place] for z in range(s.w.shape[2]) for place in places[1]]
        return jnp.concatenate(parts, axis=0)

    def store_g(chunk, half, lanes, value):
        low = value.astype(bf16)
        if linked and half == 0:
            low = low.reshape(s.g.shape[2:5] + (low.shape[1],))
            s.g[chunk % slots, 0, :, :, :, lanes] = low
        elif linked:
            low = low.reshape((-1,) + s.g.shape[4:5] + (low.shape[1],))
            for z in range(s.g.shape[2]):
                for index, place in enumerate(places[1]):
                    s.g[chunk % slots, 1, z, place, :, lanes] = low[4 * z + index]
        else:
            s.g[chunk % slots, half, :, lanes] = low

    if linked:
        gather_start, actions, gain_steps = links(s, chunks, thirds, mlp_chunks)
    else:


        def grad_copy(chunk):
            slot = chunk % slots
            return pltpu.make_async_copy(s.g.at[slot], s.g_out.at[chunk], s.g_sem.at[slot])

        actions = {"A": lambda chunk: grad_copy(chunk).start()}
        actions["H"] = lambda chunk: grad_copy(chunk).wait()

    def events(loop, place, index=0):
        for kind, table in PLAN[loop, place]:
            if kind not in actions:
                continue
            if isinstance(index, int):
                if table[index] >= 0:
                    actions[kind](table[index])
                continue
            used = [i for i, entry in enumerate(table) if entry >= 0]
            shift = table[used[0]] - used[0]
            in_line = all(table[i] == i + shift for i in used)
            in_line = in_line and used == list(range(used[0], used[-1] + 1))
            if in_line:
                chunk = index + shift
            else:
                chunk = jnp.int32(table[used[0]])
                for i in used[1:]:
                    chunk = jnp.where(index == i, table[i], chunk)
            if len(used) == len(table):
                actions[kind](chunk)
                continue
            if in_line:
                now = (index >= used[0]) & (index <= used[-1])
            else:
                now = functools.reduce(lambda u, v: u | v, [index == i for i in used])
            pl.when(now)(functools.partial(actions[kind], chunk))

    copies = [
        pltpu.make_async_copy(s.x_in, s.x, s.local_sem.at[0]),
        pltpu.make_async_copy(s.cot_in, s.cot, s.local_sem.at[1]),
    ]
    tables = s.total.at[pl.ds(0, HEAD * blocks), pl.ds(0, BLOCK)]
    copies.append(pltpu.make_async_copy(s.tables, tables, s.local_sem.at[2]))
    for copy in copies:
        copy.start()

    docs = [s.doc[BLOCK * j] for j in range(blocks)]
    bias = [
        [jnp.where(docs[i] == docs[j], 0.0, MASKED).astype(f32) for j in range(i)] + [0.0]
        for i in range(blocks)
    ]
    causal = lax.broadcasted_iota(jnp.int32, (BLOCK, BLOCK), 0) <= lax.broadcasted_iota(
        jnp.int32, (BLOCK, BLOCK), 1
    )

    if linked:
        gather_start[0]()
    copies.pop().wait()
    for i in range(blocks):
        place = sum([(docs[j] == docs[i]).astype(jnp.int32) for j in range(i)], jnp.int32(0))
        for index, table in enumerate([s.cost, s.sint]):
            chosen = None
            for t in range(i + 1):
                first = (index * blocks + t) * (HEAD // 2)
                part = s.total[pl.ds(first, HEAD // 2), pl.ds(0, BLOCK)]
                chosen = part if t == 0 else jnp.where(place == t, part, chosen)
            table[:, rows_of(i)] = chosen
    if linked:
        gather_start[1]()
    for copy in copies:
        copy.wait()
    if linked:
        gather_start[2]()
        events("pre", 0)
    if linked:
        gather_start[3]()
    gain_one = s.gain[0:1, :]
    gain_two = s.gain[1:2, :]
    for i in range(blocks):
        stream = s.x[rows_of(i), :].astype(f32)
        normed = (stream * rms_scale(stream) * gain_one).astype(bf16)
        s.n1t[:, rows_of(i)] = normed.T
        s.dn[rows_of(i), :] = jnp.zeros((BLOCK, width), f32)

    def masked_pair(rows, h):
        zero = jnp.zeros((HEAD, BLOCK), bf16)
        parts = [rows[:HEAD], zero] if h == 0 else [zero, rows[HEAD:]]
        return jnp.concatenate(parts, axis=0)

    def scores_of(p, i, h):
        span = (i + 1) * BLOCK
        query = masked_pair(s.qt[p, :, rows_of(i)], h)
        scores = nn(s.k[p, pl.ds(0, span), :], query)
        parts = [scores[j * BLOCK : (j + 1) * BLOCK] for j in range(i + 1)]
        parts[i] = jnp.where(causal, parts[i], MASKED)
        return parts

    mixed_order = [i for j in range(blocks // 2) for i in (blocks - 1 - j, j)]
    bodies = [(q, i, h) for q in range(2) for h in range(2) for i in mixed_order]
    half_way = 2 * blocks

    def lse_at(p, i, h):
        return (p // 2, pl.ds(2 * (p % 2) + h, 1), rows_of(i))

    def project(third, q):
        p = 2 * third + q
        weights_t = load_w(third, q).T
        for i in range(blocks):
            cosine, sine = s.cost[:, rows_of(i)], s.sint[:, rows_of(i)]
            projected = nn(weights_t, s.n1t[:, rows_of(i)])
            for h in range(2):
                lo, hi = h * HEAD, (h + 1) * HEAD
                query = rotate_rows(projected[lo:hi], cosine, sine).astype(bf16)
                s.qt[p, lo:hi, rows_of(i)] = query * bf16(0.125)
                key = rotate_rows(projected[LANES + lo : LANES + hi], cosine, sine)
                s.kt[p, lo:hi, rows_of(i)] = key.astype(bf16)
            s.vt[p, :, rows_of(i)] = projected[2 * LANES :].astype(bf16)
            s.k[p, rows_of(i), :] = s.kt[p, :, rows_of(i)].T
            s.v[p, rows_of(i), :] = s.vt[p, :, rows_of(i)].T

    def attention_forward(third, carry):
        events("fwd", 0, third)
        project(third, 0)
        project(third, 1)
        events("fwd", 1, third)

        def scores(n):
            q, i, h = n
            return (scores_of(2 * third + q, i, h),)

        def shares(n, parts):
            q, i, h = n
            p = 2 * third + q
            tops = [
                jnp.max(part, axis=0, keepdims=True) + bias[i][j]
                for j, part in enumerate(parts)
            ]
            top = functools.reduce(jnp.maximum, tops)
            exps = [jnp.exp(part - (top - bias[i][j])) for j, part in enumerate(parts)]
            total = sum([jnp.sum(e, axis=0, keepdims=True) for e in exps])
            s.lse[lse_at(p, i, h)] = top + jnp.log(total)
            return jnp.concatenate([e.astype(bf16) for e in exps], axis=0), 1.0 / total

        def mix(n, exps_low, inverse):
            q, i, h = n
            p = 2 * third + q
            heads = pl.ds(h * HEAD, HEAD)
            mixed = nn(s.vt[p, heads, pl.ds(0, (i + 1) * BLOCK)], exps_low)
            s.mixt[p, heads, rows_of(i)] = (mixed * inverse).astype(bf16)

        in_turn(
            bodies,
            [scores, shares, mix],
            {half_way: lambda: events("fwd", 2, third)},
        )
        return carry

    lax.fori_loop(0, thirds, attention_forward, 0)

    out_chunk = thirds
    for i in range(blocks):
        if i % 2 == 0:
            events("wo", i // 2)
        mixed = s.mixt[:, :, rows_of(i)].reshape(width, BLOCK).T
        branch = jnp.concatenate(
            [nn(mixed, load_w(out_chunk, half)) for half in range(2)], axis=1
        )
        after = s.x[rows_of(i), :].astype(f32) + branch
        s.y[rows_of(i), :] = after
        s.total[rows_of(i), :] = after
        normed = (after * rms_scale(after) * gain_two).astype(bf16)
        store_pairs(i, normed)
        s.n2t[:, :, rows_of(i)] = normed.T.reshape(pairs, LANES, BLOCK)

    tiles = [pl.ds(t * BLOCK, BLOCK) for t in range(width // BLOCK)]
    for i in range(blocks):
        for tile in tiles:
            s.x[rows_of(i), tile] = s.cot[rows_of(i), tile].T

    def feed_forward(chunk, carry):
        events("mlp", 0, chunk)
        low = [load_w(thirds + 1 + chunk, half) for half in range(2)]
        w_gu = [w[:, : 2 * LANES] for w in low]
        w_gu_all = jnp.concatenate(w_gu, axis=1)
        w_down = jnp.concatenate([w[:, 2 * LANES :] for w in low], axis=1)

        def products(i):
            normed = load_pairs(i)
            d_hidden = nn(s.cot[rows_of(i), :], w_down)
            return d_hidden, [nn(normed, w) for w in w_gu]

        def slopes(i, d_hidden, gate_ups):
            for half, gate_up in enumerate(gate_ups):
                gate, up = gate_up[:, :LANES], gate_up[:, LANES:]
                back = d_hidden[:, half * LANES : (half + 1) * LANES]
                sig = jax.nn.sigmoid(gate)
                silu = gate * sig
                s.hid[rows_of(i), pl.ds(half * LANES, LANES)] = (silu * up).astype(bf16)
                s.dgu[rows_of(i), pl.ds(2 * half * LANES, LANES)] = (
                    back * up * (sig + silu * (1.0 - sig))
                ).astype(bf16)
                s.dgu[rows_of(i), pl.ds((2 * half + 1) * LANES, LANES)] = (
                    back * silu
                ).astype(bf16)
            return ()

        def sums(i):
            s.total[rows_of(i), :] += nt(s.hid[rows_of(i), :], w_down)
            s.dn[rows_of(i), :] += nt(s.dgu[rows_of(i), :], w_gu_all)

        in_turn(list(range(blocks)), [products, slopes, sums])
        events("mlp", 1, chunk)
        n2t = s.n2t[...].reshape(width, row_count)
        for half in range(2):
            store_g(
                chunk,
                half,
                pl.ds(0, 2 * LANES),
                nn(n2t, s.dgu[:, pl.ds(2 * half * LANES, 2 * LANES)]),
            )
        grad_down = jnp.concatenate(
            [
                nn(
                    jnp.concatenate([s.x[rows_of(i), tile] for i in range(blocks)], axis=1),
                    s.hid[...],
                )
                for tile in tiles
            ],
            axis=0,
        )
        for half in range(2):
            store_g(
                chunk,
                half,
                pl.ds(2 * LANES, LANES),
                grad_down[:, half * LANES : (half + 1) * LANES],
            )
        return carry

    lax.fori_loop(0, mlp_chunks, feed_forward, 0)

    events("d", 0)
    x_copy = pltpu.make_async_copy(s.x_in, s.x, s.local_sem.at[1])
    x_copy.start()

    gain_grad_two = jnp.zeros((1, width), f32)
    for i in range(blocks):
        after = s.y[rows_of(i), :]
        scale = rms_scale(after)
        unit = after * scale
        d_normed = s.dn[rows_of(i), :]
        d_unit = d_normed * gain_two
        gain_grad_two += jnp.sum(d_normed * unit, axis=0, keepdims=True)
        grad_after = s.cot[rows_of(i), :].astype(f32) + scale * (
            d_unit - unit * jnp.mean(d_unit * unit, axis=-1, keepdims=True)
        )
        s.y[rows_of(i), :] = grad_after
        store_pairs(i, grad_after.astype(bf16))
        s.cot[rows_of(i), :] = s.total[rows_of(i), :].astype(bf16)
    out_copy = pltpu.make_async_copy(s.cot, s.block_out, s.local_sem.at[0])
    out_copy.start()

    events("o", 0)
    mixt = s.mixt[...].reshape(width, row_count)
    for half in range(2):
        store_g(
            mlp_chunks,
            half,
            pl.ds(0, half_width),
            nn(mixt, jnp.concatenate([s.n2[p] for p in range(half * thirds, (half + 1) * thirds)], axis=1)),
        )
    events("o", 1)
    dmt = s.n2t
    w_out = jnp.concatenate([load_w(out_chunk, half) for half in range(2)], axis=1)
    for i in range(blocks):
        d_mixed = nt(w_out, load_pairs(i))
        dmt[:, :, rows_of(i)] = d_mixed.astype(bf16).reshape(pairs, LANES, BLOCK)

    def turn_back(p, q, i):
        cosine, sine = s.cost[:, rows_of(i)], -s.sint[:, rows_of(i)]
        pieces = []
        for kind in range(2):
            for h in range(2):
                piece = s.total[sums_at(kind, h * HEAD, HEAD, q * blocks + i)]
                piece = rotate_rows(piece, cosine, sine)
                pieces.append((piece * 0.125 if kind == 0 else piece).astype(bf16))
        s.k[p, rows_of(i), :] = jnp.concatenate(pieces[:2], axis=0).T
        s.v[p, rows_of(i), :] = jnp.concatenate(pieces[2:], axis=0).T
        s.n2[p, rows_of(i), :] = s.total[sums_at(2, 0, LANES, q * blocks + i)].astype(bf16).T

    def attention_backward(third, carry):
        events("bwd", 0, third)
        for j in range(2 * blocks):
            for kind in (1, 2):
                s.total[sums_at(kind, 0, LANES, j)] = jnp.zeros((LANES, BLOCK), f32)

        def begin(n):
            q, i, h = n
            p = 2 * third + q
            back = masked_pair(dmt[p, :, rows_of(i)], h)
            return scores_of(p, i, h), nn(s.v[p, pl.ds(0, (i + 1) * BLOCK), :], back)

        def middle(n, parts, d_probs):
            q, i, h = n
            lse = s.lse[lse_at(2 * third + q, i, h)]
            probs = [jnp.exp(part - (lse - bias[i][j])) for j, part in enumerate(parts)]
            probs = jnp.concatenate(probs, axis=0)
            weighted = probs * d_probs
            inner = jnp.sum(weighted, axis=0, keepdims=True)
            return (weighted - probs * inner).astype(bf16), probs.astype(bf16)

        def finish(n, d_scores, probs_low):
            q, i, h = n
            p = 2 * third + q
            heads, keys = pl.ds(h * HEAD, HEAD), pl.ds(0, (i + 1) * BLOCK)
            s.total[sums_at(0, h * HEAD, HEAD, q * blocks + i)] = nn(
                s.kt[p, heads, keys], d_scores
            )
            d_keys = nt(s.qt[p, heads, rows_of(i)], d_scores)
            d_values = nt(dmt[p, heads, rows_of(i)], probs_low)
            for j in range(i + 1):
                span = slice(j * BLOCK, (j + 1) * BLOCK)
                s.total[sums_at(1, h * HEAD, HEAD, q * blocks + j)] += d_keys[:, span]
                s.total[sums_at(2, h * HEAD, HEAD, q * blocks + j)] += d_values[:, span]
            number = bodies.index(n) - half_way
            if 0 <= number < blocks:
                turn_back(2 * third, 0, number)

        in_turn(
            bodies,
            [begin, middle, finish],
            {
                half_way // 2 + 2: lambda: events("bwd", 1, third),
                half_way + 2: lambda: events("bwd", 2, third),
                half_way + half_way // 2 + 2: lambda: events("bwd", 3, third),
            },
        )
        events("bwd", 4, third)
        for i in range(blocks):
            turn_back(2 * third + 1, 1, i)
        for q in range(2):
            p = 2 * third + q
            d_qkv = jnp.concatenate([s.k[p], s.v[p], s.n2[p]], axis=1)
            store_g(
                mlp_chunks + 1 + third, q, pl.ds(0, half_width), nn(s.n1t[...], d_qkv)
            )
        events("bwd", 5, third)
        return carry

    lax.fori_loop(0, thirds, attention_backward, 0)

    x_copy.wait()
    w_qkv_t = jnp.concatenate([load_w(p // 2, p % 2).T for p in range(pairs)], axis=0)
    gain_grad_one = jnp.zeros((1, width), f32)
    for i in range(blocks):
        events("tail", i)
        d_qkv = [
            ref[p, rows_of(i), :] for p in range(pairs) for ref in (s.k, s.v, s.n2)
        ]
        d_normed = nn(jnp.concatenate(d_qkv, axis=1), w_qkv_t)
        stream = s.x[rows_of(i), :].astype(f32)
        scale = rms_scale(stream)
        unit = stream * scale
        d_unit = d_normed * gain_one
        gain_grad_one += jnp.sum(d_normed * unit, axis=0, keepdims=True)
        s.x[rows_of(i), :] = (
            s.y[rows_of(i), :]
            + scale * (d_unit - unit * jnp.mean(d_unit * unit, axis=-1, keepdims=True))
        ).astype(bf16)
    grad_copy_out = pltpu.make_async_copy(s.x, s.input_grad, s.local_sem.at[1])
    grad_copy_out.start()
    gain_grads = jnp.concatenate(
        [gain_grad_one, gain_grad_two, jnp.zeros((6, width), f32)], axis=0
    )
    if linked:
        gain_steps[0](gain_grads)
        left = list(gain_steps[1:4])
        for kind, table in PLAN["end", 0]:
            actions[kind](table[0])
            if kind in "QLE" and left:
                left.pop(0)()
        for step in left:
            step()
        gain_steps[4]()
    else:
        events("end", 0)
        s.gain_out[...] = gain_grads
    out_copy.wait()
    grad_copy_out.wait()


def links(s, chunks, thirds, mlp_chunks):
    planes = s.w.shape[2]
    me = lax.axis_index("fsdp")
    core = lax.axis_index("rep")
    z, m = me // 4, me % 4
    over_x, over_y, over_both = m + 1 - 2 * (m % 2), (m + 2) % 4, 3 - m
    m1 = (1 - core) * over_x + core * over_y
    m2 = (1 - core) * over_y + core * over_x
    other = 1 - core
    low = (1 - core) * (m % 2) + core * (m // 2)
    high = (1 - core) * (m // 2) + core * (m % 2)
    place = 2 * high + low

    def chip(plane, place):
        return (plane * 4 + place, core)

    sibling = (me, other)

    def far(k):
        return (z + k) % planes

    peers = [chip(far(k), m) for k in range(1, planes)]
    first, second = chip(z, m1), chip(z, m2)

    def remote(src, dst, send_sem, recv_sem, device):
        return pltpu.make_async_remote_copy(
            src_ref=src,
            dst_ref=dst,
            send_sem=send_sem,
            recv_sem=recv_sem,
            device_id=device,
            device_id_type=pl.DeviceIdType.MESH,
        )

    def along_z(chunk, k):
        block = s.w.at[chunk, core, z, place]
        return remote(block, block, s.sent_sem.at[0], s.hop_sem.at[chunk, 0], peers[k])

    def along_z_here(chunk):
        blocks = s.w.at[chunk, core, pl.ds(0, planes - 1), place]
        return remote(blocks, blocks, s.sent_sem.at[0], s.hop_sem.at[chunk, 0], peers[0])

    def hop(chunk, index):
        if index == 1:
            blocks, device = s.w.at[chunk, core, :, place], first
        elif index == 2:
            blocks, device = s.w.at[chunk, core, :, pl.ds(2 * high, 2)], second
        else:
            blocks, device = s.w.at[chunk, core], sibling
        return remote(blocks, blocks, s.sent_sem.at[index], s.hop_sem.at[chunk, index], device)

    def alone(chunk):
        block = s.w.at[chunk, core, z, place]
        return remote(block, block, s.sent_sem.at[5], s.hop_sem.at[chunk, 1], first)

    def along_z_again(chunk, k):
        block = s.w.at[chunk, core, z, place + 1 - 2 * low]
        return remote(block, block, s.sent_sem.at[4], s.hop_sem.at[chunk, 4], peers[k])

    def along_z_again_here(chunk):
        blocks = s.w.at[chunk, core, pl.ds(0, planes - 1), place]
        return remote(blocks, blocks, s.sent_sem.at[4], s.hop_sem.at[chunk, 4], peers[0])

    def gather_end():
        late = pl.ds(LATE, chunks - LATE)
        blocks = s.w.at[late, core, pl.ds(0, planes - 1), place]
        remote(blocks, blocks, s.sent_sem.at[4], s.hop_sem.at[0, 4], peers[0]).wait_send()
        blocks = s.w.at[late, core, z, place]
        remote(blocks, blocks, s.sent_sem.at[5], s.hop_sem.at[0, 1], first).wait_send()
        blocks = s.w.at[:, core, pl.ds(0, planes - 1), place]
        remote(blocks, blocks, s.sent_sem.at[0], s.hop_sem.at[0, 0], peers[0]).wait_send()
        blocks = s.w.at[pl.ds(0, LATE), core, :, place]
        remote(blocks, blocks, s.sent_sem.at[1], s.hop_sem.at[0, 1], first).wait_send()
        blocks = s.w.at[:, core, :, pl.ds(2 * high, 2)]
        remote(blocks, blocks, s.sent_sem.at[2], s.hop_sem.at[0, 2], second).wait_send()
        blocks = s.w.at[:, core]
        remote(blocks, blocks, s.sent_sem.at[3], s.hop_sem.at[0, 3], sibling).wait_send()

    def gain_along_z(k):
        block = s.gt.at[z, m]
        return remote(block, block, s.gain_sem.at[0, k], s.gain_sem.at[1, k], peers[k])

    def gain_hop(index):
        blocks = s.gt.at[:, [m, m, m1][index]]
        device = [first, second, second][index]
        k = planes - 1 + index
        return remote(blocks, blocks, s.gain_sem.at[0, k], s.gain_sem.at[1, k], device)

    width = s.x.shape[1]
    pairs = width // LANES
    shard_rows = s.w.shape[4]
    half_width = s.w.shape[5]
    hidden = s.mlp_in.shape[1] // 3
    loads = [
        functools.partial(
            pltpu.make_async_copy,
            s.attn_in.at[:, pl.ds(k * width, width)],
            s.dn.at[pl.ds(k * shard_rows, shard_rows)],
            s.load_sem.at[k],
        )
        for k in range(4)
    ] + [
        functools.partial(
            pltpu.make_async_copy,
            s.mlp_in.at[:, pl.ds(k * width, width)],
            s.dn.at[pl.ds((4 + k) * shard_rows, shard_rows)],
            s.load_sem.at[4 + k],
        )
        for k in range(3 * hidden // width)
    ]

    def piece(row, lane):
        rows = s.dn[pl.ds(row * shard_rows, shard_rows), pl.ds(lane, LANES)]
        return rows.astype(bf16)

    def round_third(third):
        lane = pl.multiple_of((2 * third + core) * LANES, LANES)
        for kind in range(3):
            s.w[third, core, z, place, :, kind * LANES : (kind + 1) * LANES] = piece(kind, lane)

    def gather_start():
        barrier = pltpu.get_barrier_semaphore()
        partners = [chip(z, over_x), chip(z, over_y), chip(z, over_both), sibling] + peers
        for partner in partners:
            pl.semaphore_signal(
                barrier, inc=1, device_id=partner, device_id_type=pl.DeviceIdType.MESH
            )
        for load in loads:
            load().start()
        own = s.gains_in[...].astype(bf16)
        own = jnp.concatenate([own, jnp.zeros((2, LANES - shard_rows), bf16)], axis=1)
        s.gt[z, m] = jnp.concatenate([own, jnp.zeros((14, LANES), bf16)], axis=0)
        for load in loads[:3]:
            load().wait()
        round_third(0)
        pl.semaphore_wait(barrier, len(partners))
        for k in range(planes - 1):
            along_z(0, k).start()
        for k in range(planes - 1):
            gain_along_z(k).start()
        loads[3]().wait()
        for third in range(1, thirds):
            round_third(third)
        lane = pl.multiple_of(core * half_width, LANES)
        s.w[thirds, core, z, place] = s.dn[
            pl.ds(3 * shard_rows, shard_rows), pl.ds(lane, half_width)
        ].astype(bf16)
        for chunk in range(1, thirds + 1):
            for k in range(planes - 1):
                along_z(chunk, k).start()

    def gather_feed_forward():
        for load in loads[4:]:
            load().wait()
        for j in range(mlp_chunks):
            for kind in range(3):
                column = kind * hidden + 2 * j * LANES
                row, begin = 4 + column // width, column % width
                lane = pl.multiple_of(begin + core * LANES, LANES)
                s.w[thirds + 1 + j, core, z, place, :, kind * LANES : (kind + 1) * LANES] = (
                    piece(row, lane)
                )
            for k in range(planes - 1):
                along_z(thirds + 1 + j, k).start()
            if thirds + 1 + j >= LATE:
                alone(thirds + 1 + j).start()

    def gather_one():
        first_hop(0)
        for k in range(planes - 1):
            gain_along_z(k).wait()
        gain_hop(0).start()
        gain_hop(1).start()
        gather_feed_forward()

    def gather_two():
        second_hop(0)
        gain_hop(0).wait()
        gain_hop(2).start()

    def gather_three():
        gain_hop(1).wait()
        gain_hop(2).wait()
        rows = jnp.zeros((8, width), f32)
        for d in range(planes * 4):
            tile = s.gt[d // 4, d % 4].astype(f32)[:8]
            wide = jnp.concatenate([tile, jnp.zeros((8, width - LANES), f32)], axis=1)
            rows += pltpu.roll(wide, d * shard_rows, 1) if d else wide
        s.gain[...] = rows
        third_hop(0)

    def first_hop(chunk):
        along_z_here(chunk).wait_recv()
        hop(chunk, 1).start()

    def first_hop_late(chunk):
        alone(chunk).wait_recv()
        for k in range(planes - 1):
            along_z_again(chunk, k).start()

    def second_hop_late(chunk):
        along_z_here(chunk).wait_recv()
        along_z_again_here(chunk).wait_recv()
        hop(chunk, 2).start()

    def second_hop(chunk):
        hop(chunk, 1).wait_recv()
        hop(chunk, 2).start()

    def third_hop(chunk):
        hop(chunk, 2).wait_recv()
        hop(chunk, 3).start()

    def ready(chunk):
        hop(chunk, 3).wait_recv()

    held = s.h.shape[0]

    def to_sibling(chunk):
        return remote(
            s.g.at[chunk % 2, other],
            s.a.at[chunk % 2],
            s.rs_sem.at[chunk, 0, 0],
            s.rs_sem.at[chunk, 0, 1],
            sibling,
        )

    def to_second(chunk):
        return remote(
            s.h.at[chunk % held, :, pl.ds(2 - 2 * high, 2)],
            s.b.at[chunk % 4],
            s.rs_sem.at[chunk, 1, 0],
            s.rs_sem.at[chunk, 1, 1],
            second,
        )

    def to_first(chunk):
        return remote(
            s.cs.at[chunk % 2],
            s.c.at[chunk % 4],
            s.rs_sem.at[chunk, 2, 0],
            s.rs_sem.at[chunk, 2, 1],
            first,
        )

    def to_plane(chunk, k):
        return remote(
            s.ds.at[chunk % 2, far(k + 1)],
            s.d.at[chunk % 4, k],
            s.rs_sem.at[chunk, 3, 0],
            s.rs_sem.at[chunk, 3, 1],
            peers[k],
        )

    def to_planes(chunk):
        return remote(
            s.ds.at[chunk % 2, pl.ds(0, planes - 1)],
            s.d.at[chunk % 4],
            s.rs_sem.at[chunk, 3, 0],
            s.rs_sem.at[chunk, 3, 1],
            peers[0],
        )

    def place_of(chunk):
        return jnp.where(
            chunk < mlp_chunks,
            thirds + 1 + chunk,
            jnp.where(chunk == mlp_chunks, thirds, chunk - mlp_chunks - 1),
        )

    def to_copy(chunk):
        done = s.g_out.at[place_of(chunk), core]
        sems = s.end_sem.at[chunk, 0], s.end_sem.at[0, 2]
        return remote(s.gout.at[chunk % 6], done, *sems, sibling)

    def leave(chunk):
        done = s.g_out.at[place_of(chunk), core]
        return pltpu.make_async_copy(s.gout.at[chunk % 6], done, s.end_sem.at[chunk, 1])

    def left(chunk):
        to_copy(chunk).wait_send()
        leave(chunk).wait()

    def reduce_end():
        done = s.g_out.at[:, core]
        remote(done, done, s.end_sem.at[0, 0], s.end_sem.at[0, 2], sibling).wait_recv()
        for chunk in range(chunks - 6, chunks):
            left(chunk)

    def send_half(chunk):
        to_sibling(chunk).start()

    def add_half(chunk):
        to_sibling(chunk).wait()
        s.h[chunk % held] = (
            s.g[chunk % 2, core].astype(f32) + s.a[chunk % 2].astype(f32)
        ).astype(bf16)

    def halves(chunk):
        to_second(chunk).start()

    def quarters(chunk):
        to_second(chunk).wait()
        even = chunk % 2
        s.cs[even] = (
            s.h[chunk % held, :, 2 * high + 1 - low].astype(f32)
            + s.b[chunk % 4, :, 1 - low].astype(f32)
        ).astype(bf16)
        to_first(chunk).start()
        s.kept[even] = (
            s.h[chunk % held, :, place].astype(f32) + s.b[chunk % 4, :, low].astype(f32)
        ).astype(bf16)

    def lines(chunk):
        to_first(chunk).wait()
        even = chunk % 2
        s.ds[even] = (s.kept[even].astype(f32) + s.c[chunk % 4].astype(f32)).astype(bf16)
        for k in range(planes - 1):
            to_plane(chunk, k).start()
        s.own[even] = s.kept[even, z].astype(f32) + s.c[chunk % 4, z].astype(f32)

    def last(chunk):
        to_planes(chunk).wait()
        total = s.own[chunk % 2]
        for k in range(planes - 1):
            total += s.d[chunk % 4, k].astype(f32)
        if isinstance(chunk, int):
            if chunk >= 6:
                left(chunk - 6)
        else:
            pl.when(chunk >= 6)(lambda: left(chunk - 6))
        s.gout[chunk % 6] = total
        to_copy(chunk).start()
        leave(chunk).start()

    actions = {"F": first_hop, "S": second_hop, "T": third_hop, "R": ready}
    actions.update({"A": send_half, "H": add_half, "B": halves, "Q": quarters})
    actions.update({"L": lines, "E": last, "f": first_hop_late, "s": second_hop_late})

    def plane_sum():
        block = s.gp.at[m]
        return [
            remote(block, block, s.gsum_sem.at[0, k], s.gsum_sem.at[1, k], chip(z, at))
            for k, at in enumerate([over_x, over_y, over_both])
        ]

    def line_sum():
        block = s.gz.at[z]
        return [
            remote(block, block, s.gsum_sem.at[0, 3 + k], s.gsum_sem.at[1, 3 + k], peers[k])
            for k in range(planes - 1)
        ]

    def core_sum():
        k = planes + 2
        sems = s.gsum_sem
        return remote(s.gc.at[0], s.gc.at[1], sems.at[0, k], sems.at[1, k], sibling)

    def gain_begin(value):
        s.gp[m] = value
        for copy in plane_sum():
            copy.start()

    def gain_lines_sum():
        for copy in plane_sum():
            copy.wait()
        s.gz[z] = (s.gp[0] + s.gp[1]) + (s.gp[2] + s.gp[3])
        for copy in line_sum():
            copy.start()

    def gain_cores():
        for copy in line_sum():
            copy.wait()
        total = s.gz[0]
        for k in range(1, planes):
            total += s.gz[k]
        s.gc[0] = total
        core_sum().start()

    def gain_end():
        core_sum().wait()
        total = s.gc[0] + s.gc[1]
        s.gain_out[...] = pltpu.roll(total, (width - me * shard_rows) % width, 1)[:, :LANES]

    def gain_out():
        gather_end()
        reduce_end()

    start = (gather_start, gather_one, gather_two, gather_three)
    return start, actions, (gain_begin, gain_lines_sum, gain_cores, gain_end, gain_out)


def update_kernel(rate, names, *refs):
    s = Scratch(names, refs)
    width = s.attn_w.shape[1] // 4
    hidden = s.mlp_w.shape[1] // 3
    pairs = width // LANES
    thirds = pairs // 2
    half_width = width // 2
    whats = ["grad", "next", "velocity", "average", "copy"]

    def rule(weight, grad, moment, average):
        velocity = MOMENTUM * moment + grad
        weight_new = weight - rate * (grad + MOMENTUM * velocity)
        average_new = DECAY * average + (1.0 - DECAY) * weight_new
        return grad, weight_new, velocity, average_new, weight_new.astype(bf16)

    attn_blocks = [
        (kind * width + pair * LANES, LANES, (pair // 2, pair % 2), kind * LANES)
        for kind in range(3)
        for pair in range(pairs)
    ] + [(3 * width + half * half_width, half_width, (thirds, half), 0) for half in range(2)]
    pieces = [("attn", 0, 4 * width, attn_blocks)] + [
        (
            "mlp",
            kind * hidden,
            hidden,
            [
                (kind * hidden + b * LANES, LANES, (thirds + 1 + b // 2, b % 2), kind * LANES)
                for b in range(hidden // LANES)
            ],
        )
        for kind in range(3)
    ]

    def loads(index):
        kind, first, count, _ = pieces[index]
        span = pl.ds(first, count)
        return [
            pltpu.make_async_copy(
                getattr(s, f"{kind}_{what}").at[:, span],
                getattr(s, f"{kind}_{what}_here").at[:, span],
                s.in_sem.at[index, k],
            )
            for k, what in enumerate(["w", "m", "e"])
        ]

    def stores(index):
        kind, first, count, _ = pieces[index]
        span = pl.ds(first, count)
        return [
            pltpu.make_async_copy(
                getattr(s, f"{kind}_{what}_here").at[:, span],
                getattr(s, f"{kind}_{what}").at[:, span],
                s.out_sem.at[index, k],
            )
            for k, what in enumerate(whats)
        ]

    enter = [
        pltpu.make_async_copy(s.out_in, s.pass_here.at[0], s.pass_sem.at[0]),
        pltpu.make_async_copy(s.grad_in, s.pass_here.at[1], s.pass_sem.at[1]),
    ]
    leave = [
        pltpu.make_async_copy(s.pass_here.at[0], s.block_out, s.pass_sem.at[4]),
        pltpu.make_async_copy(s.pass_here.at[1], s.input_grad, s.pass_sem.at[5]),
    ]
    grads = [
        pltpu.make_async_copy(
            s.g.at[pl.ds(0, thirds + 1)], s.g_here.at[pl.ds(0, thirds + 1)], s.pass_sem.at[2]
        ),
        pltpu.make_async_copy(
            s.g.at[pl.ds(thirds + 1, s.g.shape[0] - thirds - 1)],
            s.g_here.at[pl.ds(thirds + 1, s.g.shape[0] - thirds - 1)],
            s.pass_sem.at[3],
        ),
    ]
    grads[0].start()
    for load in loads(0):
        load.start()
    grads[1].start()
    for index in range(1, len(pieces)):
        for load in loads(index):
            load.start()
    for copy in enter:
        copy.start()
    shard_rows = s.attn_w.shape[0]
    results = rule(s.gains_w[...], s.gain_part[:2, :shard_rows], s.gains_m[...], s.gains_e[...])
    for what, result in zip(whats, results, strict=True):
        getattr(s, f"gains_{what}")[...] = result
    for index, (kind, _, _, blocks) in enumerate(pieces):
        if index < 2:
            grads[index].wait()
        for load in loads(index):
            load.wait()
        for first, count, chunk, lane in blocks:
            span = slice(first, first + count)
            results = rule(
                getattr(s, f"{kind}_w_here")[:, span],
                s.g_here[chunk[0], chunk[1], :, lane : lane + count],
                getattr(s, f"{kind}_m_here")[:, span],
                getattr(s, f"{kind}_e_here")[:, span],
            )
            for what, result in zip(whats, results, strict=True):
                getattr(s, f"{kind}_{what}_here")[:, span] = result
        for store in stores(index):
            store.start()
    for copy_in, copy_out in zip(enter, leave, strict=True):
        copy_in.wait()
        copy_out.start()
    for index in range(len(pieces)):
        for store in stores(index):
            store.wait()
    for copy in leave:
        copy.wait()


def local(
    tokens,
    doc_ids,
    cotangent,
    attn_weights,
    mlp_weights,
    gains,
    moment_attn,
    moment_mlp,
    moment_gains,
    ema_attn,
    ema_mlp,
    ema_gains,
):
    row_count, width = tokens.shape
    shard_rows = attn_weights.shape[0]
    group = width // shard_rows
    pairs = width // LANES
    hidden = mlp_weights.shape[1] // 3
    half_width = width // 2
    thirds = pairs // 2
    mlp_chunks = hidden // (2 * LANES)
    chunks = thirds + 1 + mlp_chunks

    def pack(attn, mlp):
        qkv = attn[:, : 3 * width].reshape(shard_rows, 3, pairs, LANES).transpose(2, 0, 1, 3)
        out = attn[:, 3 * width :].reshape(shard_rows, 2, half_width).transpose(1, 0, 2)
        ffn = mlp.reshape(shard_rows, 3, 2 * mlp_chunks, LANES).transpose(2, 0, 1, 3)
        return jnp.concatenate(
            [
                qkv.reshape(pairs, shard_rows, half_width),
                out,
                ffn.reshape(2 * mlp_chunks, shard_rows, half_width),
            ],
            axis=0,
        ).reshape(chunks, 2, shard_rows, half_width)

    vmem = pl.BlockSpec(memory_space=pltpu.VMEM)
    hbm = pl.BlockSpec(memory_space=pl.ANY)
    smem = pl.BlockSpec(memory_space=pltpu.SMEM)
    linked = shard_rows % 16 == 0 and group % 4 == 0
    planes = group // 4
    inputs = [("doc", smem, doc_ids), ("x_in", hbm, tokens), ("cot_in", hbm, cotangent)]
    inputs += [("tables", hbm, rotary_tables(row_count))]
    token_rows = (row_count, width)
    outputs = [
        ("block_out", hbm, jax.ShapeDtypeStruct(token_rows, bf16)),
        ("input_grad", hbm, jax.ShapeDtypeStruct(token_rows, bf16)),
    ]
    by_pair = (pairs, LANES, row_count)
    scratch = [
        ("x", pltpu.VMEM(token_rows, bf16)),
        ("cot", pltpu.VMEM(token_rows, bf16)),
        ("y", pltpu.VMEM(token_rows, f32)),
        ("total", pltpu.VMEM(token_rows, f32)),
        ("dn", pltpu.VMEM(token_rows, f32)),
        ("n1t", pltpu.VMEM((width, row_count), bf16)),
        ("qt", pltpu.VMEM(by_pair, bf16)),
        ("kt", pltpu.VMEM(by_pair, bf16)),
        ("vt", pltpu.VMEM(by_pair, bf16)),
        ("k", pltpu.VMEM((pairs, row_count, LANES), bf16)),
        ("v", pltpu.VMEM((pairs, row_count, LANES), bf16)),
        ("mixt", pltpu.VMEM(by_pair, bf16)),
        ("n2", pltpu.VMEM((pairs, row_count, LANES), bf16)),
        ("n2t", pltpu.VMEM(by_pair, bf16)),
        ("hid", pltpu.VMEM((row_count, 2 * LANES), bf16)),
        ("dgu", pltpu.VMEM((row_count, 4 * LANES), bf16)),
        ("lse", pltpu.VMEM((pairs // 2, 8, row_count), f32)),
        ("cost", pltpu.VMEM((HEAD // 2, row_count), f32)),
        ("sint", pltpu.VMEM((HEAD // 2, row_count), f32)),
        ("local_sem", pltpu.SemaphoreType.DMA((3,))),
    ]
    if linked:
        lines = (planes, shard_rows, half_width)
        pair_lines = (planes, 2, shard_rows, half_width)
        whole = (planes, 4, shard_rows, half_width)
        gain_rows = (8, width)
        inputs += [
            ("attn_in", hbm, attn_weights),
            ("mlp_in", hbm, mlp_weights),
            ("gains_in", vmem, gains),
        ]
        outputs += [
            ("g_out", hbm, jax.ShapeDtypeStruct((chunks, 2, shard_rows, half_width), f32)),
            ("gain_out", vmem, jax.ShapeDtypeStruct((8, LANES), f32)),
        ]
        scratch += [
            ("w", pltpu.VMEM((chunks, 2) + whole, bf16)),
            ("g", pltpu.VMEM((2, 2) + whole, bf16)),
            ("a", pltpu.VMEM((2,) + whole, bf16)),
            ("h", pltpu.VMEM((HELD,) + whole, bf16)),
            ("b", pltpu.VMEM((4,) + pair_lines, bf16)),
            ("cs", pltpu.VMEM((2,) + lines, bf16)),
            ("c", pltpu.VMEM((4,) + lines, bf16)),
            ("kept", pltpu.VMEM((2,) + lines, bf16)),
            ("ds", pltpu.VMEM((2,) + lines, bf16)),
            ("d", pltpu.VMEM((4, planes - 1) + lines[1:], bf16)),
            ("own", pltpu.VMEM((2,) + lines[1:], f32)),
            ("gout", pltpu.VMEM((6,) + lines[1:], f32)),
            ("gt", pltpu.VMEM((planes, 4, 16, LANES), bf16)),
            ("gain", pltpu.VMEM(gain_rows, f32)),
            ("gp", pltpu.VMEM((4,) + gain_rows, f32)),
            ("gz", pltpu.VMEM((planes,) + gain_rows, f32)),
            ("gc", pltpu.VMEM((2,) + gain_rows, f32)),
            ("load_sem", pltpu.SemaphoreType.DMA((4 + 3 * hidden // width,))),
            ("hop_sem", pltpu.SemaphoreType.DMA((chunks, 5))),
            ("sent_sem", pltpu.SemaphoreType.DMA((6,))),
            ("gain_sem", pltpu.SemaphoreType.DMA((2, planes + 2))),
            ("rs_sem", pltpu.SemaphoreType.DMA((chunks, 4, 2))),
            ("end_sem", pltpu.SemaphoreType.DMA((chunks, 3))),
            ("gsum_sem", pltpu.SemaphoreType.DMA((2, planes + 3))),
        ]
        params = pltpu.CompilerParams(
            collective_id=0, has_side_effects=True, vmem_limit_bytes=VMEM_BYTES
        )
    else:
        packed = pack(attn_weights.astype(bf16), mlp_weights.astype(bf16))
        full = lax.all_gather(packed, "fsdp", axis=2, tiled=True)
        gain_full = lax.all_gather(gains.astype(bf16), "fsdp", axis=1, tiled=True).astype(f32)
        inputs += [("w", vmem, full), ("gain", vmem, gain_full)]
        outputs += [
            ("g_out", hbm, jax.ShapeDtypeStruct((chunks, 2, width, half_width), bf16)),
            ("gain_out", vmem, jax.ShapeDtypeStruct((8, width), f32)),
        ]
        scratch += [
            ("g", pltpu.VMEM((2, 2, width, half_width), bf16)),
            ("g_sem", pltpu.SemaphoreType.DMA((2,))),
        ]
        params = pltpu.CompilerParams(vmem_limit_bytes=63 * 2**20)
    names = [entry[0] for entry in inputs + outputs + scratch]
    block_out, input_grad, part, gain_part = pl.pallas_call(
        functools.partial(block_kernel, linked, names),
        out_shape=[entry[2] for entry in outputs],
        in_specs=[entry[1] for entry in inputs],
        out_specs=[entry[1] for entry in outputs],
        scratch_shapes=[entry[1] for entry in scratch],
        compiler_params=params,
        name="block",
    )(*[entry[2] for entry in inputs])

    if not linked:
        part = lax.psum_scatter(part, "fsdp", scatter_dimension=2, tiled=True)
        part = lax.psum(part, "rep").astype(f32)
        part = jnp.concatenate([part[mlp_chunks + 1 :], part[mlp_chunks:][:1], part[:mlp_chunks]])
        gain_part = lax.psum_scatter(gain_part[:2], "fsdp", scatter_dimension=1, tiled=True)
        gain_part = lax.psum(gain_part, "rep")

    total_tokens = row_count * lax.axis_size("fsdp") * lax.axis_size("rep")
    rate = PEAK_RATE * STEP / (WARMUP * math.sqrt(total_tokens))

    sources = {
        "w": (attn_weights, mlp_weights, gains),
        "m": (moment_attn, moment_mlp, moment_gains),
        "e": (ema_attn, ema_mlp, ema_gains),
    }
    kinds = ["attn", "mlp", "gains"]
    whats = ["grad", "next", "velocity", "average", "copy"]
    inputs = [("out_in", hbm, block_out), ("grad_in", hbm, input_grad), ("g", hbm, part)]
    inputs += [("gain_part", vmem, gain_part)]
    outputs = [("block_out", hbm, block_out), ("input_grad", hbm, input_grad)]
    scratch = []
    for what, arrays in sources.items():
        for kind, array in zip(kinds, arrays, strict=True):
            inputs.append((f"{kind}_{what}", vmem if kind == "gains" else hbm, array))
            if kind != "gains":
                scratch.append((f"{kind}_{what}_here", pltpu.VMEM(array.shape, f32)))
    for what in whats:
        for kind, array in zip(kinds, sources["w"], strict=True):
            dtype = bf16 if what == "copy" else f32
            place = vmem if kind == "gains" else hbm
            outputs.append(
                (f"{kind}_{what}", place, jax.ShapeDtypeStruct(array.shape, dtype))
            )
            if kind != "gains":
                scratch.append((f"{kind}_{what}_here", pltpu.VMEM(array.shape, dtype)))
    scratch += [
        ("g_here", pltpu.VMEM(part.shape, f32)),
        ("in_sem", pltpu.SemaphoreType.DMA((4, 3))),
        ("out_sem", pltpu.SemaphoreType.DMA((4, 5))),
        ("pass_here", pltpu.VMEM((2,) + block_out.shape, bf16)),
        ("pass_sem", pltpu.SemaphoreType.DMA((6,))),
    ]
    names = [entry[0] for entry in inputs + outputs + scratch]
    return pl.pallas_call(
        functools.partial(update_kernel, rate, names),
        out_shape=[jax.ShapeDtypeStruct(entry[2].shape, entry[2].dtype) for entry in outputs],
        in_specs=[entry[1] for entry in inputs],
        out_specs=[entry[1] for entry in outputs],
        scratch_shapes=[entry[1] for entry in scratch],
        compiler_params=pltpu.CompilerParams(vmem_limit_bytes=63 * 2**20),
        name="update",
    )(*[entry[2] for entry in inputs])


def solution(mesh):
    rows = P(("fsdp", "rep"), None)
    shard = P("fsdp", None)
    columns = P(None, "fsdp")
    kinds = (shard, shard, columns)
    return jax.shard_map(
        local,
        mesh=mesh,
        in_specs=(rows, P(("fsdp", "rep")), rows) + kinds * 3,
        out_specs=(rows, rows) + kinds * 5,
        check_vma=False,
    )
```

```python
import functools
import math

import jax
import jax.numpy as jnp
import numpy as np
from jax import lax
from jax.experimental import pallas as pl
from jax.experimental.pallas import tpu as pltpu
from jax.sharding import PartitionSpec as P

HEAD = 64
VMEM_BYTES = 67_000_000
STEP = 5
WARMUP = 10
EPSILON = 1e-05
MASKED = -1e30
MOMENTUM = 0.5
DECAY = 0.5
PEAK_RATE = 0.1
LANES = 128
BLOCK = 256
PLAN = {
    ("pre", 1): [
        ("F", (1,)),
    ],
    ("pre", 0): [
        ("F", (2,)),
        ("S", (1,)),
        ("F", (3,)),
    ],
    ("fwd", 0): [
        ("S", (2, 3, 5)),
        ("R", (0, 1, -1)),
        ("F", (4, -1, 7)),
        ("f", (-1, -1, 8)),
        ("f", (-1, -1, 9)),
        ("f", (-1, -1, 10)),
        ("R", (-1, -1, 2)),
    ],
    ("fwd", 1): [
        ("F", (-1, 6, -1)),
    ],
    ("fwd", 2): [
        ("T", (1, 2, 3)),
        ("F", (5, -1, -1)),
        ("S", (-1, 4, -1)),
    ],
    ("wo", 0): [
        ("S", (6,)),
        ("f", (11,)),
        ("R", (3,)),
    ],
    ("wo", 1): [
    ],
    ("mlp", 0): [
        ("s", (-1, -1, 9, -1, -1, -1, -1, -1)),
        ("T", (4, -1, 7, 8, -1, -1, -1, -1)),
        ("R", (4, 5, 6, -1, -1, -1, -1, -1)),
        ("s", (-1, 8, -1, -1, -1, -1, -1, -1)),
        ("Q", (-1, -1, -1, -1, -1, -1, 0, -1)),
        ("H", (-1, -1, -1, 1, 2, -1, 4, -1)),
        ("L", (-1, -1, -1, -1, -1, -1, -1, 0)),
        ("A", (-1, 0, 1, 2, 3, 4, 5, 6)),
        ("B", (-1, -1, -1, -1, -1, -1, 2, -1)),
        ("R", (-1, -1, -1, -1, -1, 10, 11, -1)),
    ],
    ("mlp", 1): [
        ("T", (5, 6, -1, 9, 10, 11, -1, -1)),
        ("S", (7, -1, -1, -1, -1, -1, -1, -1)),
        ("Q", (-1, -1, -1, -1, -1, -1, 1, -1)),
        ("H", (-1, 0, -1, -1, 3, -1, 5, -1)),
        ("s", (-1, -1, 10, 11, -1, -1, -1, -1)),
        ("B", (-1, -1, -1, 0, -1, -1, 3, -1)),
        ("B", (-1, -1, -1, 1, -1, -1, -1, -1)),
        ("R", (-1, -1, 7, 8, 9, -1, -1, -1)),
    ],
    ("d", 0): [
        ("Q", (2,)),
        ("H", (6,)),
        ("A", (7,)),
        ("B", (4,)),
    ],
    ("o", 0): [
        ("L", (1,)),
    ],
    ("o", 1): [
        ("Q", (3,)),
        ("H", (7,)),
        ("A", (8,)),
        ("B", (5,)),
    ],
    ("bwd", 0): [
        ("E", (0, -1, -1)),
        ("L", (2, -1, -1)),
    ],
    ("bwd", 1): [
        ("E", (-1, -1, 4)),
        ("L", (-1, 4, 6)),
        ("H", (-1, 9, 10)),
    ],
    ("bwd", 2): [
        ("Q", (4, 6, 8)),
        ("H", (8, -1, -1)),
        ("B", (6, -1, 10)),
    ],
    ("bwd", 3): [
        ("E", (1, 3, 5)),
        ("L", (3, 5, 7)),
        ("B", (-1, 8, -1)),
    ],
    ("bwd", 4): [
    ],
    ("bwd", 5): [
        ("E", (2, -1, -1)),
        ("Q", (5, 7, 9)),
        ("A", (9, 10, 11)),
        ("B", (7, 9, -1)),
    ],
    ("tail", 0): [
    ],
    ("tail", 1): [
        ("E", (6,)),
        ("L", (8,)),
        ("H", (11,)),
        ("B", (11,)),
    ],
    ("tail", 2): [
        ("Q", (10,)),
    ],
    ("tail", 3): [
        ("E", (7,)),
        ("L", (9,)),
    ],
    ("end", 0): [
        ("Q", (11,)),
        ("E", (8,)),
        ("L", (10,)),
        ("E", (9,)),
        ("L", (11,)),
        ("E", (10,)),
        ("E", (11,)),
    ],
}
HELD = 4
LATE = 8

f32 = jnp.float32
bf16 = jnp.bfloat16


def nn(left, right):
    return jnp.dot(left, right, preferred_element_type=f32)


def nt(left, right):
    return lax.dot_general(
        left, right, (((1,), (1,)), ((), ())), preferred_element_type=f32
    )


def in_turn(items, stages, breaks=None):
    values = {}
    for turn in range(len(items) + len(stages) - 1):
        if breaks and turn in breaks:
            breaks[turn]()
        for number, stage in enumerate(stages):
            index = turn - number
            if 0 <= index < len(items):
                values[index] = stage(items[index], *values.get(index, ()))


def rotary_tables(row_count):
    half = HEAD // 2
    frequency = np.float32(10000.0) ** (-np.arange(half, dtype=np.float32) / np.float32(half))
    angles = np.arange(row_count, dtype=np.float32)[None, :] * frequency.astype(np.float32)[:, None]
    angles = angles.astype(np.float64)
    tables = np.stack([np.cos(angles), np.sin(angles)]).astype(np.float32)
    tables = tables.reshape(2, half, row_count // BLOCK, BLOCK).transpose(0, 2, 1, 3)
    return np.ascontiguousarray(tables.reshape(-1, BLOCK))


def rotate_rows(rows, cosine, sine):
    half = HEAD // 2
    first, second = rows[:half], rows[half:]
    return jnp.concatenate(
        [first * cosine - second * sine, second * cosine + first * sine], axis=0
    )


def rms_scale(rows):
    return lax.rsqrt(jnp.mean(rows * rows, axis=-1, keepdims=True) + EPSILON)


class Scratch:
    def __init__(self, names, refs):
        for name, ref in zip(names, refs, strict=True):
            setattr(self, name, ref)


def block_kernel(linked, names, *refs):
    s = Scratch(names, refs)
    row_count, width = s.x.shape
    blocks = row_count // BLOCK
    pairs = width // LANES
    thirds = pairs // 2
    half_width = width // 2
    chunks = s.w.shape[0]
    mlp_chunks = chunks - thirds - 1
    slots = s.g.shape[0]

    def rows_of(i):
        return pl.ds(i * BLOCK, BLOCK)

    def store_pairs(i, value):
        for p in range(pairs):
            s.n2[p, rows_of(i), :] = value[:, p * LANES : (p + 1) * LANES]

    def load_pairs(i):
        return jnp.concatenate([s.n2[p, rows_of(i), :] for p in range(pairs)], axis=1)

    def sums_at(kind, first, count, j):
        return (pl.ds(j * LANES + first, count), pl.ds(kind * BLOCK, BLOCK))

    places = [[0, 1, 2, 3], [0, 2, 1, 3]]

    def load_w(chunk, half):
        if not linked:
            return s.w[chunk, half]
        if half == 0:
            return s.w[chunk, 0].reshape(width, half_width)
        parts = [s.w[chunk, 1, z, place] for z in range(s.w.shape[2]) for place in places[1]]
        return jnp.concatenate(parts, axis=0)

    def store_g(chunk, half, lanes, value):
        low = value.astype(bf16)
        if linked and half == 0:
            low = low.reshape(s.g.shape[2:5] + (low.shape[1],))
            s.g[chunk % slots, 0, :, :, :, lanes] = low
        elif linked:
            low = low.reshape((-1,) + s.g.shape[4:5] + (low.shape[1],))
            for z in range(s.g.shape[2]):
                for index, place in enumerate(places[1]):
                    s.g[chunk % slots, 1, z, place, :, lanes] = low[4 * z + index]
        else:
            s.g[chunk % slots, half, :, lanes] = low

    if linked:
        gather_start, actions, gain_steps = links(s, chunks, thirds, mlp_chunks)
    else:


        def grad_copy(chunk):
            slot = chunk % slots
            return pltpu.make_async_copy(s.g.at[slot], s.g_out.at[chunk], s.g_sem.at[slot])

        actions = {"A": lambda chunk: grad_copy(chunk).start()}
        actions["H"] = lambda chunk: grad_copy(chunk).wait()

    def events(loop, place, index=0):
        for kind, table in PLAN[loop, place]:
            if kind not in actions:
                continue
            if isinstance(index, int):
                if table[index] >= 0:
                    actions[kind](table[index])
                continue
            used = [i for i, entry in enumerate(table) if entry >= 0]
            shift = table[used[0]] - used[0]
            in_line = all(table[i] == i + shift for i in used)
            in_line = in_line and used == list(range(used[0], used[-1] + 1))
            if in_line:
                chunk = index + shift
            else:
                chunk = jnp.int32(table[used[0]])
                for i in used[1:]:
                    chunk = jnp.where(index == i, table[i], chunk)
            if len(used) == len(table):
                actions[kind](chunk)
                continue
            if in_line:
                now = (index >= used[0]) & (index <= used[-1])
            else:
                now = functools.reduce(lambda u, v: u | v, [index == i for i in used])
            pl.when(now)(functools.partial(actions[kind], chunk))

    copies = [
        pltpu.make_async_copy(s.x_in, s.x, s.local_sem.at[0]),
        pltpu.make_async_copy(s.cot_in, s.cot, s.local_sem.at[1]),
    ]
    tables = s.total.at[pl.ds(0, HEAD * blocks), pl.ds(0, BLOCK)]
    copies.append(pltpu.make_async_copy(s.tables, tables, s.local_sem.at[2]))
    copies.append(pltpu.make_async_copy(s.doc_in, s.doc, s.local_sem.at[3]))
    if linked:
        gather_start[0]()
    for copy in copies:
        copy.start()

    copies.pop().wait()
    docs = [s.doc[BLOCK * j] for j in range(blocks)]
    bias = [
        [jnp.where(docs[i] == docs[j], 0.0, MASKED).astype(f32) for j in range(i)] + [0.0]
        for i in range(blocks)
    ]
    causal = lax.broadcasted_iota(jnp.int32, (BLOCK, BLOCK), 0) <= lax.broadcasted_iota(
        jnp.int32, (BLOCK, BLOCK), 1
    )

    copies.pop().wait()
    for i in range(blocks):
        place = sum([(docs[j] == docs[i]).astype(jnp.int32) for j in range(i)], jnp.int32(0))
        for index, table in enumerate([s.cost, s.sint]):
            chosen = None
            for t in range(i + 1):
                first = (index * blocks + t) * (HEAD // 2)
                part = s.total[pl.ds(first, HEAD // 2), pl.ds(0, BLOCK)]
                chosen = part if t == 0 else jnp.where(place == t, part, chosen)
            table[:, rows_of(i)] = chosen
    if linked:
        gather_start[1]()
        events("pre", 1)
    for copy in copies:
        copy.wait()
    if linked:
        gather_start[2]()
        events("pre", 0)
    if linked:
        gather_start[3]()
    gain_one = s.gain[0:1, :]
    gain_two = s.gain[1:2, :]
    for i in range(blocks):
        stream = s.x[rows_of(i), :].astype(f32)
        normed = (stream * rms_scale(stream) * gain_one).astype(bf16)
        s.n1t[:, rows_of(i)] = normed.T
        s.dn[rows_of(i), :] = jnp.zeros((BLOCK, width), f32)

    def masked_pair(rows, h):
        zero = jnp.zeros((HEAD, BLOCK), bf16)
        parts = [rows[:HEAD], zero] if h == 0 else [zero, rows[HEAD:]]
        return jnp.concatenate(parts, axis=0)

    def scores_of(p, i, h):
        span = (i + 1) * BLOCK
        query = masked_pair(s.qt[p, :, rows_of(i)], h)
        scores = nn(s.k[p, pl.ds(0, span), :], query)
        parts = [scores[j * BLOCK : (j + 1) * BLOCK] for j in range(i + 1)]
        parts[i] = jnp.where(causal, parts[i], MASKED)
        return parts

    bodies = [(q, i, h) for q in range(2) for i in range(blocks) for h in range(2)]
    half_way = 2 * blocks

    def lse_at(p, i, h):
        return (p // 2, pl.ds(2 * (p % 2) + h, 1), rows_of(i))

    def project(third, q):
        p = 2 * third + q
        weights_t = load_w(third, q).T
        for i in range(blocks):
            cosine, sine = s.cost[:, rows_of(i)], s.sint[:, rows_of(i)]
            projected = nn(weights_t, s.n1t[:, rows_of(i)])
            for h in range(2):
                lo, hi = h * HEAD, (h + 1) * HEAD
                query = rotate_rows(projected[lo:hi], cosine, sine).astype(bf16)
                s.qt[p, lo:hi, rows_of(i)] = query * bf16(0.125)
                key = rotate_rows(projected[LANES + lo : LANES + hi], cosine, sine)
                s.kt[p, lo:hi, rows_of(i)] = key.astype(bf16)
            s.vt[p, :, rows_of(i)] = projected[2 * LANES :].astype(bf16)
            s.k[p, rows_of(i), :] = s.kt[p, :, rows_of(i)].T
            s.v[p, rows_of(i), :] = s.vt[p, :, rows_of(i)].T

    def attention_forward(third, carry):
        events("fwd", 0, third)
        project(third, 0)
        project(third, 1)
        events("fwd", 1, third)

        def scores(n):
            q, i, h = n
            return (scores_of(2 * third + q, i, h),)

        def shares(n, parts):
            q, i, h = n
            p = 2 * third + q
            tops = [
                jnp.max(part, axis=0, keepdims=True) + bias[i][j]
                for j, part in enumerate(parts)
            ]
            top = functools.reduce(jnp.maximum, tops)
            exps = [jnp.exp(part - (top - bias[i][j])) for j, part in enumerate(parts)]
            total = sum([jnp.sum(e, axis=0, keepdims=True) for e in exps])
            s.lse[lse_at(p, i, h)] = top + jnp.log(total)
            return jnp.concatenate([e.astype(bf16) for e in exps], axis=0), 1.0 / total

        def mix(n, exps_low, inverse):
            q, i, h = n
            p = 2 * third + q
            heads = pl.ds(h * HEAD, HEAD)
            mixed = nn(s.vt[p, heads, pl.ds(0, (i + 1) * BLOCK)], exps_low)
            s.mixt[p, heads, rows_of(i)] = (mixed * inverse).astype(bf16)

        in_turn(
            bodies,
            [scores, shares, mix],
            {half_way: lambda: events("fwd", 2, third)},
        )
        return carry

    lax.fori_loop(0, thirds, attention_forward, 0)

    out_chunk = thirds
    for i in range(blocks):
        if i % 2 == 0:
            events("wo", i // 2)
        mixed = s.mixt[:, :, rows_of(i)].reshape(width, BLOCK).T
        branch = jnp.concatenate(
            [nn(mixed, load_w(out_chunk, half)) for half in range(2)], axis=1
        )
        after = s.x[rows_of(i), :].astype(f32) + branch
        s.y[rows_of(i), :] = after
        s.total[rows_of(i), :] = after
        normed = (after * rms_scale(after) * gain_two).astype(bf16)
        store_pairs(i, normed)
        s.n2t[:, :, rows_of(i)] = normed.T.reshape(pairs, LANES, BLOCK)

    tiles = [pl.ds(t * BLOCK, BLOCK) for t in range(width // BLOCK)]
    for i in range(blocks):
        for tile in tiles:
            s.x[rows_of(i), tile] = s.cot[rows_of(i), tile].T

    def feed_forward(chunk, carry):
        events("mlp", 0, chunk)
        low = [load_w(thirds + 1 + chunk, half) for half in range(2)]
        w_gu = [w[:, : 2 * LANES] for w in low]
        w_gu_all = jnp.concatenate(w_gu, axis=1)
        w_down = jnp.concatenate([w[:, 2 * LANES :] for w in low], axis=1)

        def products(i):
            normed = load_pairs(i)
            d_hidden = nn(s.cot[rows_of(i), :], w_down)
            return d_hidden, [nn(normed, w) for w in w_gu]

        def slopes(i, d_hidden, gate_ups):
            for half, gate_up in enumerate(gate_ups):
                gate, up = gate_up[:, :LANES], gate_up[:, LANES:]
                back = d_hidden[:, half * LANES : (half + 1) * LANES]
                sig = jax.nn.sigmoid(gate)
                silu = gate * sig
                s.hid[rows_of(i), pl.ds(half * LANES, LANES)] = (silu * up).astype(bf16)
                s.dgu[rows_of(i), pl.ds(2 * half * LANES, LANES)] = (
                    back * up * (sig + silu * (1.0 - sig))
                ).astype(bf16)
                s.dgu[rows_of(i), pl.ds((2 * half + 1) * LANES, LANES)] = (
                    back * silu
                ).astype(bf16)
            return ()

        def sums(i):
            s.total[rows_of(i), :] += nt(s.hid[rows_of(i), :], w_down)
            s.dn[rows_of(i), :] += nt(s.dgu[rows_of(i), :], w_gu_all)

        in_turn(list(range(blocks)), [products, slopes, sums])
        events("mlp", 1, chunk)
        n2t = s.n2t[...].reshape(width, row_count)
        for half in range(2):
            store_g(
                chunk,
                half,
                pl.ds(0, 2 * LANES),
                nn(n2t, s.dgu[:, pl.ds(2 * half * LANES, 2 * LANES)]),
            )
        grad_down = jnp.concatenate(
            [
                nn(
                    jnp.concatenate([s.x[rows_of(i), tile] for i in range(blocks)], axis=1),
                    s.hid[...],
                )
                for tile in tiles
            ],
            axis=0,
        )
        for half in range(2):
            store_g(
                chunk,
                half,
                pl.ds(2 * LANES, LANES),
                grad_down[:, half * LANES : (half + 1) * LANES],
            )
        return carry

    lax.fori_loop(0, mlp_chunks, feed_forward, 0)

    events("d", 0)
    x_copy = pltpu.make_async_copy(s.x_in, s.x, s.local_sem.at[1])
    x_copy.start()

    gain_grad_two = jnp.zeros((1, width), f32)
    for i in range(blocks):
        after = s.y[rows_of(i), :]
        scale = rms_scale(after)
        unit = after * scale
        d_normed = s.dn[rows_of(i), :]
        d_unit = d_normed * gain_two
        gain_grad_two += jnp.sum(d_normed * unit, axis=0, keepdims=True)
        grad_after = s.cot[rows_of(i), :].astype(f32) + scale * (
            d_unit - unit * jnp.mean(d_unit * unit, axis=-1, keepdims=True)
        )
        s.y[rows_of(i), :] = grad_after
        store_pairs(i, grad_after.astype(bf16))
        s.cot[rows_of(i), :] = s.total[rows_of(i), :].astype(bf16)
    out_copy = pltpu.make_async_copy(s.cot, s.block_out, s.local_sem.at[0])
    out_copy.start()

    events("o", 0)
    mixt = s.mixt[...].reshape(width, row_count)
    for half in range(2):
        store_g(
            mlp_chunks,
            half,
            pl.ds(0, half_width),
            nn(mixt, jnp.concatenate([s.n2[p] for p in range(half * thirds, (half + 1) * thirds)], axis=1)),
        )
    events("o", 1)
    dmt = s.n2t
    w_out = jnp.concatenate([load_w(out_chunk, half) for half in range(2)], axis=1)
    for i in range(blocks):
        d_mixed = nt(w_out, load_pairs(i))
        dmt[:, :, rows_of(i)] = d_mixed.astype(bf16).reshape(pairs, LANES, BLOCK)

    def turn_back(p, q, i):
        cosine, sine = s.cost[:, rows_of(i)], -s.sint[:, rows_of(i)]
        pieces = []
        for kind in range(2):
            for h in range(2):
                piece = s.total[sums_at(kind, h * HEAD, HEAD, q * blocks + i)]
                piece = rotate_rows(piece, cosine, sine)
                pieces.append((piece * 0.125 if kind == 0 else piece).astype(bf16))
        s.k[p, rows_of(i), :] = jnp.concatenate(pieces[:2], axis=0).T
        s.v[p, rows_of(i), :] = jnp.concatenate(pieces[2:], axis=0).T
        s.n2[p, rows_of(i), :] = s.total[sums_at(2, 0, LANES, q * blocks + i)].astype(bf16).T

    def attention_backward(third, carry):
        events("bwd", 0, third)
        for j in range(2 * blocks):
            for kind in (1, 2):
                s.total[sums_at(kind, 0, LANES, j)] = jnp.zeros((LANES, BLOCK), f32)

        def begin(n):
            q, i, h = n
            p = 2 * third + q
            back = masked_pair(dmt[p, :, rows_of(i)], h)
            return scores_of(p, i, h), nn(s.v[p, pl.ds(0, (i + 1) * BLOCK), :], back)

        def middle(n, parts, d_probs):
            q, i, h = n
            lse = s.lse[lse_at(2 * third + q, i, h)]
            probs = [jnp.exp(part - (lse - bias[i][j])) for j, part in enumerate(parts)]
            probs = jnp.concatenate(probs, axis=0)
            weighted = probs * d_probs
            inner = jnp.sum(weighted, axis=0, keepdims=True)
            return (weighted - probs * inner).astype(bf16), probs.astype(bf16)

        def finish(n, d_scores, probs_low):
            q, i, h = n
            p = 2 * third + q
            heads, keys = pl.ds(h * HEAD, HEAD), pl.ds(0, (i + 1) * BLOCK)
            s.total[sums_at(0, h * HEAD, HEAD, q * blocks + i)] = nn(
                s.kt[p, heads, keys], d_scores
            )
            d_keys = nt(s.qt[p, heads, rows_of(i)], d_scores)
            d_values = nt(dmt[p, heads, rows_of(i)], probs_low)
            for j in range(i + 1):
                span = slice(j * BLOCK, (j + 1) * BLOCK)
                s.total[sums_at(1, h * HEAD, HEAD, q * blocks + j)] += d_keys[:, span]
                s.total[sums_at(2, h * HEAD, HEAD, q * blocks + j)] += d_values[:, span]
            number = bodies.index(n) - half_way
            if 0 <= number < blocks:
                turn_back(2 * third, 0, number)

        in_turn(
            bodies,
            [begin, middle, finish],
            {
                half_way // 2 + 2: lambda: events("bwd", 1, third),
                half_way + 2: lambda: events("bwd", 2, third),
                half_way + half_way // 2 + 2: lambda: events("bwd", 3, third),
            },
        )
        events("bwd", 4, third)
        for i in range(blocks):
            turn_back(2 * third + 1, 1, i)
        for q in range(2):
            p = 2 * third + q
            d_qkv = jnp.concatenate([s.k[p], s.v[p], s.n2[p]], axis=1)
            store_g(
                mlp_chunks + 1 + third, q, pl.ds(0, half_width), nn(s.n1t[...], d_qkv)
            )
        events("bwd", 5, third)
        return carry

    lax.fori_loop(0, thirds, attention_backward, 0)

    x_copy.wait()
    w_qkv_t = jnp.concatenate([load_w(p // 2, p % 2).T for p in range(pairs)], axis=0)
    gain_grad_one = jnp.zeros((1, width), f32)
    for i in range(blocks):
        events("tail", i)
        d_qkv = [
            ref[p, rows_of(i), :] for p in range(pairs) for ref in (s.k, s.v, s.n2)
        ]
        d_normed = nn(jnp.concatenate(d_qkv, axis=1), w_qkv_t)
        stream = s.x[rows_of(i), :].astype(f32)
        scale = rms_scale(stream)
        unit = stream * scale
        d_unit = d_normed * gain_one
        gain_grad_one += jnp.sum(d_normed * unit, axis=0, keepdims=True)
        s.x[rows_of(i), :] = (
            s.y[rows_of(i), :]
            + scale * (d_unit - unit * jnp.mean(d_unit * unit, axis=-1, keepdims=True))
        ).astype(bf16)
    grad_copy_out = pltpu.make_async_copy(s.x, s.input_grad, s.local_sem.at[1])
    grad_copy_out.start()
    gain_grads = jnp.concatenate(
        [gain_grad_one, gain_grad_two, jnp.zeros((6, width), f32)], axis=0
    )
    if linked:
        gain_steps[0](gain_grads)
        left = list(gain_steps[1:4])
        for kind, table in PLAN["end", 0]:
            actions[kind](table[0])
            if table[0] == chunks - 1 and kind in "QLE" and left:
                left.pop(0)()
        for step in left:
            step()
        gain_steps[4]()
    else:
        events("end", 0)
        s.gain_out[...] = gain_grads
    out_copy.wait()
    grad_copy_out.wait()


def links(s, chunks, thirds, mlp_chunks):
    planes = s.w.shape[2]
    me = lax.axis_index("fsdp")
    core = lax.axis_index("rep")
    z, m = me // 4, me % 4
    over_x, over_y, over_both = m + 1 - 2 * (m % 2), (m + 2) % 4, 3 - m
    m1 = (1 - core) * over_x + core * over_y
    m2 = (1 - core) * over_y + core * over_x
    other = 1 - core
    low = (1 - core) * (m % 2) + core * (m // 2)
    high = (1 - core) * (m // 2) + core * (m % 2)
    place = 2 * high + low

    def chip(plane, place):
        return (plane * 4 + place, core)

    sibling = (me, other)

    def far(k):
        return (z + k) % planes

    peers = [chip(far(k), m) for k in range(1, planes)]
    first, second = chip(z, m1), chip(z, m2)

    def remote(src, dst, send_sem, recv_sem, device):
        return pltpu.make_async_remote_copy(
            src_ref=src,
            dst_ref=dst,
            send_sem=send_sem,
            recv_sem=recv_sem,
            device_id=device,
            device_id_type=pl.DeviceIdType.MESH,
        )

    def along_z(chunk, k):
        block = s.w.at[chunk, core, z, place]
        return remote(block, block, s.sent_sem.at[0], s.hop_sem.at[chunk, 0], peers[k])

    def along_z_here(chunk):
        blocks = s.w.at[chunk, core, pl.ds(0, planes - 1), place]
        return remote(blocks, blocks, s.sent_sem.at[0], s.hop_sem.at[chunk, 0], peers[0])

    def hop(chunk, index):
        if index == 1:
            blocks, device = s.w.at[chunk, core, :, place], first
        elif index == 2:
            blocks, device = s.w.at[chunk, core, :, pl.ds(2 * high, 2)], second
        else:
            blocks, device = s.w.at[chunk, core], sibling
        return remote(blocks, blocks, s.sent_sem.at[index], s.hop_sem.at[chunk, index], device)

    def alone(chunk):
        block = s.w.at[chunk, core, z, place]
        return remote(block, block, s.sent_sem.at[5], s.hop_sem.at[chunk, 1], first)

    def along_z_again(chunk, k):
        block = s.w.at[chunk, core, z, place + 1 - 2 * low]
        return remote(block, block, s.sent_sem.at[4], s.hop_sem.at[chunk, 4], peers[k])

    def along_z_again_here(chunk):
        blocks = s.w.at[chunk, core, pl.ds(0, planes - 1), place]
        return remote(blocks, blocks, s.sent_sem.at[4], s.hop_sem.at[chunk, 4], peers[0])

    def gather_end():
        late = pl.ds(LATE, chunks - LATE)
        blocks = s.w.at[late, core, pl.ds(0, planes - 1), place]
        remote(blocks, blocks, s.sent_sem.at[4], s.hop_sem.at[0, 4], peers[0]).wait_send()
        blocks = s.w.at[late, core, z, place]
        remote(blocks, blocks, s.sent_sem.at[5], s.hop_sem.at[0, 1], first).wait_send()
        blocks = s.w.at[:, core, pl.ds(0, planes - 1), place]
        remote(blocks, blocks, s.sent_sem.at[0], s.hop_sem.at[0, 0], peers[0]).wait_send()
        blocks = s.w.at[pl.ds(0, LATE), core, :, place]
        remote(blocks, blocks, s.sent_sem.at[1], s.hop_sem.at[0, 1], first).wait_send()
        blocks = s.w.at[:, core, :, pl.ds(2 * high, 2)]
        remote(blocks, blocks, s.sent_sem.at[2], s.hop_sem.at[0, 2], second).wait_send()
        blocks = s.w.at[:, core]
        remote(blocks, blocks, s.sent_sem.at[3], s.hop_sem.at[0, 3], sibling).wait_send()

    def gain_along_z(k):
        block = s.gt.at[z, m]
        return remote(block, block, s.gain_sem.at[0, k], s.gain_sem.at[1, k], peers[k])

    def gain_hop(index):
        blocks = s.gt.at[:, [m, m, m1][index]]
        device = [first, second, second][index]
        k = planes - 1 + index
        return remote(blocks, blocks, s.gain_sem.at[0, k], s.gain_sem.at[1, k], device)

    width = s.x.shape[1]
    pairs = width // LANES
    shard_rows = s.w.shape[4]
    half_width = s.w.shape[5]
    hidden = s.mlp_in.shape[1] // 3
    loads = [
        functools.partial(
            pltpu.make_async_copy,
            s.attn_in.at[:, pl.ds(k * width, width)],
            s.dn.at[pl.ds(k * shard_rows, shard_rows)],
            s.load_sem.at[k],
        )
        for k in range(4)
    ] + [
        functools.partial(
            pltpu.make_async_copy,
            s.mlp_in.at[:, pl.ds(k * width, width)],
            s.dn.at[pl.ds((4 + k) * shard_rows, shard_rows)],
            s.load_sem.at[4 + k],
        )
        for k in range(3 * hidden // width)
    ]

    def piece(row, lane):
        rows = s.dn[pl.ds(row * shard_rows, shard_rows), pl.ds(lane, LANES)]
        return rows.astype(bf16)

    def round_third(third):
        lane = pl.multiple_of((2 * third + core) * LANES, LANES)
        for kind in range(3):
            s.w[third, core, z, place, :, kind * LANES : (kind + 1) * LANES] = piece(kind, lane)

    def gather_start():
        barrier = pltpu.get_barrier_semaphore()
        partners = [chip(z, over_x), chip(z, over_y), chip(z, over_both), sibling] + peers
        for partner in partners:
            pl.semaphore_signal(
                barrier, inc=1, device_id=partner, device_id_type=pl.DeviceIdType.MESH
            )
        for load in loads:
            load().start()
        gains_copy = pltpu.make_async_copy(s.gains_hbm, s.gains_in, s.gains_sem.at[0])
        gains_copy.start()
        gains_copy.wait()
        own = s.gains_in[...].astype(bf16)
        own = jnp.concatenate([own, jnp.zeros((2, LANES - shard_rows), bf16)], axis=1)
        s.gt[z, m] = jnp.concatenate([own, jnp.zeros((14, LANES), bf16)], axis=0)
        for load in loads[:3]:
            load().wait()
        round_third(0)
        pl.semaphore_wait(barrier, len(partners))
        for k in range(planes - 1):
            along_z(0, k).start()
        for k in range(planes - 1):
            gain_along_z(k).start()
        loads[3]().wait()
        for third in range(1, thirds):
            round_third(third)
        lane = pl.multiple_of(core * half_width, LANES)
        s.w[thirds, core, z, place] = s.dn[
            pl.ds(3 * shard_rows, shard_rows), pl.ds(lane, half_width)
        ].astype(bf16)
        for chunk in range(1, thirds + 1):
            for k in range(planes - 1):
                along_z(chunk, k).start()

    def gather_feed_forward():
        for load in loads[4:]:
            load().wait()
        for j in range(mlp_chunks):
            for kind in range(3):
                column = kind * hidden + 2 * j * LANES
                row, begin = 4 + column // width, column % width
                lane = pl.multiple_of(begin + core * LANES, LANES)
                s.w[thirds + 1 + j, core, z, place, :, kind * LANES : (kind + 1) * LANES] = (
                    piece(row, lane)
                )
            for k in range(planes - 1):
                along_z(thirds + 1 + j, k).start()
            if thirds + 1 + j >= LATE:
                alone(thirds + 1 + j).start()

    def gather_one():
        first_hop(0)
        for k in range(planes - 1):
            gain_along_z(k).wait()
        gain_hop(0).start()
        gain_hop(1).start()
        gather_feed_forward()

    def gather_two():
        second_hop(0)
        gain_hop(0).wait()
        gain_hop(2).start()

    def gather_three():
        gain_hop(1).wait()
        gain_hop(2).wait()
        rows = jnp.zeros((8, width), f32)
        for d in range(planes * 4):
            tile = s.gt[d // 4, d % 4].astype(f32)[:8]
            wide = jnp.concatenate([tile, jnp.zeros((8, width - LANES), f32)], axis=1)
            rows += pltpu.roll(wide, d * shard_rows, 1) if d else wide
        s.gain[...] = rows
        third_hop(0)

    def first_hop(chunk):
        along_z_here(chunk).wait_recv()
        hop(chunk, 1).start()

    def first_hop_late(chunk):
        alone(chunk).wait_recv()
        for k in range(planes - 1):
            along_z_again(chunk, k).start()

    def second_hop_late(chunk):
        along_z_here(chunk).wait_recv()
        along_z_again_here(chunk).wait_recv()
        hop(chunk, 2).start()

    def second_hop(chunk):
        hop(chunk, 1).wait_recv()
        hop(chunk, 2).start()

    def third_hop(chunk):
        hop(chunk, 2).wait_recv()
        hop(chunk, 3).start()

    def ready(chunk):
        hop(chunk, 3).wait_recv()

    held = s.h.shape[0]

    def to_sibling(chunk):
        return remote(
            s.g.at[chunk % 2, other],
            s.a.at[chunk % 2],
            s.rs_sem.at[chunk, 0, 0],
            s.rs_sem.at[chunk, 0, 1],
            sibling,
        )

    def to_second(chunk):
        return remote(
            s.h.at[chunk % held, :, pl.ds(2 - 2 * high, 2)],
            s.b.at[chunk % 4],
            s.rs_sem.at[chunk, 1, 0],
            s.rs_sem.at[chunk, 1, 1],
            second,
        )

    def to_first(chunk):
        return remote(
            s.cs.at[chunk % 2],
            s.c.at[chunk % 4],
            s.rs_sem.at[chunk, 2, 0],
            s.rs_sem.at[chunk, 2, 1],
            first,
        )

    def to_plane(chunk, k):
        return remote(
            s.ds.at[chunk % 2, far(k + 1)],
            s.d.at[chunk % 4, k],
            s.rs_sem.at[chunk, 3, 0],
            s.rs_sem.at[chunk, 3, 1],
            peers[k],
        )

    def to_planes(chunk):
        return remote(
            s.ds.at[chunk % 2, pl.ds(0, planes - 1)],
            s.d.at[chunk % 4],
            s.rs_sem.at[chunk, 3, 0],
            s.rs_sem.at[chunk, 3, 1],
            peers[0],
        )

    def place_of(chunk):
        return jnp.where(
            chunk < mlp_chunks,
            thirds + 1 + chunk,
            jnp.where(chunk == mlp_chunks, thirds, chunk - mlp_chunks - 1),
        )

    def to_copy(chunk):
        done = s.g_out.at[place_of(chunk), core]
        sems = s.end_sem.at[chunk, 0], s.end_sem.at[0, 2]
        return remote(s.gout.at[chunk % 6], done, *sems, sibling)

    def leave(chunk):
        done = s.g_out.at[place_of(chunk), core]
        return pltpu.make_async_copy(s.gout.at[chunk % 6], done, s.end_sem.at[chunk, 1])

    def left(chunk):
        to_copy(chunk).wait_send()
        leave(chunk).wait()

    def reduce_end():
        done = s.g_out.at[:, core]
        remote(done, done, s.end_sem.at[0, 0], s.end_sem.at[0, 2], sibling).wait_recv()
        for chunk in range(chunks - 6, chunks):
            left(chunk)

    def send_half(chunk):
        to_sibling(chunk).start()

    def add_half(chunk):
        to_sibling(chunk).wait()
        s.h[chunk % held] = (
            s.g[chunk % 2, core].astype(f32) + s.a[chunk % 2].astype(f32)
        ).astype(bf16)

    def halves(chunk):
        to_second(chunk).start()

    def quarters(chunk):
        to_second(chunk).wait()
        even = chunk % 2
        s.cs[even] = (
            s.h[chunk % held, :, 2 * high + 1 - low].astype(f32)
            + s.b[chunk % 4, :, 1 - low].astype(f32)
        ).astype(bf16)
        to_first(chunk).start()
        s.kept[even] = (
            s.h[chunk % held, :, place].astype(f32) + s.b[chunk % 4, :, low].astype(f32)
        ).astype(bf16)

    def lines(chunk):
        to_first(chunk).wait()
        even = chunk % 2
        s.ds[even] = (s.kept[even].astype(f32) + s.c[chunk % 4].astype(f32)).astype(bf16)
        for k in range(planes - 1):
            to_plane(chunk, k).start()
        s.own[even] = s.kept[even, z].astype(f32) + s.c[chunk % 4, z].astype(f32)

    def last(chunk):
        to_planes(chunk).wait()
        total = s.own[chunk % 2]
        for k in range(planes - 1):
            total += s.d[chunk % 4, k].astype(f32)
        if isinstance(chunk, int):
            if chunk >= 6:
                left(chunk - 6)
        else:
            pl.when(chunk >= 6)(lambda: left(chunk - 6))
        s.gout[chunk % 6] = total
        to_copy(chunk).start()
        leave(chunk).start()

    actions = {"F": first_hop, "S": second_hop, "T": third_hop, "R": ready}
    actions.update({"A": send_half, "H": add_half, "B": halves, "Q": quarters})
    actions.update({"L": lines, "E": last, "f": first_hop_late, "s": second_hop_late})

    def plane_sum():
        block = s.gp.at[m]
        return [
            remote(block, block, s.gsum_sem.at[0, k], s.gsum_sem.at[1, k], chip(z, at))
            for k, at in enumerate([over_x, over_y, over_both])
        ]

    def line_sum():
        block = s.gz.at[z]
        return [
            remote(block, block, s.gsum_sem.at[0, 3 + k], s.gsum_sem.at[1, 3 + k], peers[k])
            for k in range(planes - 1)
        ]

    def core_sum():
        k = planes + 2
        sems = s.gsum_sem
        return remote(s.gc.at[0], s.gc.at[1], sems.at[0, k], sems.at[1, k], sibling)

    def gain_begin(value):
        s.gp[m] = value
        for copy in plane_sum():
            copy.start()

    def gain_lines_sum():
        for copy in plane_sum():
            copy.wait()
        s.gz[z] = (s.gp[0] + s.gp[1]) + (s.gp[2] + s.gp[3])
        for copy in line_sum():
            copy.start()

    def gain_cores():
        for copy in line_sum():
            copy.wait()
        total = s.gz[0]
        for k in range(1, planes):
            total += s.gz[k]
        s.gc[0] = total
        core_sum().start()

    def gain_end():
        core_sum().wait()
        total = s.gc[0] + s.gc[1]
        s.gains_end[...] = pltpu.roll(total, (width - me * shard_rows) % width, 1)[:, :LANES]
        pltpu.make_async_copy(s.gains_end, s.gain_out, s.gains_sem.at[1]).start()

    def gain_out():
        gather_end()
        reduce_end()
        pltpu.make_async_copy(s.gains_end, s.gain_out, s.gains_sem.at[1]).wait()

    start = (gather_start, gather_one, gather_two, gather_three)
    return start, actions, (gain_begin, gain_lines_sum, gain_cores, gain_end, gain_out)


def update_kernel(rate, names, *refs):
    s = Scratch(names, refs)
    width = s.attn_w.shape[1] // 4
    hidden = s.mlp_w.shape[1] // 3
    pairs = width // LANES
    thirds = pairs // 2
    half_width = width // 2
    whats = ["grad", "next", "velocity", "average", "copy"]

    def rule(weight, grad, moment, average):
        velocity = MOMENTUM * moment + grad
        weight_new = weight - rate * (grad + MOMENTUM * velocity)
        average_new = DECAY * average + (1.0 - DECAY) * weight_new
        return grad, weight_new, velocity, average_new, weight_new.astype(bf16)

    attn_blocks = [
        (kind * width + pair * LANES, LANES, (pair // 2, pair % 2), kind * LANES)
        for kind in range(3)
        for pair in range(pairs)
    ] + [(3 * width + half * half_width, half_width, (thirds, half), 0) for half in range(2)]
    pieces = [("attn", 0, 4 * width, attn_blocks)] + [
        (
            "mlp",
            kind * hidden,
            hidden,
            [
                (kind * hidden + b * LANES, LANES, (thirds + 1 + b // 2, b % 2), kind * LANES)
                for b in range(hidden // LANES)
            ],
        )
        for kind in range(3)
    ]

    def loads(index):
        kind, first, count, _ = pieces[index]
        span = pl.ds(first, count)
        return [
            pltpu.make_async_copy(
                getattr(s, f"{kind}_{what}").at[:, span],
                getattr(s, f"{kind}_{what}_here").at[:, span],
                s.in_sem.at[index, k],
            )
            for k, what in enumerate(["w", "m", "e"])
        ]

    def stores(index):
        kind, first, count, _ = pieces[index]
        span = pl.ds(first, count)
        return [
            pltpu.make_async_copy(
                getattr(s, f"{kind}_{what}_here").at[:, span],
                getattr(s, f"{kind}_{what}").at[:, span],
                s.out_sem.at[index, k],
            )
            for k, what in enumerate(whats)
        ]

    enter = [
        pltpu.make_async_copy(s.out_in, s.pass_here.at[0], s.pass_sem.at[0]),
        pltpu.make_async_copy(s.grad_in, s.pass_here.at[1], s.pass_sem.at[1]),
    ]
    leave = [
        pltpu.make_async_copy(s.pass_here.at[0], s.block_out, s.pass_sem.at[4]),
        pltpu.make_async_copy(s.pass_here.at[1], s.input_grad, s.pass_sem.at[5]),
    ]
    grads = [
        pltpu.make_async_copy(
            s.g.at[pl.ds(0, thirds + 1)], s.g_here.at[pl.ds(0, thirds + 1)], s.pass_sem.at[2]
        ),
        pltpu.make_async_copy(
            s.g.at[pl.ds(thirds + 1, s.g.shape[0] - thirds - 1)],
            s.g_here.at[pl.ds(thirds + 1, s.g.shape[0] - thirds - 1)],
            s.pass_sem.at[3],
        ),
    ]
    enter[0].start()
    grads[0].start()
    for load in loads(0):
        load.start()
    enter[1].start()
    grads[1].start()
    for index in range(1, len(pieces)):
        for load in loads(index):
            load.start()
    small_in = [
        pltpu.make_async_copy(
            getattr(s, f"gains_{what}"), getattr(s, f"gains_{what}_here"), s.in_sem.at[4, k]
        )
        for k, what in enumerate(["w", "m", "e"])
    ] + [pltpu.make_async_copy(s.gain_part_in, s.gain_part, s.in_sem.at[4, 3])]
    small_out = [
        pltpu.make_async_copy(
            getattr(s, f"gains_{what}_here"), getattr(s, f"gains_{what}"), s.out_sem.at[4, k]
        )
        for k, what in enumerate(whats)
    ]
    for copy in small_in:
        copy.start()
    enter[0].wait()
    leave[0].start()
    for copy in small_in:
        copy.wait()
    shard_rows = s.attn_w.shape[0]
    results = rule(
        s.gains_w_here[...],
        s.gain_part[:2, :shard_rows],
        s.gains_m_here[...],
        s.gains_e_here[...],
    )
    for what, result in zip(whats, results, strict=True):
        getattr(s, f"gains_{what}_here")[...] = result
    for copy in small_out:
        copy.start()
    for index, (kind, _, _, blocks) in enumerate(pieces):
        if index < 2:
            grads[index].wait()
        for load in loads(index):
            load.wait()
        for first, count, chunk, lane in blocks:
            span = slice(first, first + count)
            results = rule(
                getattr(s, f"{kind}_w_here")[:, span],
                s.g_here[chunk[0], chunk[1], :, lane : lane + count],
                getattr(s, f"{kind}_m_here")[:, span],
                getattr(s, f"{kind}_e_here")[:, span],
            )
            for what, result in zip(whats, results, strict=True):
                getattr(s, f"{kind}_{what}_here")[:, span] = result
        for store in stores(index):
            store.start()
        if index == 0:
            enter[1].wait()
            leave[1].start()
    for index in range(len(pieces)):
        for store in stores(index):
            store.wait()
    for copy in leave + small_out:
        copy.wait()


def local(
    tokens,
    doc_ids,
    cotangent,
    attn_weights,
    mlp_weights,
    gains,
    moment_attn,
    moment_mlp,
    moment_gains,
    ema_attn,
    ema_mlp,
    ema_gains,
):
    row_count, width = tokens.shape
    shard_rows = attn_weights.shape[0]
    group = width // shard_rows
    pairs = width // LANES
    hidden = mlp_weights.shape[1] // 3
    half_width = width // 2
    thirds = pairs // 2
    mlp_chunks = hidden // (2 * LANES)
    chunks = thirds + 1 + mlp_chunks

    def pack(attn, mlp):
        qkv = attn[:, : 3 * width].reshape(shard_rows, 3, pairs, LANES).transpose(2, 0, 1, 3)
        out = attn[:, 3 * width :].reshape(shard_rows, 2, half_width).transpose(1, 0, 2)
        ffn = mlp.reshape(shard_rows, 3, 2 * mlp_chunks, LANES).transpose(2, 0, 1, 3)
        return jnp.concatenate(
            [
                qkv.reshape(pairs, shard_rows, half_width),
                out,
                ffn.reshape(2 * mlp_chunks, shard_rows, half_width),
            ],
            axis=0,
        ).reshape(chunks, 2, shard_rows, half_width)

    vmem = pl.BlockSpec(memory_space=pltpu.VMEM)
    hbm = pl.BlockSpec(memory_space=pl.ANY)
    linked = shard_rows % 16 == 0 and group % 4 == 0
    planes = group // 4
    inputs = [("doc_in", hbm, doc_ids), ("x_in", hbm, tokens), ("cot_in", hbm, cotangent)]
    inputs += [("tables", hbm, rotary_tables(row_count))]
    token_rows = (row_count, width)
    outputs = [
        ("block_out", hbm, jax.ShapeDtypeStruct(token_rows, bf16)),
        ("input_grad", hbm, jax.ShapeDtypeStruct(token_rows, bf16)),
    ]
    by_pair = (pairs, LANES, row_count)
    scratch = [
        ("x", pltpu.VMEM(token_rows, bf16)),
        ("cot", pltpu.VMEM(token_rows, bf16)),
        ("y", pltpu.VMEM(token_rows, f32)),
        ("total", pltpu.VMEM(token_rows, f32)),
        ("dn", pltpu.VMEM(token_rows, f32)),
        ("n1t", pltpu.VMEM((width, row_count), bf16)),
        ("qt", pltpu.VMEM(by_pair, bf16)),
        ("kt", pltpu.VMEM(by_pair, bf16)),
        ("vt", pltpu.VMEM(by_pair, bf16)),
        ("k", pltpu.VMEM((pairs, row_count, LANES), bf16)),
        ("v", pltpu.VMEM((pairs, row_count, LANES), bf16)),
        ("mixt", pltpu.VMEM(by_pair, bf16)),
        ("n2", pltpu.VMEM((pairs, row_count, LANES), bf16)),
        ("n2t", pltpu.VMEM(by_pair, bf16)),
        ("hid", pltpu.VMEM((row_count, 2 * LANES), bf16)),
        ("dgu", pltpu.VMEM((row_count, 4 * LANES), bf16)),
        ("lse", pltpu.VMEM((pairs // 2, 8, row_count), f32)),
        ("cost", pltpu.VMEM((HEAD // 2, row_count), f32)),
        ("sint", pltpu.VMEM((HEAD // 2, row_count), f32)),
        ("local_sem", pltpu.SemaphoreType.DMA((4,))),
        ("doc", pltpu.SMEM(doc_ids.shape, jnp.int32)),
    ]
    if linked:
        lines = (planes, shard_rows, half_width)
        pair_lines = (planes, 2, shard_rows, half_width)
        whole = (planes, 4, shard_rows, half_width)
        gain_rows = (8, width)
        inputs += [
            ("attn_in", hbm, attn_weights),
            ("mlp_in", hbm, mlp_weights),
            ("gains_hbm", hbm, gains),
        ]
        outputs += [
            ("g_out", hbm, jax.ShapeDtypeStruct((chunks, 2, shard_rows, half_width), f32)),
            ("gain_out", hbm, jax.ShapeDtypeStruct((8, LANES), f32)),
        ]
        scratch += [
            ("w", pltpu.VMEM((chunks, 2) + whole, bf16)),
            ("g", pltpu.VMEM((2, 2) + whole, bf16)),
            ("a", pltpu.VMEM((2,) + whole, bf16)),
            ("h", pltpu.VMEM((HELD,) + whole, bf16)),
            ("b", pltpu.VMEM((4,) + pair_lines, bf16)),
            ("cs", pltpu.VMEM((2,) + lines, bf16)),
            ("c", pltpu.VMEM((4,) + lines, bf16)),
            ("kept", pltpu.VMEM((2,) + lines, bf16)),
            ("ds", pltpu.VMEM((2,) + lines, bf16)),
            ("d", pltpu.VMEM((4, planes - 1) + lines[1:], bf16)),
            ("own", pltpu.VMEM((2,) + lines[1:], f32)),
            ("gout", pltpu.VMEM((6,) + lines[1:], f32)),
            ("gains_in", pltpu.VMEM(gains.shape, f32)),
            ("gains_end", pltpu.VMEM((8, LANES), f32)),
            ("gains_sem", pltpu.SemaphoreType.DMA((2,))),
            ("gt", pltpu.VMEM((planes, 4, 16, LANES), bf16)),
            ("gain", pltpu.VMEM(gain_rows, f32)),
            ("gp", pltpu.VMEM((4,) + gain_rows, f32)),
            ("gz", pltpu.VMEM((planes,) + gain_rows, f32)),
            ("gc", pltpu.VMEM((2,) + gain_rows, f32)),
            ("load_sem", pltpu.SemaphoreType.DMA((4 + 3 * hidden // width,))),
            ("hop_sem", pltpu.SemaphoreType.DMA((chunks, 5))),
            ("sent_sem", pltpu.SemaphoreType.DMA((6,))),
            ("gain_sem", pltpu.SemaphoreType.DMA((2, planes + 2))),
            ("rs_sem", pltpu.SemaphoreType.DMA((chunks, 4, 2))),
            ("end_sem", pltpu.SemaphoreType.DMA((chunks, 3))),
            ("gsum_sem", pltpu.SemaphoreType.DMA((2, planes + 3))),
        ]
        params = pltpu.CompilerParams(
            collective_id=0, has_side_effects=True, vmem_limit_bytes=VMEM_BYTES
        )
    else:
        packed = pack(attn_weights.astype(bf16), mlp_weights.astype(bf16))
        full = lax.all_gather(packed, "fsdp", axis=2, tiled=True)
        gain_full = lax.all_gather(gains.astype(bf16), "fsdp", axis=1, tiled=True).astype(f32)
        inputs += [("w", vmem, full), ("gain", vmem, gain_full)]
        outputs += [
            ("g_out", hbm, jax.ShapeDtypeStruct((chunks, 2, width, half_width), bf16)),
            ("gain_out", vmem, jax.ShapeDtypeStruct((8, width), f32)),
        ]
        scratch += [
            ("g", pltpu.VMEM((2, 2, width, half_width), bf16)),
            ("g_sem", pltpu.SemaphoreType.DMA((2,))),
        ]
        params = pltpu.CompilerParams(vmem_limit_bytes=63 * 2**20)
    names = [entry[0] for entry in inputs + outputs + scratch]
    block_out, input_grad, part, gain_part = pl.pallas_call(
        functools.partial(block_kernel, linked, names),
        out_shape=[entry[2] for entry in outputs],
        in_specs=[entry[1] for entry in inputs],
        out_specs=[entry[1] for entry in outputs],
        scratch_shapes=[entry[1] for entry in scratch],
        compiler_params=params,
        name="block",
    )(*[entry[2] for entry in inputs])

    if not linked:
        part = lax.psum_scatter(part, "fsdp", scatter_dimension=2, tiled=True)
        part = lax.psum(part, "rep").astype(f32)
        part = jnp.concatenate([part[mlp_chunks + 1 :], part[mlp_chunks:][:1], part[:mlp_chunks]])
        gain_part = lax.psum_scatter(gain_part[:2], "fsdp", scatter_dimension=1, tiled=True)
        gain_part = lax.psum(gain_part, "rep")
        gain_part = jnp.pad(gain_part, ((0, 6), (0, LANES - shard_rows)))

    total_tokens = row_count * lax.axis_size("fsdp") * lax.axis_size("rep")
    rate = PEAK_RATE * STEP / (WARMUP * math.sqrt(total_tokens))

    sources = {
        "w": (attn_weights, mlp_weights, gains),
        "m": (moment_attn, moment_mlp, moment_gains),
        "e": (ema_attn, ema_mlp, ema_gains),
    }
    kinds = ["attn", "mlp", "gains"]
    whats = ["grad", "next", "velocity", "average", "copy"]
    inputs = [("out_in", hbm, block_out), ("grad_in", hbm, input_grad), ("g", hbm, part)]
    inputs += [("gain_part_in", hbm, gain_part)]
    outputs = [("block_out", hbm, block_out), ("input_grad", hbm, input_grad)]
    scratch = []
    for what, arrays in sources.items():
        for kind, array in zip(kinds, arrays, strict=True):
            inputs.append((f"{kind}_{what}", hbm, array))
            scratch.append((f"{kind}_{what}_here", pltpu.VMEM(array.shape, f32)))
    for what in whats:
        for kind, array in zip(kinds, sources["w"], strict=True):
            dtype = bf16 if what == "copy" else f32
            outputs.append((f"{kind}_{what}", hbm, jax.ShapeDtypeStruct(array.shape, dtype)))
            scratch.append((f"{kind}_{what}_here", pltpu.VMEM(array.shape, dtype)))
    scratch += [
        ("g_here", pltpu.VMEM(part.shape, f32)),
        ("gain_part", pltpu.VMEM(gain_part.shape, f32)),
        ("in_sem", pltpu.SemaphoreType.DMA((5, 4))),
        ("out_sem", pltpu.SemaphoreType.DMA((5, 5))),
        ("pass_here", pltpu.VMEM((2,) + block_out.shape, bf16)),
        ("pass_sem", pltpu.SemaphoreType.DMA((6,))),
    ]
    names = [entry[0] for entry in inputs + outputs + scratch]
    return pl.pallas_call(
        functools.partial(update_kernel, rate, names),
        out_shape=[jax.ShapeDtypeStruct(entry[2].shape, entry[2].dtype) for entry in outputs],
        in_specs=[entry[1] for entry in inputs],
        out_specs=[entry[1] for entry in outputs],
        scratch_shapes=[entry[1] for entry in scratch],
        compiler_params=pltpu.CompilerParams(vmem_limit_bytes=63 * 2**20),
        name="update",
    )(*[entry[2] for entry in inputs])


def solution(mesh):
    rows = P(("fsdp", "rep"), None)
    shard = P("fsdp", None)
    columns = P(None, "fsdp")
    kinds = (shard, shard, columns)
    return jax.shard_map(
        local,
        mesh=mesh,
        in_specs=(rows, P(("fsdp", "rep")), rows) + kinds * 3,
        out_specs=(rows, rows) + kinds * 5,
        check_vma=False,
    )
```

```python
import functools
import math

import jax
import jax.numpy as jnp
import numpy as np
from jax import lax
from jax.experimental import pallas as pl
from jax.experimental.pallas import tpu as pltpu
from jax.sharding import PartitionSpec as P

HEAD = 64
VMEM_BYTES = 67_000_000
STEP = 5
WARMUP = 10
EPSILON = 1e-05
MASKED = -1e30
MOMENTUM = 0.5
DECAY = 0.5
PEAK_RATE = 0.1
LANES = 128
BLOCK = 256
PLAN = {
    ("pre", 1): [
        ("F", (1,)),
    ],
    ("pre", 0): [
        ("F", (2,)),
        ("S", (1,)),
        ("F", (3,)),
    ],
    ("fwd", 0): [
        ("S", (2, 3, 5)),
        ("R", (0, 1, -1)),
        ("F", (4, -1, 7)),
        ("f", (-1, -1, 8)),
        ("f", (-1, -1, 9)),
        ("f", (-1, -1, 10)),
        ("R", (-1, -1, 2)),
    ],
    ("fwd", 1): [
        ("F", (-1, 6, -1)),
    ],
    ("fwd", 2): [
        ("T", (1, 2, 3)),
        ("F", (5, -1, -1)),
        ("S", (-1, 4, -1)),
    ],
    ("wo", 0): [
        ("S", (6,)),
        ("f", (11,)),
        ("R", (3,)),
    ],
    ("wo", 1): [
    ],
    ("mlp", 0): [
        ("s", (-1, -1, 9, -1, -1, -1, -1, -1)),
        ("T", (4, -1, 7, 8, -1, -1, -1, -1)),
        ("R", (4, 5, 6, -1, -1, -1, -1, -1)),
        ("s", (-1, 8, -1, -1, -1, -1, -1, -1)),
        ("Q", (-1, -1, -1, -1, -1, -1, 0, -1)),
        ("H", (-1, -1, -1, 1, 2, -1, 4, -1)),
        ("L", (-1, -1, -1, -1, -1, -1, -1, 0)),
        ("A", (-1, 0, 1, 2, 3, 4, 5, 6)),
        ("B", (-1, -1, -1, -1, -1, -1, 2, -1)),
        ("R", (-1, -1, -1, -1, -1, 10, 11, -1)),
    ],
    ("mlp", 1): [
        ("T", (5, 6, -1, 9, 10, 11, -1, -1)),
        ("S", (7, -1, -1, -1, -1, -1, -1, -1)),
        ("Q", (-1, -1, -1, -1, -1, -1, 1, -1)),
        ("H", (-1, 0, -1, -1, 3, -1, 5, -1)),
        ("s", (-1, -1, 10, 11, -1, -1, -1, -1)),
        ("B", (-1, -1, -1, 0, -1, -1, 3, -1)),
        ("B", (-1, -1, -1, 1, -1, -1, -1, -1)),
        ("R", (-1, -1, 7, 8, 9, -1, -1, -1)),
    ],
    ("d", 0): [
        ("Q", (2,)),
        ("H", (6,)),
        ("A", (7,)),
        ("B", (4,)),
    ],
    ("o", 0): [
        ("L", (1,)),
    ],
    ("o", 1): [
        ("Q", (3,)),
        ("H", (7,)),
        ("A", (8,)),
        ("B", (5,)),
    ],
    ("bwd", 0): [
        ("E", (0, -1, -1)),
        ("L", (2, -1, -1)),
    ],
    ("bwd", 1): [
        ("E", (-1, -1, 4)),
        ("L", (-1, 4, 6)),
        ("H", (-1, 9, 10)),
    ],
    ("bwd", 2): [
        ("Q", (4, 6, 8)),
        ("H", (8, -1, -1)),
        ("B", (6, -1, 10)),
    ],
    ("bwd", 3): [
        ("E", (1, 3, 5)),
        ("L", (3, 5, 7)),
        ("B", (-1, 8, -1)),
    ],
    ("bwd", 4): [
    ],
    ("bwd", 5): [
        ("E", (2, -1, -1)),
        ("Q", (5, 7, 9)),
        ("A", (9, 10, 11)),
        ("B", (7, 9, -1)),
    ],
    ("tail", 0): [
    ],
    ("tail", 1): [
        ("E", (6,)),
        ("L", (8,)),
        ("H", (11,)),
        ("B", (11,)),
    ],
    ("tail", 2): [
        ("Q", (10,)),
    ],
    ("tail", 3): [
        ("E", (7,)),
        ("L", (9,)),
    ],
    ("end", 0): [
        ("Q", (11,)),
        ("E", (8,)),
        ("L", (10,)),
        ("E", (9,)),
        ("L", (11,)),
        ("E", (10,)),
        ("E", (11,)),
    ],
}
HELD = 4
LATE = 8

f32 = jnp.float32
bf16 = jnp.bfloat16


def nn(left, right):
    return jnp.dot(left, right, preferred_element_type=f32)


def nt(left, right):
    return lax.dot_general(
        left, right, (((1,), (1,)), ((), ())), preferred_element_type=f32
    )


def in_turn(items, stages, breaks=None):
    values = {}
    for turn in range(len(items) + len(stages) - 1):
        if breaks and turn in breaks:
            breaks[turn]()
        for number, stage in enumerate(stages):
            index = turn - number
            if 0 <= index < len(items):
                values[index] = stage(items[index], *values.get(index, ()))


def rotary_tables(row_count):
    half = HEAD // 2
    frequency = np.float32(10000.0) ** (-np.arange(half, dtype=np.float32) / np.float32(half))
    angles = np.arange(row_count, dtype=np.float32)[None, :] * frequency.astype(np.float32)[:, None]
    angles = angles.astype(np.float64)
    tables = np.stack([np.cos(angles), np.sin(angles)]).astype(np.float32)
    tables = tables.reshape(2, half, row_count // BLOCK, BLOCK).transpose(0, 2, 1, 3)
    return np.ascontiguousarray(tables.reshape(-1, BLOCK))


def rotate_rows(rows, cosine, sine):
    half = HEAD // 2
    first, second = rows[:half], rows[half:]
    return jnp.concatenate(
        [first * cosine - second * sine, second * cosine + first * sine], axis=0
    )


def rms_scale(rows):
    return lax.rsqrt(jnp.mean(rows * rows, axis=-1, keepdims=True) + EPSILON)


class Scratch:
    def __init__(self, names, refs):
        for name, ref in zip(names, refs, strict=True):
            setattr(self, name, ref)


def block_kernel(linked, names, *refs):
    s = Scratch(names, refs)
    row_count, width = s.x.shape
    blocks = row_count // BLOCK
    pairs = width // LANES
    thirds = pairs // 2
    half_width = width // 2
    chunks = s.w.shape[0]
    mlp_chunks = chunks - thirds - 1
    slots = s.g.shape[0]

    def rows_of(i):
        return pl.ds(i * BLOCK, BLOCK)

    def store_pairs(i, value):
        for p in range(pairs):
            s.n2[p, rows_of(i), :] = value[:, p * LANES : (p + 1) * LANES]

    def load_pairs(i):
        return jnp.concatenate([s.n2[p, rows_of(i), :] for p in range(pairs)], axis=1)

    def sums_at(kind, first, count, j):
        return (pl.ds(j * LANES + first, count), pl.ds(kind * BLOCK, BLOCK))

    places = [[0, 1, 2, 3], [0, 2, 1, 3]]

    def load_w(chunk, half):
        if not linked:
            return s.w[chunk, half]
        if half == 0:
            return s.w[chunk, 0].reshape(width, half_width)
        parts = [s.w[chunk, 1, z, place] for z in range(s.w.shape[2]) for place in places[1]]
        return jnp.concatenate(parts, axis=0)

    def store_g(chunk, half, lanes, value):
        low = value.astype(bf16)
        if linked and half == 0:
            low = low.reshape(s.g.shape[2:5] + (low.shape[1],))
            s.g[chunk % slots, 0, :, :, :, lanes] = low
        elif linked:
            low = low.reshape((-1,) + s.g.shape[4:5] + (low.shape[1],))
            for z in range(s.g.shape[2]):
                for index, place in enumerate(places[1]):
                    s.g[chunk % slots, 1, z, place, :, lanes] = low[4 * z + index]
        else:
            s.g[chunk % slots, half, :, lanes] = low

    if linked:
        gather_start, actions, gain_steps = links(s, chunks, thirds, mlp_chunks)
    else:


        def grad_copy(chunk):
            slot = chunk % slots
            return pltpu.make_async_copy(s.g.at[slot], s.g_out.at[chunk], s.g_sem.at[slot])

        actions = {"A": lambda chunk: grad_copy(chunk).start()}
        actions["H"] = lambda chunk: grad_copy(chunk).wait()

    def events(loop, place, index=0):
        for kind, table in PLAN[loop, place]:
            if kind not in actions:
                continue
            if isinstance(index, int):
                if table[index] >= 0:
                    actions[kind](table[index])
                continue
            used = [i for i, entry in enumerate(table) if entry >= 0]
            shift = table[used[0]] - used[0]
            in_line = all(table[i] == i + shift for i in used)
            in_line = in_line and used == list(range(used[0], used[-1] + 1))
            if in_line:
                chunk = index + shift
            else:
                chunk = jnp.int32(table[used[0]])
                for i in used[1:]:
                    chunk = jnp.where(index == i, table[i], chunk)
            if len(used) == len(table):
                actions[kind](chunk)
                continue
            if in_line:
                now = (index >= used[0]) & (index <= used[-1])
            else:
                now = functools.reduce(lambda u, v: u | v, [index == i for i in used])
            pl.when(now)(functools.partial(actions[kind], chunk))

    copies = [
        pltpu.make_async_copy(s.x_in, s.x, s.local_sem.at[0]),
        pltpu.make_async_copy(s.cot_in, s.cot, s.local_sem.at[1]),
    ]
    tables = s.total.at[pl.ds(0, HEAD * blocks), pl.ds(0, BLOCK)]
    copies.append(pltpu.make_async_copy(s.tables, tables, s.local_sem.at[2]))
    copies.append(pltpu.make_async_copy(s.doc_in, s.doc, s.local_sem.at[3]))
    if linked:
        gather_start[0]()
    for copy in copies:
        copy.start()

    copies.pop().wait()
    docs = [s.doc[BLOCK * j] for j in range(blocks)]
    bias = [
        [jnp.where(docs[i] == docs[j], 0.0, MASKED).astype(f32) for j in range(i)] + [0.0]
        for i in range(blocks)
    ]
    causal = lax.broadcasted_iota(jnp.int32, (BLOCK, BLOCK), 0) <= lax.broadcasted_iota(
        jnp.int32, (BLOCK, BLOCK), 1
    )

    copies.pop().wait()
    for i in range(blocks):
        place = sum([(docs[j] == docs[i]).astype(jnp.int32) for j in range(i)], jnp.int32(0))
        for index, table in enumerate([s.cost, s.sint]):
            chosen = None
            for t in range(i + 1):
                first = (index * blocks + t) * (HEAD // 2)
                part = s.total[pl.ds(first, HEAD // 2), pl.ds(0, BLOCK)]
                chosen = part if t == 0 else jnp.where(place == t, part, chosen)
            table[:, rows_of(i)] = chosen
    if linked:
        gather_start[1]()
        events("pre", 1)
    for copy in copies:
        copy.wait()
    if linked:
        gather_start[2]()
        events("pre", 0)
    if linked:
        gather_start[3]()
    gain_one = s.gain[0:1, :]
    gain_two = s.gain[1:2, :]
    for i in range(blocks):
        stream = s.x[rows_of(i), :].astype(f32)
        normed = (stream * rms_scale(stream) * gain_one).astype(bf16)
        s.n1t[:, rows_of(i)] = normed.T
        s.dn[rows_of(i), :] = jnp.zeros((BLOCK, width), f32)

    def masked_pair(rows, h):
        zero = jnp.zeros((HEAD, BLOCK), bf16)
        parts = [rows[:HEAD], zero] if h == 0 else [zero, rows[HEAD:]]
        return jnp.concatenate(parts, axis=0)

    def scores_of(p, i, h):
        span = (i + 1) * BLOCK
        query = masked_pair(s.qt[p, :, rows_of(i)], h)
        scores = nn(s.k[p, pl.ds(0, span), :], query)
        parts = [scores[j * BLOCK : (j + 1) * BLOCK] for j in range(i + 1)]
        parts[i] = jnp.where(causal, parts[i], MASKED)
        return parts

    bodies = [(q, i, h) for q in range(2) for i in range(blocks) for h in range(2)]
    half_way = 2 * blocks

    def lse_at(p, i, h):
        return (p // 2, pl.ds(2 * (p % 2) + h, 1), rows_of(i))

    def project(third, q):
        p = 2 * third + q
        weights_t = load_w(third, q).T
        for i in range(blocks):
            cosine, sine = s.cost[:, rows_of(i)], s.sint[:, rows_of(i)]
            projected = nn(weights_t, s.n1t[:, rows_of(i)])
            for h in range(2):
                lo, hi = h * HEAD, (h + 1) * HEAD
                query = rotate_rows(projected[lo:hi], cosine, sine).astype(bf16)
                s.qt[p, lo:hi, rows_of(i)] = query * bf16(0.125)
                key = rotate_rows(projected[LANES + lo : LANES + hi], cosine, sine)
                s.kt[p, lo:hi, rows_of(i)] = key.astype(bf16)
            s.vt[p, :, rows_of(i)] = projected[2 * LANES :].astype(bf16)
            s.k[p, rows_of(i), :] = s.kt[p, :, rows_of(i)].T
            s.v[p, rows_of(i), :] = s.vt[p, :, rows_of(i)].T

    def attention_forward(third, carry):
        events("fwd", 0, third)
        project(third, 0)
        project(third, 1)
        events("fwd", 1, third)

        def scores(n):
            q, i, h = n
            return (scores_of(2 * third + q, i, h),)

        def shares(n, parts):
            q, i, h = n
            p = 2 * third + q
            tops = [
                jnp.max(part, axis=0, keepdims=True) + bias[i][j]
                for j, part in enumerate(parts)
            ]
            top = functools.reduce(jnp.maximum, tops)
            exps = [jnp.exp(part - (top - bias[i][j])) for j, part in enumerate(parts)]
            total = sum([jnp.sum(e, axis=0, keepdims=True) for e in exps])
            s.lse[lse_at(p, i, h)] = top + jnp.log(total)
            return jnp.concatenate([e.astype(bf16) for e in exps], axis=0), 1.0 / total

        def mix(n, exps_low, inverse):
            q, i, h = n
            p = 2 * third + q
            heads = pl.ds(h * HEAD, HEAD)
            mixed = nn(s.vt[p, heads, pl.ds(0, (i + 1) * BLOCK)], exps_low)
            s.mixt[p, heads, rows_of(i)] = (mixed * inverse).astype(bf16)

        in_turn(
            bodies,
            [scores, shares, mix],
            {half_way: lambda: events("fwd", 2, third)},
        )
        return carry

    lax.fori_loop(0, thirds, attention_forward, 0)

    out_chunk = thirds
    for i in range(blocks):
        if i % 2 == 0:
            events("wo", i // 2)
        mixed = s.mixt[:, :, rows_of(i)].reshape(width, BLOCK).T
        branch = jnp.concatenate(
            [nn(mixed, load_w(out_chunk, half)) for half in range(2)], axis=1
        )
        after = s.x[rows_of(i), :].astype(f32) + branch
        s.y[rows_of(i), :] = after
        s.total[rows_of(i), :] = after
        normed = (after * rms_scale(after) * gain_two).astype(bf16)
        store_pairs(i, normed)
        s.n2t[:, :, rows_of(i)] = normed.T.reshape(pairs, LANES, BLOCK)

    tiles = [pl.ds(t * BLOCK, BLOCK) for t in range(width // BLOCK)]
    for i in range(blocks):
        for tile in tiles:
            s.x[rows_of(i), tile] = s.cot[rows_of(i), tile].T

    def feed_forward(chunk, carry):
        events("mlp", 0, chunk)
        low = [load_w(thirds + 1 + chunk, half) for half in range(2)]
        w_gu = [w[:, : 2 * LANES] for w in low]
        w_gu_all = jnp.concatenate(w_gu, axis=1)
        w_down = jnp.concatenate([w[:, 2 * LANES :] for w in low], axis=1)

        def products(i):
            normed = load_pairs(i)
            d_hidden = nn(s.cot[rows_of(i), :], w_down)
            return d_hidden, [nn(normed, w) for w in w_gu]

        def slopes(i, d_hidden, gate_ups):
            for half, gate_up in enumerate(gate_ups):
                gate, up = gate_up[:, :LANES], gate_up[:, LANES:]
                back = d_hidden[:, half * LANES : (half + 1) * LANES]
                sig = jax.nn.sigmoid(gate)
                silu = gate * sig
                s.hid[rows_of(i), pl.ds(half * LANES, LANES)] = (silu * up).astype(bf16)
                s.dgu[rows_of(i), pl.ds(2 * half * LANES, LANES)] = (
                    back * up * (sig + silu * (1.0 - sig))
                ).astype(bf16)
                s.dgu[rows_of(i), pl.ds((2 * half + 1) * LANES, LANES)] = (
                    back * silu
                ).astype(bf16)
            return ()

        def sums(i):
            s.total[rows_of(i), :] += nt(s.hid[rows_of(i), :], w_down)
            s.dn[rows_of(i), :] += nt(s.dgu[rows_of(i), :], w_gu_all)

        in_turn(list(range(blocks)), [products, slopes, sums])
        events("mlp", 1, chunk)
        n2t = s.n2t[...].reshape(width, row_count)
        for half in range(2):
            store_g(
                chunk,
                half,
                pl.ds(0, 2 * LANES),
                nn(n2t, s.dgu[:, pl.ds(2 * half * LANES, 2 * LANES)]),
            )
        grad_down = jnp.concatenate(
            [
                nn(
                    jnp.concatenate([s.x[rows_of(i), tile] for i in range(blocks)], axis=1),
                    s.hid[...],
                )
                for tile in tiles
            ],
            axis=0,
        )
        for half in range(2):
            store_g(
                chunk,
                half,
                pl.ds(2 * LANES, LANES),
                grad_down[:, half * LANES : (half + 1) * LANES],
            )
        return carry

    lax.fori_loop(0, mlp_chunks, feed_forward, 0)

    events("d", 0)
    x_copy = pltpu.make_async_copy(s.x_in, s.x, s.local_sem.at[1])
    x_copy.start()

    gain_grad_two = jnp.zeros((1, width), f32)
    for i in range(blocks):
        after = s.y[rows_of(i), :]
        scale = rms_scale(after)
        unit = after * scale
        d_normed = s.dn[rows_of(i), :]
        d_unit = d_normed * gain_two
        gain_grad_two += jnp.sum(d_normed * unit, axis=0, keepdims=True)
        grad_after = s.cot[rows_of(i), :].astype(f32) + scale * (
            d_unit - unit * jnp.mean(d_unit * unit, axis=-1, keepdims=True)
        )
        s.y[rows_of(i), :] = grad_after
        store_pairs(i, grad_after.astype(bf16))
        s.cot[rows_of(i), :] = s.total[rows_of(i), :].astype(bf16)
    out_copy = pltpu.make_async_copy(s.cot, s.block_out, s.local_sem.at[0])
    out_copy.start()

    events("o", 0)
    mixt = s.mixt[...].reshape(width, row_count)
    for half in range(2):
        store_g(
            mlp_chunks,
            half,
            pl.ds(0, half_width),
            nn(mixt, jnp.concatenate([s.n2[p] for p in range(half * thirds, (half + 1) * thirds)], axis=1)),
        )
    events("o", 1)
    dmt = s.n2t
    w_out = jnp.concatenate([load_w(out_chunk, half) for half in range(2)], axis=1)
    for i in range(blocks):
        d_mixed = nt(w_out, load_pairs(i))
        dmt[:, :, rows_of(i)] = d_mixed.astype(bf16).reshape(pairs, LANES, BLOCK)

    def turn_back(p, q, i):
        cosine, sine = s.cost[:, rows_of(i)], -s.sint[:, rows_of(i)]
        pieces = []
        for kind in range(2):
            for h in range(2):
                piece = s.total[sums_at(kind, h * HEAD, HEAD, q * blocks + i)]
                piece = rotate_rows(piece, cosine, sine)
                pieces.append((piece * 0.125 if kind == 0 else piece).astype(bf16))
        s.k[p, rows_of(i), :] = jnp.concatenate(pieces[:2], axis=0).T
        s.v[p, rows_of(i), :] = jnp.concatenate(pieces[2:], axis=0).T
        s.n2[p, rows_of(i), :] = s.total[sums_at(2, 0, LANES, q * blocks + i)].astype(bf16).T

    def attention_backward(third, carry):
        events("bwd", 0, third)
        for j in range(2 * blocks):
            for kind in (1, 2):
                s.total[sums_at(kind, 0, LANES, j)] = jnp.zeros((LANES, BLOCK), f32)

        def begin(n):
            q, i, h = n
            p = 2 * third + q
            back = masked_pair(dmt[p, :, rows_of(i)], h)
            return scores_of(p, i, h), nn(s.v[p, pl.ds(0, (i + 1) * BLOCK), :], back)

        def middle(n, parts, d_probs):
            q, i, h = n
            lse = s.lse[lse_at(2 * third + q, i, h)]
            probs = [jnp.exp(part - (lse - bias[i][j])) for j, part in enumerate(parts)]
            probs = jnp.concatenate(probs, axis=0)
            weighted = probs * d_probs
            inner = jnp.sum(weighted, axis=0, keepdims=True)
            return (weighted - probs * inner).astype(bf16), probs.astype(bf16)

        def finish(n, d_scores, probs_low):
            q, i, h = n
            p = 2 * third + q
            heads, keys = pl.ds(h * HEAD, HEAD), pl.ds(0, (i + 1) * BLOCK)
            s.total[sums_at(0, h * HEAD, HEAD, q * blocks + i)] = nn(
                s.kt[p, heads, keys], d_scores
            )
            d_keys = nt(s.qt[p, heads, rows_of(i)], d_scores)
            d_values = nt(dmt[p, heads, rows_of(i)], probs_low)
            for j in range(i + 1):
                span = slice(j * BLOCK, (j + 1) * BLOCK)
                s.total[sums_at(1, h * HEAD, HEAD, q * blocks + j)] += d_keys[:, span]
                s.total[sums_at(2, h * HEAD, HEAD, q * blocks + j)] += d_values[:, span]
            number = bodies.index(n) - half_way
            if 0 <= number < blocks:
                turn_back(2 * third, 0, number)

        in_turn(
            bodies,
            [begin, middle, finish],
            {
                half_way // 2 + 2: lambda: events("bwd", 1, third),
                half_way + 2: lambda: events("bwd", 2, third),
                half_way + half_way // 2 + 2: lambda: events("bwd", 3, third),
            },
        )
        events("bwd", 4, third)
        for i in range(blocks):
            turn_back(2 * third + 1, 1, i)
        for q in range(2):
            p = 2 * third + q
            d_qkv = jnp.concatenate([s.k[p], s.v[p], s.n2[p]], axis=1)
            store_g(
                mlp_chunks + 1 + third, q, pl.ds(0, half_width), nn(s.n1t[...], d_qkv)
            )
        events("bwd", 5, third)
        return carry

    lax.fori_loop(0, thirds, attention_backward, 0)

    x_copy.wait()
    w_qkv_t = jnp.concatenate([load_w(p // 2, p % 2).T for p in range(pairs)], axis=0)
    gain_grad_one = jnp.zeros((1, width), f32)
    for i in range(blocks):
        events("tail", i)
        d_qkv = [
            ref[p, rows_of(i), :] for p in range(pairs) for ref in (s.k, s.v, s.n2)
        ]
        d_normed = nn(jnp.concatenate(d_qkv, axis=1), w_qkv_t)
        stream = s.x[rows_of(i), :].astype(f32)
        scale = rms_scale(stream)
        unit = stream * scale
        d_unit = d_normed * gain_one
        gain_grad_one += jnp.sum(d_normed * unit, axis=0, keepdims=True)
        s.x[rows_of(i), :] = (
            s.y[rows_of(i), :]
            + scale * (d_unit - unit * jnp.mean(d_unit * unit, axis=-1, keepdims=True))
        ).astype(bf16)
    grad_copy_out = pltpu.make_async_copy(s.x, s.input_grad, s.local_sem.at[1])
    grad_copy_out.start()
    gain_grads = jnp.concatenate(
        [gain_grad_one, gain_grad_two, jnp.zeros((6, width), f32)], axis=0
    )
    if linked:
        gain_steps[0](gain_grads)
        left = list(gain_steps[1:4])
        for kind, table in PLAN["end", 0]:
            actions[kind](table[0])
            if table[0] == chunks - 1 and kind in "QLE" and left:
                left.pop(0)()
        for step in left:
            step()
        gain_steps[4]()
    else:
        events("end", 0)
        s.gain_out[...] = gain_grads
    out_copy.wait()
    grad_copy_out.wait()


def links(s, chunks, thirds, mlp_chunks):
    planes = s.w.shape[2]
    me = lax.axis_index("fsdp")
    core = lax.axis_index("rep")
    z, m = me // 4, me % 4
    over_x, over_y, over_both = m + 1 - 2 * (m % 2), (m + 2) % 4, 3 - m
    m1 = (1 - core) * over_x + core * over_y
    m2 = (1 - core) * over_y + core * over_x
    other = 1 - core
    low = (1 - core) * (m % 2) + core * (m // 2)
    high = (1 - core) * (m // 2) + core * (m % 2)
    place = 2 * high + low

    def chip(plane, place):
        return (plane * 4 + place, core)

    sibling = (me, other)

    def far(k):
        return (z + k) % planes

    peers = [chip(far(k), m) for k in range(1, planes)]
    first, second = chip(z, m1), chip(z, m2)

    def remote(src, dst, send_sem, recv_sem, device):
        return pltpu.make_async_remote_copy(
            src_ref=src,
            dst_ref=dst,
            send_sem=send_sem,
            recv_sem=recv_sem,
            device_id=device,
            device_id_type=pl.DeviceIdType.MESH,
        )

    def along_z(chunk, k):
        block = s.w.at[chunk, core, z, place]
        return remote(block, block, s.sent_sem.at[0], s.hop_sem.at[chunk, 0], peers[k])

    def along_z_here(chunk):
        blocks = s.w.at[chunk, core, pl.ds(0, planes - 1), place]
        return remote(blocks, blocks, s.sent_sem.at[0], s.hop_sem.at[chunk, 0], peers[0])

    def hop(chunk, index):
        if index == 1:
            blocks, device = s.w.at[chunk, core, :, place], first
        elif index == 2:
            blocks, device = s.w.at[chunk, core, :, pl.ds(2 * high, 2)], second
        else:
            blocks, device = s.w.at[chunk, core], sibling
        return remote(blocks, blocks, s.sent_sem.at[index], s.hop_sem.at[chunk, index], device)

    def alone(chunk):
        block = s.w.at[chunk, core, z, place]
        return remote(block, block, s.sent_sem.at[5], s.hop_sem.at[chunk, 1], first)

    def along_z_again(chunk, k):
        block = s.w.at[chunk, core, z, place + 1 - 2 * low]
        return remote(block, block, s.sent_sem.at[4], s.hop_sem.at[chunk, 4], peers[k])

    def along_z_again_here(chunk):
        blocks = s.w.at[chunk, core, pl.ds(0, planes - 1), place]
        return remote(blocks, blocks, s.sent_sem.at[4], s.hop_sem.at[chunk, 4], peers[0])

    def gather_end():
        late = pl.ds(LATE, chunks - LATE)
        blocks = s.w.at[late, core, pl.ds(0, planes - 1), place]
        remote(blocks, blocks, s.sent_sem.at[4], s.hop_sem.at[0, 4], peers[0]).wait_send()
        blocks = s.w.at[late, core, z, place]
        remote(blocks, blocks, s.sent_sem.at[5], s.hop_sem.at[0, 1], first).wait_send()
        blocks = s.w.at[:, core, pl.ds(0, planes - 1), place]
        remote(blocks, blocks, s.sent_sem.at[0], s.hop_sem.at[0, 0], peers[0]).wait_send()
        blocks = s.w.at[pl.ds(0, LATE), core, :, place]
        remote(blocks, blocks, s.sent_sem.at[1], s.hop_sem.at[0, 1], first).wait_send()
        blocks = s.w.at[:, core, :, pl.ds(2 * high, 2)]
        remote(blocks, blocks, s.sent_sem.at[2], s.hop_sem.at[0, 2], second).wait_send()
        blocks = s.w.at[:, core]
        remote(blocks, blocks, s.sent_sem.at[3], s.hop_sem.at[0, 3], sibling).wait_send()

    def gain_along_z(k):
        block = s.gt.at[z, m]
        return remote(block, block, s.gain_sem.at[0, k], s.gain_sem.at[1, k], peers[k])

    def gain_hop(index):
        blocks = s.gt.at[:, [m, m, m1][index]]
        device = [first, second, second][index]
        k = planes - 1 + index
        return remote(blocks, blocks, s.gain_sem.at[0, k], s.gain_sem.at[1, k], device)

    width = s.x.shape[1]
    pairs = width // LANES
    shard_rows = s.w.shape[4]
    half_width = s.w.shape[5]
    hidden = s.mlp_in.shape[1] // 3
    loads = [
        functools.partial(
            pltpu.make_async_copy,
            s.attn_in.at[:, pl.ds(k * width, width)],
            s.dn.at[pl.ds(k * shard_rows, shard_rows)],
            s.load_sem.at[k],
        )
        for k in range(4)
    ] + [
        functools.partial(
            pltpu.make_async_copy,
            s.mlp_in.at[:, pl.ds(k * width, width)],
            s.dn.at[pl.ds((4 + k) * shard_rows, shard_rows)],
            s.load_sem.at[4 + k],
        )
        for k in range(3 * hidden // width)
    ]

    def piece(row, lane):
        rows = s.dn[pl.ds(row * shard_rows, shard_rows), pl.ds(lane, LANES)]
        return rows.astype(bf16)

    def round_third(third):
        lane = pl.multiple_of((2 * third + core) * LANES, LANES)
        for kind in range(3):
            s.w[third, core, z, place, :, kind * LANES : (kind + 1) * LANES] = piece(kind, lane)

    def gather_start():
        barrier = pltpu.get_barrier_semaphore()
        partners = [chip(z, over_x), chip(z, over_y), chip(z, over_both), sibling] + peers
        for partner in partners:
            pl.semaphore_signal(
                barrier, inc=1, device_id=partner, device_id_type=pl.DeviceIdType.MESH
            )
        for load in loads:
            load().start()
        gains_copy = pltpu.make_async_copy(s.gains_hbm, s.gains_in, s.gains_sem.at[0])
        gains_copy.start()
        gains_copy.wait()
        own = s.gains_in[...].astype(bf16)
        own = jnp.concatenate([own, jnp.zeros((2, LANES - shard_rows), bf16)], axis=1)
        s.gt[z, m] = jnp.concatenate([own, jnp.zeros((14, LANES), bf16)], axis=0)
        for load in loads[:3]:
            load().wait()
        round_third(0)
        pl.semaphore_wait(barrier, len(partners))
        for k in range(planes - 1):
            along_z(0, k).start()
        for k in range(planes - 1):
            gain_along_z(k).start()
        loads[3]().wait()
        for third in range(1, thirds):
            round_third(third)
        lane = pl.multiple_of(core * half_width, LANES)
        s.w[thirds, core, z, place] = s.dn[
            pl.ds(3 * shard_rows, shard_rows), pl.ds(lane, half_width)
        ].astype(bf16)
        for chunk in range(1, thirds + 1):
            for k in range(planes - 1):
                along_z(chunk, k).start()

    def gather_feed_forward():
        for load in loads[4:]:
            load().wait()
        for j in range(mlp_chunks):
            for kind in range(3):
                column = kind * hidden + 2 * j * LANES
                row, begin = 4 + column // width, column % width
                lane = pl.multiple_of(begin + core * LANES, LANES)
                s.w[thirds + 1 + j, core, z, place, :, kind * LANES : (kind + 1) * LANES] = (
                    piece(row, lane)
                )
            for k in range(planes - 1):
                along_z(thirds + 1 + j, k).start()
            if thirds + 1 + j >= LATE:
                alone(thirds + 1 + j).start()

    def gather_one():
        first_hop(0)
        for k in range(planes - 1):
            gain_along_z(k).wait()
        gain_hop(0).start()
        gain_hop(1).start()
        gather_feed_forward()

    def gather_two():
        second_hop(0)
        gain_hop(0).wait()
        gain_hop(2).start()

    def gather_three():
        gain_hop(1).wait()
        gain_hop(2).wait()
        rows = jnp.zeros((8, width), f32)
        for d in range(planes * 4):
            tile = s.gt[d // 4, d % 4].astype(f32)[:8]
            wide = jnp.concatenate([tile, jnp.zeros((8, width - LANES), f32)], axis=1)
            rows += pltpu.roll(wide, d * shard_rows, 1) if d else wide
        s.gain[...] = rows
        third_hop(0)

    def first_hop(chunk):
        along_z_here(chunk).wait_recv()
        hop(chunk, 1).start()

    def first_hop_late(chunk):
        alone(chunk).wait_recv()
        for k in range(planes - 1):
            along_z_again(chunk, k).start()

    def second_hop_late(chunk):
        along_z_here(chunk).wait_recv()
        along_z_again_here(chunk).wait_recv()
        hop(chunk, 2).start()

    def second_hop(chunk):
        hop(chunk, 1).wait_recv()
        hop(chunk, 2).start()

    def third_hop(chunk):
        hop(chunk, 2).wait_recv()
        hop(chunk, 3).start()

    def ready(chunk):
        hop(chunk, 3).wait_recv()

    held = s.h.shape[0]

    def to_sibling(chunk):
        return remote(
            s.g.at[chunk % 2, other],
            s.a.at[chunk % 2],
            s.rs_sem.at[chunk, 0, 0],
            s.rs_sem.at[chunk, 0, 1],
            sibling,
        )

    def to_second(chunk):
        return remote(
            s.h.at[chunk % held, :, pl.ds(2 - 2 * high, 2)],
            s.b.at[chunk % 4],
            s.rs_sem.at[chunk, 1, 0],
            s.rs_sem.at[chunk, 1, 1],
            second,
        )

    def to_first(chunk):
        return remote(
            s.cs.at[chunk % 2],
            s.c.at[chunk % 4],
            s.rs_sem.at[chunk, 2, 0],
            s.rs_sem.at[chunk, 2, 1],
            first,
        )

    def to_plane(chunk, k):
        return remote(
            s.ds.at[chunk % 2, far(k + 1)],
            s.d.at[chunk % 4, k],
            s.rs_sem.at[chunk, 3, 0],
            s.rs_sem.at[chunk, 3, 1],
            peers[k],
        )

    def to_planes(chunk):
        return remote(
            s.ds.at[chunk % 2, pl.ds(0, planes - 1)],
            s.d.at[chunk % 4],
            s.rs_sem.at[chunk, 3, 0],
            s.rs_sem.at[chunk, 3, 1],
            peers[0],
        )

    def place_of(chunk):
        return jnp.where(
            chunk < mlp_chunks,
            thirds + 1 + chunk,
            jnp.where(chunk == mlp_chunks, thirds, chunk - mlp_chunks - 1),
        )

    def to_copy(chunk):
        done = s.g_out.at[place_of(chunk), core]
        sems = s.end_sem.at[chunk, 0], s.end_sem.at[0, 2]
        return remote(s.gout.at[chunk % 6], done, *sems, sibling)

    def leave(chunk):
        done = s.g_out.at[place_of(chunk), core]
        return pltpu.make_async_copy(s.gout.at[chunk % 6], done, s.end_sem.at[chunk, 1])

    def left(chunk):
        to_copy(chunk).wait_send()
        leave(chunk).wait()

    def reduce_end():
        done = s.g_out.at[:, core]
        remote(done, done, s.end_sem.at[0, 0], s.end_sem.at[0, 2], sibling).wait_recv()
        for chunk in range(chunks - 6, chunks):
            left(chunk)

    def send_half(chunk):
        to_sibling(chunk).start()

    def add_half(chunk):
        to_sibling(chunk).wait()
        s.h[chunk % held] = (
            s.g[chunk % 2, core].astype(f32) + s.a[chunk % 2].astype(f32)
        ).astype(bf16)

    def halves(chunk):
        to_second(chunk).start()

    def quarters(chunk):
        to_second(chunk).wait()
        even = chunk % 2
        s.cs[even] = (
            s.h[chunk % held, :, 2 * high + 1 - low].astype(f32)
            + s.b[chunk % 4, :, 1 - low].astype(f32)
        ).astype(bf16)
        to_first(chunk).start()
        s.kept[even] = (
            s.h[chunk % held, :, place].astype(f32) + s.b[chunk % 4, :, low].astype(f32)
        ).astype(bf16)

    def lines(chunk):
        to_first(chunk).wait()
        even = chunk % 2
        s.ds[even] = (s.kept[even].astype(f32) + s.c[chunk % 4].astype(f32)).astype(bf16)
        for k in range(planes - 1):
            to_plane(chunk, k).start()
        s.own[even] = s.kept[even, z].astype(f32) + s.c[chunk % 4, z].astype(f32)

    def last(chunk):
        to_planes(chunk).wait()
        total = s.own[chunk % 2]
        for k in range(planes - 1):
            total += s.d[chunk % 4, k].astype(f32)
        if isinstance(chunk, int):
            if chunk >= 6:
                left(chunk - 6)
        else:
            pl.when(chunk >= 6)(lambda: left(chunk - 6))
        s.gout[chunk % 6] = total
        to_copy(chunk).start()
        leave(chunk).start()

    actions = {"F": first_hop, "S": second_hop, "T": third_hop, "R": ready}
    actions.update({"A": send_half, "H": add_half, "B": halves, "Q": quarters})
    actions.update({"L": lines, "E": last, "f": first_hop_late, "s": second_hop_late})

    def plane_sum():
        block = s.gp.at[m]
        return [
            remote(block, block, s.gsum_sem.at[0, k], s.gsum_sem.at[1, k], chip(z, at))
            for k, at in enumerate([over_x, over_y, over_both])
        ]

    def line_sum():
        block = s.gz.at[z]
        return [
            remote(block, block, s.gsum_sem.at[0, 3 + k], s.gsum_sem.at[1, 3 + k], peers[k])
            for k in range(planes - 1)
        ]

    def core_sum():
        k = planes + 2
        sems = s.gsum_sem
        return remote(s.gc.at[0], s.gc.at[1], sems.at[0, k], sems.at[1, k], sibling)

    def gain_begin(value):
        s.gp[m] = value
        for copy in plane_sum():
            copy.start()

    def gain_lines_sum():
        for copy in plane_sum():
            copy.wait()
        s.gz[z] = (s.gp[0] + s.gp[1]) + (s.gp[2] + s.gp[3])
        for copy in line_sum():
            copy.start()

    def gain_cores():
        for copy in line_sum():
            copy.wait()
        total = s.gz[0]
        for k in range(1, planes):
            total += s.gz[k]
        s.gc[0] = total
        core_sum().start()

    def gain_end():
        core_sum().wait()
        total = s.gc[0] + s.gc[1]
        s.gains_end[...] = pltpu.roll(total, (width - me * shard_rows) % width, 1)[:, :LANES]
        pltpu.make_async_copy(s.gains_end, s.gain_out, s.gains_sem.at[1]).start()

    def gain_out():
        gather_end()
        reduce_end()
        pltpu.make_async_copy(s.gains_end, s.gain_out, s.gains_sem.at[1]).wait()

    start = (gather_start, gather_one, gather_two, gather_three)
    return start, actions, (gain_begin, gain_lines_sum, gain_cores, gain_end, gain_out)


def update_kernel(rate, names, *refs):
    s = Scratch(names, refs)
    width = s.attn_w.shape[1] // 4
    hidden = s.mlp_w.shape[1] // 3
    pairs = width // LANES
    thirds = pairs // 2
    half_width = width // 2
    whats = ["grad", "next", "velocity", "average", "copy"]

    def rule(weight, grad, moment, average):
        velocity = MOMENTUM * moment + grad
        weight_new = weight - rate * (grad + MOMENTUM * velocity)
        average_new = DECAY * average + (1.0 - DECAY) * weight_new
        return grad, weight_new, velocity, average_new, weight_new.astype(bf16)

    attn_blocks = [
        (kind * width + pair * LANES, LANES, (pair // 2, pair % 2), kind * LANES)
        for kind in range(3)
        for pair in range(pairs)
    ] + [(3 * width + half * half_width, half_width, (thirds, half), 0) for half in range(2)]
    pieces = [("attn", 0, 4 * width, attn_blocks)] + [
        (
            "mlp",
            kind * hidden,
            hidden,
            [
                (kind * hidden + b * LANES, LANES, (thirds + 1 + b // 2, b % 2), kind * LANES)
                for b in range(hidden // LANES)
            ],
        )
        for kind in range(3)
    ]

    def loads(index):
        kind, first, count, _ = pieces[index]
        span = pl.ds(first, count)
        return [
            pltpu.make_async_copy(
                getattr(s, f"{kind}_{what}").at[:, span],
                getattr(s, f"{kind}_{what}_here").at[:, span],
                s.in_sem.at[index, k],
            )
            for k, what in enumerate(["w", "m", "e"])
        ]

    def stores(index):
        kind, first, count, _ = pieces[index]
        span = pl.ds(first, count)
        return [
            pltpu.make_async_copy(
                getattr(s, f"{kind}_{what}_here").at[:, span],
                getattr(s, f"{kind}_{what}").at[:, span],
                s.out_sem.at[index, k],
            )
            for k, what in enumerate(whats)
        ]

    enter = [
        pltpu.make_async_copy(s.out_in, s.pass_here.at[0], s.pass_sem.at[0]),
        pltpu.make_async_copy(s.grad_in, s.pass_here.at[1], s.pass_sem.at[1]),
    ]
    leave = [
        pltpu.make_async_copy(s.pass_here.at[0], s.block_out, s.pass_sem.at[4]),
        pltpu.make_async_copy(s.pass_here.at[1], s.input_grad, s.pass_sem.at[5]),
    ]
    grads = [
        pltpu.make_async_copy(
            s.g.at[pl.ds(0, thirds + 1)], s.g_here.at[pl.ds(0, thirds + 1)], s.pass_sem.at[2]
        ),
        pltpu.make_async_copy(
            s.g.at[pl.ds(thirds + 1, s.g.shape[0] - thirds - 1)],
            s.g_here.at[pl.ds(thirds + 1, s.g.shape[0] - thirds - 1)],
            s.pass_sem.at[3],
        ),
    ]
    enter[0].start()
    grads[0].start()
    for load in loads(0):
        load.start()
    enter[1].start()
    grads[1].start()
    for index in range(1, len(pieces)):
        for load in loads(index):
            load.start()
    small_in = [
        pltpu.make_async_copy(
            getattr(s, f"gains_{what}"), getattr(s, f"gains_{what}_here"), s.in_sem.at[4, k]
        )
        for k, what in enumerate(["w", "m", "e"])
    ] + [pltpu.make_async_copy(s.gain_part_in, s.gain_part, s.in_sem.at[4, 3])]
    small_out = [
        pltpu.make_async_copy(
            getattr(s, f"gains_{what}_here"), getattr(s, f"gains_{what}"), s.out_sem.at[4, k]
        )
        for k, what in enumerate(whats)
    ]
    for copy in small_in:
        copy.start()
    enter[0].wait()
    leave[0].start()
    for copy in small_in:
        copy.wait()
    shard_rows = s.attn_w.shape[0]
    results = rule(
        s.gains_w_here[...],
        s.gain_part[:2, :shard_rows],
        s.gains_m_here[...],
        s.gains_e_here[...],
    )
    for what, result in zip(whats, results, strict=True):
        getattr(s, f"gains_{what}_here")[...] = result
    for copy in small_out:
        copy.start()
    for index, (kind, _, _, blocks) in enumerate(pieces):
        if index < 2:
            grads[index].wait()
        for load in loads(index):
            load.wait()
        for first, count, chunk, lane in blocks:
            span = slice(first, first + count)
            results = rule(
                getattr(s, f"{kind}_w_here")[:, span],
                s.g_here[chunk[0], chunk[1], :, lane : lane + count],
                getattr(s, f"{kind}_m_here")[:, span],
                getattr(s, f"{kind}_e_here")[:, span],
            )
            for what, result in zip(whats, results, strict=True):
                getattr(s, f"{kind}_{what}_here")[:, span] = result
        for store in stores(index):
            store.start()
        if index == 0:
            enter[1].wait()
            leave[1].start()
    for index in range(len(pieces)):
        for store in stores(index):
            store.wait()
    for copy in leave + small_out:
        copy.wait()


def local(
    tokens,
    doc_ids,
    cotangent,
    attn_weights,
    mlp_weights,
    gains,
    moment_attn,
    moment_mlp,
    moment_gains,
    ema_attn,
    ema_mlp,
    ema_gains,
):
    row_count, width = tokens.shape
    shard_rows = attn_weights.shape[0]
    group = width // shard_rows
    pairs = width // LANES
    hidden = mlp_weights.shape[1] // 3
    half_width = width // 2
    thirds = pairs // 2
    mlp_chunks = hidden // (2 * LANES)
    chunks = thirds + 1 + mlp_chunks

    def pack(attn, mlp):
        qkv = attn[:, : 3 * width].reshape(shard_rows, 3, pairs, LANES).transpose(2, 0, 1, 3)
        out = attn[:, 3 * width :].reshape(shard_rows, 2, half_width).transpose(1, 0, 2)
        ffn = mlp.reshape(shard_rows, 3, 2 * mlp_chunks, LANES).transpose(2, 0, 1, 3)
        return jnp.concatenate(
            [
                qkv.reshape(pairs, shard_rows, half_width),
                out,
                ffn.reshape(2 * mlp_chunks, shard_rows, half_width),
            ],
            axis=0,
        ).reshape(chunks, 2, shard_rows, half_width)

    vmem = pl.BlockSpec(memory_space=pltpu.VMEM)
    hbm = pl.BlockSpec(memory_space=pl.ANY)
    linked = shard_rows % 16 == 0 and group % 4 == 0
    planes = group // 4
    inputs = [("doc_in", hbm, doc_ids), ("x_in", hbm, tokens), ("cot_in", hbm, cotangent)]
    inputs += [("tables", hbm, rotary_tables(row_count))]
    token_rows = (row_count, width)
    outputs = [
        ("block_out", hbm, jax.ShapeDtypeStruct(token_rows, bf16)),
        ("input_grad", hbm, jax.ShapeDtypeStruct(token_rows, bf16)),
    ]
    by_pair = (pairs, LANES, row_count)
    scratch = [
        ("x", pltpu.VMEM(token_rows, bf16)),
        ("cot", pltpu.VMEM(token_rows, bf16)),
        ("y", pltpu.VMEM(token_rows, f32)),
        ("total", pltpu.VMEM(token_rows, f32)),
        ("dn", pltpu.VMEM(token_rows, f32)),
        ("n1t", pltpu.VMEM((width, row_count), bf16)),
        ("qt", pltpu.VMEM(by_pair, bf16)),
        ("kt", pltpu.VMEM(by_pair, bf16)),
        ("vt", pltpu.VMEM(by_pair, bf16)),
        ("k", pltpu.VMEM((pairs, row_count, LANES), bf16)),
        ("v", pltpu.VMEM((pairs, row_count, LANES), bf16)),
        ("mixt", pltpu.VMEM(by_pair, bf16)),
        ("n2", pltpu.VMEM((pairs, row_count, LANES), bf16)),
        ("n2t", pltpu.VMEM(by_pair, bf16)),
        ("hid", pltpu.VMEM((row_count, 2 * LANES), bf16)),
        ("dgu", pltpu.VMEM((row_count, 4 * LANES), bf16)),
        ("lse", pltpu.VMEM((pairs // 2, 8, row_count), f32)),
        ("cost", pltpu.VMEM((HEAD // 2, row_count), f32)),
        ("sint", pltpu.VMEM((HEAD // 2, row_count), f32)),
        ("local_sem", pltpu.SemaphoreType.DMA((4,))),
        ("doc", pltpu.SMEM(doc_ids.shape, jnp.int32)),
    ]
    if linked:
        lines = (planes, shard_rows, half_width)
        pair_lines = (planes, 2, shard_rows, half_width)
        whole = (planes, 4, shard_rows, half_width)
        gain_rows = (8, width)
        inputs += [
            ("attn_in", hbm, attn_weights),
            ("mlp_in", hbm, mlp_weights),
            ("gains_hbm", hbm, gains),
        ]
        outputs += [
            ("g_out", hbm, jax.ShapeDtypeStruct((chunks, 2, shard_rows, half_width), f32)),
            ("gain_out", hbm, jax.ShapeDtypeStruct((8, LANES), f32)),
        ]
        scratch += [
            ("w", pltpu.VMEM((chunks, 2) + whole, bf16)),
            ("g", pltpu.VMEM((2, 2) + whole, bf16)),
            ("a", pltpu.VMEM((2,) + whole, bf16)),
            ("h", pltpu.VMEM((HELD,) + whole, bf16)),
            ("b", pltpu.VMEM((4,) + pair_lines, bf16)),
            ("cs", pltpu.VMEM((2,) + lines, bf16)),
            ("c", pltpu.VMEM((4,) + lines, bf16)),
            ("kept", pltpu.VMEM((2,) + lines, bf16)),
            ("ds", pltpu.VMEM((2,) + lines, bf16)),
            ("d", pltpu.VMEM((4, planes - 1) + lines[1:], bf16)),
            ("own", pltpu.VMEM((2,) + lines[1:], f32)),
            ("gout", pltpu.VMEM((6,) + lines[1:], f32)),
            ("gains_in", pltpu.VMEM(gains.shape, f32)),
            ("gains_end", pltpu.VMEM((8, LANES), f32)),
            ("gains_sem", pltpu.SemaphoreType.DMA((2,))),
            ("gt", pltpu.VMEM((planes, 4, 16, LANES), bf16)),
            ("gain", pltpu.VMEM(gain_rows, f32)),
            ("gp", pltpu.VMEM((4,) + gain_rows, f32)),
            ("gz", pltpu.VMEM((planes,) + gain_rows, f32)),
            ("gc", pltpu.VMEM((2,) + gain_rows, f32)),
            ("load_sem", pltpu.SemaphoreType.DMA((4 + 3 * hidden // width,))),
            ("hop_sem", pltpu.SemaphoreType.DMA((chunks, 5))),
            ("sent_sem", pltpu.SemaphoreType.DMA((6,))),
            ("gain_sem", pltpu.SemaphoreType.DMA((2, planes + 2))),
            ("rs_sem", pltpu.SemaphoreType.DMA((chunks, 4, 2))),
            ("end_sem", pltpu.SemaphoreType.DMA((chunks, 3))),
            ("gsum_sem", pltpu.SemaphoreType.DMA((2, planes + 3))),
        ]
        params = pltpu.CompilerParams(
            collective_id=0, has_side_effects=True, vmem_limit_bytes=VMEM_BYTES
        )
    else:
        packed = pack(attn_weights.astype(bf16), mlp_weights.astype(bf16))
        full = lax.all_gather(packed, "fsdp", axis=2, tiled=True)
        gain_full = lax.all_gather(gains.astype(bf16), "fsdp", axis=1, tiled=True).astype(f32)
        inputs += [("w", vmem, full), ("gain", vmem, gain_full)]
        outputs += [
            ("g_out", hbm, jax.ShapeDtypeStruct((chunks, 2, width, half_width), bf16)),
            ("gain_out", vmem, jax.ShapeDtypeStruct((8, width), f32)),
        ]
        scratch += [
            ("g", pltpu.VMEM((2, 2, width, half_width), bf16)),
            ("g_sem", pltpu.SemaphoreType.DMA((2,))),
        ]
        params = pltpu.CompilerParams(vmem_limit_bytes=63 * 2**20)
    names = [entry[0] for entry in inputs + outputs + scratch]
    block_out, input_grad, part, gain_part = pl.pallas_call(
        functools.partial(block_kernel, linked, names),
        out_shape=[entry[2] for entry in outputs],
        in_specs=[entry[1] for entry in inputs],
        out_specs=[entry[1] for entry in outputs],
        scratch_shapes=[entry[1] for entry in scratch],
        compiler_params=params,
        name="block",
    )(*[entry[2] for entry in inputs])

    if not linked:
        part = lax.psum_scatter(part.astype(f32), "fsdp", scatter_dimension=2, tiled=True)
        part = lax.psum(part.astype(bf16), "rep").astype(f32)
        part = jnp.concatenate([part[mlp_chunks + 1 :], part[mlp_chunks:][:1], part[:mlp_chunks]])
        gain_part = lax.psum_scatter(gain_part[:2], "fsdp", scatter_dimension=1, tiled=True)
        gain_part = lax.psum(gain_part, "rep")
        gain_part = jnp.pad(gain_part, ((0, 6), (0, LANES - shard_rows)))

    total_tokens = row_count * lax.axis_size("fsdp") * lax.axis_size("rep")
    rate = PEAK_RATE * STEP / (WARMUP * math.sqrt(total_tokens))

    sources = {
        "w": (attn_weights, mlp_weights, gains),
        "m": (moment_attn, moment_mlp, moment_gains),
        "e": (ema_attn, ema_mlp, ema_gains),
    }
    kinds = ["attn", "mlp", "gains"]
    whats = ["grad", "next", "velocity", "average", "copy"]
    inputs = [("out_in", hbm, block_out), ("grad_in", hbm, input_grad), ("g", hbm, part)]
    inputs += [("gain_part_in", hbm, gain_part)]
    outputs = [("block_out", hbm, block_out), ("input_grad", hbm, input_grad)]
    scratch = []
    for what, arrays in sources.items():
        for kind, array in zip(kinds, arrays, strict=True):
            inputs.append((f"{kind}_{what}", hbm, array))
            scratch.append((f"{kind}_{what}_here", pltpu.VMEM(array.shape, f32)))
    for what in whats:
        for kind, array in zip(kinds, sources["w"], strict=True):
            dtype = bf16 if what == "copy" else f32
            outputs.append((f"{kind}_{what}", hbm, jax.ShapeDtypeStruct(array.shape, dtype)))
            scratch.append((f"{kind}_{what}_here", pltpu.VMEM(array.shape, dtype)))
    scratch += [
        ("g_here", pltpu.VMEM(part.shape, f32)),
        ("gain_part", pltpu.VMEM(gain_part.shape, f32)),
        ("in_sem", pltpu.SemaphoreType.DMA((5, 4))),
        ("out_sem", pltpu.SemaphoreType.DMA((5, 5))),
        ("pass_here", pltpu.VMEM((2,) + block_out.shape, bf16)),
        ("pass_sem", pltpu.SemaphoreType.DMA((6,))),
    ]
    names = [entry[0] for entry in inputs + outputs + scratch]
    return pl.pallas_call(
        functools.partial(update_kernel, rate, names),
        out_shape=[jax.ShapeDtypeStruct(entry[2].shape, entry[2].dtype) for entry in outputs],
        in_specs=[entry[1] for entry in inputs],
        out_specs=[entry[1] for entry in outputs],
        scratch_shapes=[entry[1] for entry in scratch],
        compiler_params=pltpu.CompilerParams(vmem_limit_bytes=63 * 2**20),
        name="update",
    )(*[entry[2] for entry in inputs])


def solution(mesh):
    rows = P(("fsdp", "rep"), None)
    shard = P("fsdp", None)
    columns = P(None, "fsdp")
    kinds = (shard, shard, columns)
    return jax.shard_map(
        local,
        mesh=mesh,
        in_specs=(rows, P(("fsdp", "rep")), rows) + kinds * 3,
        out_specs=(rows, rows) + kinds * 5,
        check_vma=False,
    )
```
